32 devices in a mesh: grp: 2 (over y), ex: 4 (over z), feat: 2 (over x), pb: 2 (over core).
Axes of the slice: x: 2, y: 2, z: 4, core: 2. Of those that a mesh axis runs over, the one named last changes fastest.
Arguments:
- train_grads: bfloat16 [1024, 256, 256], P(('grp', 'ex'), 'feat'), parts along dimension 0, may hold values from -0.029907227 to 0.029907227
- queries: bfloat16 [2, 96, 256, 256], P('pb', ('grp', 'ex'), 'feat'), parts along dimension 1, may hold values from -6 to 6
- left_factor: float32 [512, 256], P('grp'), parts along dimension 0
- right_factor: float32 [512, 256], P('grp'), parts along dimension 0
- block_order: int32 [8], P('grp'), parts along dimension 0, may hold values from 0 to 3, each once
Outputs:
- scores: float32 [1024, 2, 48], P(('grp', 'ex'), 'pb', 'feat'), parts along dimension 0
The draws below stay inside these ranges and needn't reach their ends.
There are 2 independent parts, one for each index of `grp`. The reference program is written for one: setup_inputs(seed, part) draws one part's arguments, and reference() takes and returns one part's arrays. A program takes and returns all parts, laid end to end along the dimension named above; each array names one. Nothing has to cross between parts.
Inputs may be any that keep to these rules, and one draw needn't show every extreme that they name: `block_order`: a permutation of the query blocks.
All inputs are finite; a program needn't handle non-finite values.
Results may differ from the reference program's by a relative error of at most 0.0029.
Values may be sent and summed in bfloat16 or wider, within the bound.
No kernel may reach another device: no remote copies, remote signals or barrier semaphores. Data moves between devices by JAX's collectives and lax.ppermute only.
A program may use at most 128 MiB of HBM per device.

```python
import jax
import jax.numpy as jnp
from jax import lax

A = 256
B = 256
QD = 12
NTRAIN = 512
NQH = 48
N_EX = 4
N_PB = 2


def factor_draw(key, width):
    diag_key, off_key = jax.random.split(key)
    diag_vals = jnp.exp(jax.random.uniform(diag_key, (width,), jnp.float32, jnp.log(0.5), jnp.log(2.0)))
    off_vals = jax.random.normal(off_key, (width, width), jnp.float32) * (0.6 / jnp.sqrt(width * 1.0))
    return off_vals + jnp.diag(diag_vals)


def draw_left_factor(key, part):
    key = jax.random.fold_in(key, 1)
    return factor_draw(key, A)


def draw_right_factor(key, part):
    key = jax.random.fold_in(key, 2)
    return factor_draw(key, B)


def shard_levels(rng, shape, cuts, least, top_value):
    factor_of = 1.0
    for dim, blocks in cuts:
        draws = jax.random.uniform(jax.random.fold_in(jax.random.fold_in(rng, 6), dim), (blocks,), jnp.float32, least / len(cuts), top_value / len(cuts))
        factor_of = factor_of * jnp.repeat(jnp.exp(draws), shape[dim] // blocks).reshape((-1,) + (1,) * (len(shape) - 1 - dim))
    return factor_of


def noise(own_key, extent, scale, reach, cuts=(), dtype=jnp.bfloat16):
    values = scale * jax.random.normal(own_key, extent, jnp.float32)
    if cuts:
        values = values * shard_levels(own_key, extent, cuts, -0.22, 0.18)
    return jnp.clip(values, -reach, reach).astype(dtype)


def setup_inputs(seed: int = 0, part: int = 0) -> dict:
    seeds = jax.random.split(jax.random.key(seed), 6)
    own_keys = jax.random.split(jax.random.fold_in(seeds[5], part), 6)
    train_grads = noise(own_keys[0], (NTRAIN, A, B), 0.00390625, 0.029907227, ((0, 4), (1, 2)))
    queries = noise(own_keys[1], (N_PB, NQH, A, B), 1.0, 6.0, ((0, 2), (1, 4), (2, 2)))
    left_factor = draw_left_factor(jax.random.fold_in(jax.random.fold_in(seeds[5], part), 71), part)
    right_factor = draw_right_factor(jax.random.fold_in(jax.random.fold_in(seeds[5], part), 71), part)
    block_order = jax.random.permutation(own_keys[4], N_EX).astype(jnp.int32)
    return dict(train_grads=train_grads, queries=queries, left_factor=left_factor, right_factor=right_factor, block_order=block_order)


def reference(train_grads, queries, left_factor, right_factor, block_order):
    query_wide = queries.astype(jnp.float32)
    mixed_rows = jnp.einsum('ik,hqkj->hqij', left_factor, query_wide, precision=lax.Precision.HIGHEST)
    conditioned = jnp.einsum('hqij,jl->hqil', mixed_rows, right_factor, precision=lax.Precision.HIGHEST).astype(jnp.bfloat16)
    flat_grads = train_grads.reshape(NTRAIN, A * B)
    half_list = []
    for half_index in range(N_PB):
        half_queries = conditioned[half_index].reshape(NQH, A * B)
        half_list.append(lax.dot_general(flat_grads, half_queries, (((1,), (1,)), ((), ())), preferred_element_type=jnp.float32))
    all_scores = jnp.stack(half_list, axis=1)
    all_scores = all_scores.reshape(NTRAIN, N_PB, N_EX, QD)[:, :, block_order.astype(jnp.int32), :]
    return all_scores.reshape(NTRAIN, N_PB, NQH)
```

```python
import jax
import jax.numpy as jnp
from jax import lax
from jax.experimental import pallas as pl
from jax.experimental.pallas import tpu as pltpu
from jax.sharding import PartitionSpec as P

F32 = jnp.float32
BF16 = jnp.bfloat16
EARLY = 4
PIECES = 4
VMEM = pl.BlockSpec(memory_space=pltpu.VMEM)
SMEM = pl.BlockSpec(memory_space=pltpu.SMEM)


def parts_of(x, count):
    terms = []
    for _ in range(count):
        top = x.astype(BF16)
        terms.append(top)
        x = x - top.astype(F32)
    return terms


def condition_kernel(own_ref, far_ref, left_ref, right_ref, out_ref, wide_ref):
    count, rows, _ = own_ref.shape
    side = lax.axis_index("feat")
    here = pl.ds(pl.multiple_of(side * rows, rows), rows)
    there = pl.ds(pl.multiple_of((1 - side) * rows, rows), rows)
    left = jnp.concatenate([left_ref[here, here], left_ref[here, there]], axis=1)
    left_terms = jnp.concatenate(parts_of(left, 3), axis=0)
    right_0, right_1 = parts_of(right_ref[...], 2)
    for q in range(count):
        query = jnp.concatenate([own_ref[q], far_ref[q]], axis=0)
        mixed = jnp.dot(left_terms, query, preferred_element_type=F32)
        mixed = mixed[:rows] + (mixed[rows : 2 * rows] + mixed[2 * rows :])
        mixed_0, mixed_1 = parts_of(mixed, 2)
        both = jnp.dot(jnp.concatenate([mixed_0, mixed_1], axis=0), right_0, preferred_element_type=F32)
        cross = jnp.dot(mixed_0, right_1, preferred_element_type=F32)
        wide_ref[:, q, :] = both[:rows] + (both[rows:] + cross)
    out_ref[...] = wide_ref[...].astype(BF16)


def condition(own, far, left, right):
    count, rows, width = own.shape
    return pl.pallas_call(
        condition_kernel,
        out_shape=jax.ShapeDtypeStruct((rows, count, width), BF16),
        in_specs=[VMEM] * 4,
        out_specs=VMEM,
        scratch_shapes=[pltpu.VMEM((rows, count, width), F32)],
        compiler_params=pltpu.CompilerParams(vmem_limit_bytes=24 << 20),
        cost_estimate=pl.CostEstimate(flops=count * 3_000_000 * 40, bytes_accessed=8 * count * rows * width, transcendentals=0),
    )(own, far, left, right)


def inner_products(query_refs, grad_refs):
    total = sum(ref.shape[1] for ref in query_refs)
    acc = jnp.zeros((total, grad_refs[0].shape[1]), F32)
    first = 0
    for grad_ref in grad_refs:
        count = grad_ref.shape[0]
        unroll = 16

        def body(i, acc, grad_ref=grad_ref, first=first):
            for j in range(unroll):
                r = i * unroll + j
                queries = jnp.concatenate([ref[first + r] for ref in query_refs], axis=0)
                acc = acc + lax.dot_general(
                    queries, grad_ref[r], (((1,), (1,)), ((), ())), preferred_element_type=F32
                )
            return acc

        acc = lax.fori_loop(0, count // unroll, body, acc)
        first += count
    return acc


def first_pass_kernel(ex, early_ref, own_ref, up0, down0, up1, down1, *rest):
    *grad_refs, order_ref, out_ref = rest
    late = own_ref.shape[1]
    acc = inner_products((early_ref, own_ref, up0, down0, up1, down1), grad_refs)
    me = lax.axis_index("ex")
    early = [acc[EARLY * s : EARLY * (s + 1)] for s in range(ex)]
    base = EARLY * ex
    slots = [acc[base + late * s : base + late * (s + 1)] for s in range(5)]
    sources = [me, me - 1, me + 1, me - 2, me + 2]
    for b in range(ex):
        block = order_ref[b]
        low = jnp.zeros_like(early[0])
        for s in range(ex):
            low = low + jnp.where(lax.rem(me - s + ex, ex) == block, early[s], 0.0)
        high = jnp.zeros_like(slots[0])
        for slot, source in zip(slots, sources):
            high = high + jnp.where(source == block, slot, 0.0)
        at = b * (EARLY + late)
        out_ref[at : at + EARLY, :] = low
        out_ref[at + EARLY : at + EARLY + late, :] = high


def last_pass_kernel(ex, base_ref, up2, down2, *rest):
    *grad_refs, order_ref, mine_ref, send_ref, full_ref = rest
    late = up2.shape[1]
    acc = inner_products((up2, down2), grad_refs)
    me = lax.axis_index("ex")
    full_ref[...] = base_ref[...]
    for b in range(ex):
        block = order_ref[b]
        at = b * (EARLY + late) + EARLY
        high = jnp.where(block == me - 3, acc[:late], 0.0) + jnp.where(block == me + 3, acc[late:], 0.0)
        full_ref[at : at + late, :] = full_ref[at : at + late, :] + high
    half = mine_ref.shape[0]
    side = lax.axis_index("feat")
    mine_ref[...] = full_ref[pl.ds(pl.multiple_of(side * half, half), half), :]
    send_ref[...] = full_ref[pl.ds(pl.multiple_of((1 - side) * half, half), half), :]


def score_call(kernel, ex, arrays, pieces, order, out_shape, scratch=()):
    count = len(arrays) + len(pieces)
    return pl.pallas_call(
        lambda *refs: kernel(ex, *refs),
        out_shape=out_shape,
        in_specs=[VMEM] * count + [SMEM],
        out_specs=jax.tree.map(lambda _: VMEM, out_shape),
        scratch_shapes=scratch,
        compiler_params=pltpu.CompilerParams(vmem_limit_bytes=32 << 20),
        cost_estimate=pl.CostEstimate(flops=3_000_000_000, bytes_accessed=12_000_000, transcendentals=0),
    )(*arrays, *pieces, order)


def line_step(x, y, step, ex):
    up = [(i, i + 1) for i in range(step, ex - 1)]
    down = [(i + 1, i) for i in range(ex - 1 - step)]
    return lax.ppermute(x, "ex", up), lax.ppermute(y, "ex", down)


def per_device_line(train_grads, queries, left_factor, right_factor, block_order):
    ex = lax.axis_size("ex")
    swap = [(0, 1), (1, 0)]
    rows = train_grads.shape[1]
    count = queries.shape[1]
    raw = queries[0, :EARLY]
    late_raw = queries[0, EARLY:]
    ups, downs = [raw], [raw]
    u, d = line_step(raw, raw, 0, ex)
    ups.append(u)
    downs.append(d)
    late_far = lax.ppermute(late_raw, "feat", swap)
    for s in (1, 2):
        u, d = line_step(ups[-1], downs[-1], s, ex)
        ups.append(u)
        downs.append(d)
    late = condition(late_raw, late_far, left_factor, right_factor)
    up0, down0 = line_step(late, late, 0, ex)
    up1, down1 = line_step(up0, down0, 1, ex)
    up2, down2 = line_step(up1, down1, 2, ex)
    early = jnp.concatenate([raw] + [ups[s] + downs[ex - s] for s in range(1, ex)], axis=0)
    early_far = lax.ppermute(early, "feat", swap)
    early_cond = condition(early, early_far, left_factor, right_factor)
    step = rows // PIECES
    pieces = [train_grads[:, p * step : (p + 1) * step].transpose(1, 0, 2) for p in range(PIECES)]
    n = train_grads.shape[0]
    base = score_call(
        first_pass_kernel, ex, (early_cond, late, up0, down0, up1, down1), pieces, block_order,
        jax.ShapeDtypeStruct((ex * count, n), F32),
    )
    half = jax.ShapeDtypeStruct((ex * count // 2, n), F32)
    mine, send = score_call(
        last_pass_kernel, ex, (base, up2, down2), pieces, block_order, (half, half),
        [pltpu.VMEM((ex * count, n), F32)],
    )
    scores = mine + lax.ppermute(send, "feat", swap)
    return scores.T[:, None, :]


def per_device_gather(train_grads, queries, left_factor, right_factor, block_order):
    row_count = train_grads.shape[0]
    part_rows = train_grads.shape[1]
    right_width = train_grads.shape[2]
    flat_grads = train_grads.reshape(row_count, part_rows * right_width)
    local_queries = queries[0]
    block_size = local_queries.shape[0]
    regrouped = lax.all_to_all(local_queries, "feat", split_axis=0, concat_axis=1, tiled=True)
    whole_mix = jnp.einsum(
        "ik,qkj->qij", left_factor, regrouped.astype(F32), precision=lax.Precision.HIGHEST
    )
    whole_cond = jnp.einsum(
        "qij,jl->qil", whole_mix, right_factor, precision=lax.Precision.HIGHEST
    ).astype(BF16)
    conditioned = lax.all_to_all(whole_cond, "feat", split_axis=1, concat_axis=0, tiled=True)
    conditioned = conditioned.reshape(block_size, part_rows * right_width)
    partials = lax.dot_general(
        flat_grads,
        lax.all_gather(conditioned, "ex", axis=0, tiled=True),
        (((1,), (1,)), ((), ())),
        preferred_element_type=F32,
    )
    block_count = lax.axis_size("ex")
    partials = jnp.take(partials.reshape(row_count, block_count, block_size), block_order, axis=1)
    partials = partials.reshape(row_count, block_count * block_size)
    owned_scores = lax.psum_scatter(partials, "feat", scatter_dimension=1, tiled=True)
    return owned_scores.reshape(row_count, 1, owned_scores.shape[1])


def solution(mesh):
    short_line = mesh.shape["ex"] == 4 and mesh.shape["feat"] == 2
    return jax.shard_map(
        per_device_line if short_line else per_device_gather,
        mesh=mesh,
        in_specs=(
            P(("grp", "ex"), "feat", None),
            P("pb", ("grp", "ex"), "feat", None),
            P("grp", None),
            P("grp", None),
            P("grp"),
        ),
        out_specs=P(("grp", "ex"), "pb", "feat"),
        check_vma=False,
    )
```

```python
import jax
import jax.numpy as jnp
from jax import lax
from jax.experimental import pallas as pl
from jax.experimental.pallas import tpu as pltpu
from jax.sharding import PartitionSpec as P

F32 = jnp.float32
BF16 = jnp.bfloat16
EARLY = 4
VMEM = pl.BlockSpec(memory_space=pltpu.VMEM)
SMEM = pl.BlockSpec(memory_space=pltpu.SMEM)


def parts_of(x, count):
    terms = []
    for _ in range(count):
        top = x.astype(BF16)
        terms.append(top)
        x = x - top.astype(F32)
    return terms


def factor_kernel(left_ref, right_ref, left_out, right_out):
    rows = left_out.shape[0] // 3
    side = lax.axis_index("feat")
    here = pl.ds(pl.multiple_of(side * rows, rows), rows)
    there = pl.ds(pl.multiple_of((1 - side) * rows, rows), rows)
    left = jnp.concatenate([left_ref[here, here], left_ref[here, there]], axis=1)
    left_out[...] = jnp.concatenate(parts_of(left, 3), axis=0)
    right_out[...] = jnp.concatenate(parts_of(right_ref[...], 2), axis=0)


def factor_terms(left, right, rows):
    wide, width = left.shape[1], right.shape[1]
    return pl.pallas_call(
        factor_kernel,
        out_shape=(
            jax.ShapeDtypeStruct((3 * rows, wide), BF16),
            jax.ShapeDtypeStruct((2 * width, width), BF16),
        ),
        in_specs=[VMEM] * 2,
        out_specs=(VMEM, VMEM),
        compiler_params=pltpu.CompilerParams(vmem_limit_bytes=16 << 20),
    )(left, right)


def condition_kernel(own_ref, far_ref, left_ref, right_ref, out_ref, wide_ref):
    count, rows, width = own_ref.shape
    left_terms = left_ref[...]
    right_0, right_1 = right_ref[:width], right_ref[width:]
    for q in range(count):
        query = jnp.concatenate([own_ref[q], far_ref[q]], axis=0)
        mixed = jnp.dot(left_terms, query, preferred_element_type=F32)
        mixed = mixed[:rows] + (mixed[rows : 2 * rows] + mixed[2 * rows :])
        mixed_0, mixed_1 = parts_of(mixed, 2)
        both = jnp.dot(jnp.concatenate([mixed_0, mixed_1], axis=0), right_0, preferred_element_type=F32)
        cross = jnp.dot(mixed_0, right_1, preferred_element_type=F32)
        wide_ref[:, q, :] = both[:rows] + (both[rows:] + cross)
    out_ref[...] = wide_ref[...].astype(BF16)


def condition(own, far, left_terms, right_terms):
    count, rows, width = own.shape
    return pl.pallas_call(
        condition_kernel,
        out_shape=jax.ShapeDtypeStruct((rows, count, width), BF16),
        in_specs=[VMEM] * 4,
        out_specs=VMEM,
        scratch_shapes=[pltpu.VMEM((rows, count, width), F32)],
        compiler_params=pltpu.CompilerParams(vmem_limit_bytes=24 << 20),
        cost_estimate=pl.CostEstimate(flops=count * 3_000_000 * 40, bytes_accessed=8 * count * rows * width, transcendentals=0),
    )(own, far, left_terms, right_terms)


def inner_products(query_refs, grad_refs):
    total = sum(ref.shape[1] for ref in query_refs)
    acc = jnp.zeros((total, grad_refs[0].shape[1]), F32)
    first = 0
    for grad_ref in grad_refs:
        count = grad_ref.shape[0]
        unroll = 16

        def body(i, acc, grad_ref=grad_ref, first=first):
            for j in range(unroll):
                r = i * unroll + j
                queries = jnp.concatenate([ref[first + r] for ref in query_refs], axis=0)
                acc = acc + lax.dot_general(
                    queries, grad_ref[r], (((1,), (1,)), ((), ())), preferred_element_type=F32
                )
            return acc

        acc = lax.fori_loop(0, count // unroll, body, acc)
        first += count
    return acc


def first_pass_kernel(ex, early_0, early_1, own_ref, near, mid, far_in, *rest):
    *grad_refs, order_ref, out_ref = rest
    late = own_ref.shape[1]
    acc = inner_products((early_0, early_1, own_ref, near, mid, far_in), grad_refs)
    me = lax.axis_index("ex")
    sources = slot_sources(me)
    early = [acc[EARLY * s : EARLY * (s + 1)] for s in range(ex)]
    base = EARLY * ex
    slots = [acc[base + late * s : base + late * (s + 1)] for s in range(4)]
    for b in range(ex):
        block = order_ref[b]
        low = jnp.zeros_like(early[0])
        high = jnp.zeros_like(slots[0])
        for s in range(ex):
            hit = sources[s] == block
            low = low + jnp.where(hit, early[s], 0.0)
            high = high + jnp.where(hit, slots[s], 0.0)
        at = b * (EARLY + late)
        out_ref[at : at + EARLY, :] = low
        out_ref[at + EARLY : at + EARLY + late, :] = high


def slot_sources(me):
    low_pair = me < 2
    near = jnp.where(low_pair, 1 - me, 5 - me)
    return [me, near, jnp.where(low_pair, 2, 1), jnp.where(low_pair, 3, 0)]


def last_pass_kernel(ex, base_ref, far_out, *rest):
    *grad_refs, order_ref, mine_ref, send_ref, full_ref = rest
    late = far_out.shape[1]
    acc = inner_products((far_out,), grad_refs)
    far = slot_sources(lax.axis_index("ex"))[3]
    full_ref[...] = base_ref[...]
    for b in range(ex):
        at = b * (EARLY + late) + EARLY
        full_ref[at : at + late, :] = full_ref[at : at + late, :] + jnp.where(order_ref[b] == far, acc, 0.0)
    half = mine_ref.shape[0]
    side = lax.axis_index("feat")
    mine_ref[...] = full_ref[pl.ds(pl.multiple_of(side * half, half), half), :]
    send_ref[...] = full_ref[pl.ds(pl.multiple_of((1 - side) * half, half), half), :]


def score_call(kernel, ex, arrays, pieces, order, out_shape, scratch=()):
    count = len(arrays) + len(pieces)
    return pl.pallas_call(
        lambda *refs: kernel(ex, *refs),
        out_shape=out_shape,
        in_specs=[VMEM] * count + [SMEM],
        out_specs=jax.tree.map(lambda _: VMEM, out_shape),
        scratch_shapes=scratch,
        compiler_params=pltpu.CompilerParams(vmem_limit_bytes=32 << 20),
        cost_estimate=pl.CostEstimate(flops=3_000_000_000, bytes_accessed=12_000_000, transcendentals=0),
    )(*arrays, *pieces, order)


def after(x, *others):
    return lax.optimization_barrier((x, *others))[0]


PAIRS = [(0, 1), (1, 0), (2, 3), (3, 2)]
MIDDLE = [(1, 2), (2, 1)]
OUTWARD = [(1, 0), (2, 3)]


def per_device_line(train_grads, queries, left_factor, right_factor, block_order):
    ex = lax.axis_size("ex")
    swap = [(0, 1), (1, 0)]
    count = queries.shape[1]
    n = train_grads.shape[0]
    raw = queries[0, :EARLY]
    late_raw = after(queries, raw)[0, EARLY:]
    raw_near = lax.ppermute(raw, "ex", PAIRS)
    raw_mid = lax.ppermute(raw, "ex", MIDDLE)
    late_other = lax.ppermute(late_raw, "feat", swap)
    terms = factor_terms(left_factor, after(right_factor, late_raw), train_grads.shape[1])
    raw_far_mid = lax.ppermute(after(raw_near, *terms), "ex", MIDDLE)
    raw_mid_out = lax.ppermute(after(raw_mid, *terms), "ex", OUTWARD)
    early_0 = jnp.concatenate([raw, raw_near], axis=0)
    early_0_other = lax.ppermute(early_0, "feat", swap)

    late = condition(after(late_raw, raw_far_mid, raw_mid_out), late_other, *terms)
    raw_far_out = lax.ppermute(raw_far_mid, "ex", OUTWARD)
    near = lax.ppermute(late, "ex", PAIRS)
    mid = lax.ppermute(late, "ex", MIDDLE)
    grads = after(train_grads, late).transpose(1, 0, 2)
    early_1 = jnp.concatenate([raw_mid + raw_mid_out, raw_far_mid + raw_far_out], axis=0)
    early_1_other = lax.ppermute(early_1, "feat", swap)
    far_mid = lax.ppermute(after(near, grads, early_0_other), "ex", MIDDLE)
    mid_out = lax.ppermute(after(mid, grads), "ex", OUTWARD)
    cond_0 = condition(after(early_0, far_mid, mid_out), early_0_other, *terms)
    cond_1 = condition(after(early_1, cond_0), early_1_other, *terms)
    far_out = lax.ppermute(far_mid, "ex", OUTWARD)
    pieces = [grads]
    base = score_call(
        first_pass_kernel, ex, (cond_0, cond_1, late, near, mid + mid_out, far_mid), pieces, block_order,
        jax.ShapeDtypeStruct((ex * count, n), F32),
    )
    half = jax.ShapeDtypeStruct((ex * count // 2, n), F32)
    mine, send = score_call(
        last_pass_kernel, ex, (base, far_out), pieces, block_order, (half, half),
        [pltpu.VMEM((ex * count, n), F32)],
    )
    scores = mine + lax.ppermute(send, "feat", swap)
    return scores.T[:, None, :]


def per_device_gather(train_grads, queries, left_factor, right_factor, block_order):
    row_count = train_grads.shape[0]
    part_rows = train_grads.shape[1]
    right_width = train_grads.shape[2]
    flat_grads = train_grads.reshape(row_count, part_rows * right_width)
    local_queries = queries[0]
    block_size = local_queries.shape[0]
    regrouped = lax.all_to_all(local_queries, "feat", split_axis=0, concat_axis=1, tiled=True)
    whole_mix = jnp.einsum(
        "ik,qkj->qij", left_factor, regrouped.astype(F32), precision=lax.Precision.HIGHEST
    )
    whole_cond = jnp.einsum(
        "qij,jl->qil", whole_mix, right_factor, precision=lax.Precision.HIGHEST
    ).astype(BF16)
    conditioned = lax.all_to_all(whole_cond, "feat", split_axis=1, concat_axis=0, tiled=True)
    conditioned = conditioned.reshape(block_size, part_rows * right_width)
    partials = lax.dot_general(
        flat_grads,
        lax.all_gather(conditioned, "ex", axis=0, tiled=True),
        (((1,), (1,)), ((), ())),
        preferred_element_type=F32,
    )
    block_count = lax.axis_size("ex")
    partials = jnp.take(partials.reshape(row_count, block_count, block_size), block_order, axis=1)
    partials = partials.reshape(row_count, block_count * block_size)
    owned_scores = lax.psum_scatter(partials, "feat", scatter_dimension=1, tiled=True)
    return owned_scores.reshape(row_count, 1, owned_scores.shape[1])


def solution(mesh):
    short_line = mesh.shape["ex"] == 4 and mesh.shape["feat"] == 2
    return jax.shard_map(
        per_device_line if short_line else per_device_gather,
        mesh=mesh,
        in_specs=(
            P(("grp", "ex"), "feat", None),
            P("pb", ("grp", "ex"), "feat", None),
            P("grp", None),
            P("grp", None),
            P("grp"),
        ),
        out_specs=P(("grp", "ex"), "pb", "feat"),
        check_vma=False,
    )
```

```python
import functools

import jax
import jax.numpy as jnp
from jax import lax
from jax.experimental import pallas as pl
from jax.experimental.pallas import tpu as pltpu
from jax.sharding import PartitionSpec as P

F32 = jnp.float32
BF16 = jnp.bfloat16
EARLY = 4
TILE = 16
EXAMPLES = 32
DEEP = 32
VMEM = pl.BlockSpec(memory_space=pltpu.VMEM)
SMEM = pl.BlockSpec(memory_space=pltpu.SMEM)


def parts_of(x, count):
    terms = []
    for _ in range(count):
        top = x.astype(BF16)
        terms.append(top)
        x = x - top.astype(F32)
    return terms


def factor_kernel(left_ref, right_ref, left_out, right_out):
    rows = left_out.shape[0] // 3
    side = lax.axis_index("feat")
    here = pl.ds(pl.multiple_of(side * rows, rows), rows)
    there = pl.ds(pl.multiple_of((1 - side) * rows, rows), rows)
    left = jnp.concatenate([left_ref[here, here], left_ref[here, there]], axis=1)
    left_out[...] = jnp.concatenate(parts_of(left, 3), axis=0)
    right_out[...] = jnp.concatenate(parts_of(right_ref[...], 2), axis=0)


def factor_terms(left, right, rows):
    wide, width = left.shape[1], right.shape[1]
    return pl.pallas_call(
        factor_kernel,
        out_shape=(
            jax.ShapeDtypeStruct((3 * rows, wide), BF16),
            jax.ShapeDtypeStruct((2 * width, width), BF16),
        ),
        in_specs=[VMEM] * 2,
        out_specs=(VMEM, VMEM),
        compiler_params=pltpu.CompilerParams(vmem_limit_bytes=16 << 20),
    )(left, right)


def condition_kernel(own_ref, far_ref, left_ref, right_ref, out_ref, wide_ref):
    count, rows, width = own_ref.shape
    left_terms = left_ref[...]
    right_0, right_1 = right_ref[:width], right_ref[width:]
    for q in range(count):
        query = jnp.concatenate([own_ref[q], far_ref[q]], axis=0)
        mixed = jnp.dot(left_terms, query, preferred_element_type=F32)
        mixed = mixed[:rows] + (mixed[rows : 2 * rows] + mixed[2 * rows :])
        mixed_0, mixed_1 = parts_of(mixed, 2)
        both = jnp.dot(jnp.concatenate([mixed_0, mixed_1], axis=0), right_0, preferred_element_type=F32)
        cross = jnp.dot(mixed_0, right_1, preferred_element_type=F32)
        wide_ref[:, q, :] = both[:rows] + (both[rows:] + cross)
    out_ref[...] = wide_ref[...].astype(BF16)


def condition(own, far, left_terms, right_terms):
    count, rows, width = own.shape
    return pl.pallas_call(
        condition_kernel,
        out_shape=jax.ShapeDtypeStruct((rows, count, width), BF16),
        in_specs=[VMEM] * 4,
        out_specs=VMEM,
        scratch_shapes=[pltpu.VMEM((rows, count, width), F32)],
        compiler_params=pltpu.CompilerParams(vmem_limit_bytes=24 << 20),
        cost_estimate=pl.CostEstimate(flops=count * 3_000_000 * 40, bytes_accessed=8 * count * rows * width, transcendentals=0),
    )(own, far, left_terms, right_terms)


def regroup_kernel(grads_ref, out_ref, held_ref, sems):
    examples, rows, width = held_ref.shape
    blocks = examples // EXAMPLES
    copies = []
    for b in range(blocks):
        part = pl.ds(b * EXAMPLES, EXAMPLES)
        copies.append(pltpu.make_async_copy(grads_ref.at[part], held_ref.at[part], sems.at[b]))
        copies[-1].start()
    i = lax.broadcasted_iota(jnp.int32, (TILE * TILE, TILE * TILE), 0)
    j = lax.broadcasted_iota(jnp.int32, (TILE * TILE, TILE * TILE), 1)
    swap = jnp.where((i // TILE == j % TILE) & (i % TILE == j // TILE), 1.0, 0.0).astype(BF16)
    for b in range(blocks):
        copies[b].wait()

        @pl.loop(b * EXAMPLES // TILE, (b + 1) * EXAMPLES // TILE)
        def _(step):
            n = pl.ds(pl.multiple_of(step * TILE, TILE), TILE)
            for r in range(0, rows, TILE):
                tile = held_ref[n, r : r + TILE, :].reshape(TILE * TILE, width)
                turned = jnp.dot(swap, tile, preferred_element_type=F32).astype(BF16)
                out_ref[r : r + TILE, n, :] = turned.reshape(TILE, TILE, width)


def regroup(grads):
    n, rows, width = grads.shape
    return pl.pallas_call(
        regroup_kernel,
        out_shape=jax.ShapeDtypeStruct((rows, n, width), BF16),
        in_specs=[pl.BlockSpec(memory_space=pltpu.HBM)],
        out_specs=VMEM,
        scratch_shapes=[pltpu.VMEM((n, rows, width), BF16), pltpu.SemaphoreType.DMA((n // EXAMPLES,))],
        compiler_params=pltpu.CompilerParams(vmem_limit_bytes=48 << 20),
        cost_estimate=pl.CostEstimate(flops=6_000_000_000, bytes_accessed=16_000_000, transcendentals=0),
    )(grads)


def inner_products(query_refs, grad_ref):
    total = sum(ref.shape[1] for ref in query_refs)

    def body(i, acc):
        at = [i * DEEP + j for j in range(DEEP)]
        queries = [jnp.concatenate([ref[r] for ref in query_refs], axis=0) for r in at]
        return acc + lax.dot_general(
            jnp.concatenate(queries, axis=1),
            jnp.concatenate([grad_ref[r] for r in at], axis=1),
            (((1,), (1,)), ((), ())),
            preferred_element_type=F32,
        )

    start = jnp.zeros((total, grad_ref.shape[1]), F32)
    return lax.fori_loop(0, grad_ref.shape[0] // DEEP, body, start)


def first_pass_kernel(ex, early_0, early_1, own_ref, near, mid, far_in, grad_ref, order_ref, out_ref):
    late = own_ref.shape[1]
    acc = inner_products((early_0, early_1, own_ref, near, mid, far_in), grad_ref)
    me = lax.axis_index("ex")
    sources = slot_sources(me)
    early = [acc[EARLY * s : EARLY * (s + 1)] for s in range(ex)]
    base = EARLY * ex
    slots = [acc[base + late * s : base + late * (s + 1)] for s in range(4)]
    for b in range(ex):
        block = order_ref[b]
        low = jnp.zeros_like(early[0])
        high = jnp.zeros_like(slots[0])
        for s in range(ex):
            hit = sources[s] == block
            low = low + jnp.where(hit, early[s], 0.0)
            high = high + jnp.where(hit, slots[s], 0.0)
        at = b * (EARLY + late)
        out_ref[at : at + EARLY, :] = low
        out_ref[at + EARLY : at + EARLY + late, :] = high


def slot_sources(me):
    low_pair = me < 2
    near = jnp.where(low_pair, 1 - me, 5 - me)
    return [me, near, jnp.where(low_pair, 2, 1), jnp.where(low_pair, 3, 0)]


def last_pass_kernel(ex, base_ref, far_out, grad_ref, order_ref, mine_ref, send_ref, full_ref):
    late = far_out.shape[1]
    acc = inner_products((far_out,), grad_ref)
    far = slot_sources(lax.axis_index("ex"))[3]
    full_ref[...] = base_ref[...]
    for b in range(ex):
        at = b * (EARLY + late) + EARLY
        full_ref[at : at + late, :] = full_ref[at : at + late, :] + jnp.where(order_ref[b] == far, acc, 0.0)
    half = mine_ref.shape[0]
    side = lax.axis_index("feat")
    mine_ref[...] = full_ref[pl.ds(pl.multiple_of(side * half, half), half), :]
    send_ref[...] = full_ref[pl.ds(pl.multiple_of((1 - side) * half, half), half), :]


def score_call(kernel, ex, arrays, order, out_shape, scratch=()):
    return pl.pallas_call(
        functools.partial(kernel, ex),
        out_shape=out_shape,
        in_specs=[VMEM] * len(arrays) + [SMEM],
        out_specs=jax.tree.map(lambda _: VMEM, out_shape),
        scratch_shapes=scratch,
        compiler_params=pltpu.CompilerParams(vmem_limit_bytes=40 << 20),
        cost_estimate=pl.CostEstimate(flops=3_000_000_000, bytes_accessed=12_000_000, transcendentals=0),
    )(*arrays, order)


def after(x, *others):
    return lax.optimization_barrier((x, *others))[0]


PAIRS = [(0, 1), (1, 0), (2, 3), (3, 2)]
MIDDLE = [(1, 2), (2, 1)]
OUTWARD = [(1, 0), (2, 3)]


def per_device_line(train_grads, queries, left_factor, right_factor, block_order):
    ex = lax.axis_size("ex")
    swap = [(0, 1), (1, 0)]
    count = queries.shape[1]
    n = train_grads.shape[0]
    late_raw = queries[0, EARLY:]
    late_other = lax.ppermute(late_raw, "feat", swap)
    raw = after(queries, late_raw)[0, :EARLY]
    terms = factor_terms(left_factor, after(right_factor, raw), train_grads.shape[1])
    raw_near = lax.ppermute(raw, "ex", PAIRS)
    raw_mid = lax.ppermute(raw, "ex", MIDDLE)
    grads = regroup(after(train_grads, late_other))
    raw_far_mid = lax.ppermute(after(raw_near, *terms), "ex", MIDDLE)
    raw_mid_out = lax.ppermute(raw_mid, "ex", OUTWARD)

    late = condition(after(late_raw, raw_far_mid, raw_mid_out, grads), late_other, *terms)
    near = lax.ppermute(late, "ex", PAIRS)
    mid = lax.ppermute(late, "ex", MIDDLE)
    early_0 = jnp.concatenate([raw, after(raw_near, late)], axis=0)
    early_0_other = lax.ppermute(early_0, "feat", swap)
    raw_far_out = lax.ppermute(after(raw_far_mid, near), "ex", OUTWARD)
    far_mid = lax.ppermute(near, "ex", MIDDLE)
    mid_out = lax.ppermute(after(mid, near), "ex", OUTWARD)
    cond_0 = condition(after(early_0, near, mid), early_0_other, *terms)
    early_1 = jnp.concatenate([raw_mid + raw_mid_out, raw_far_mid + raw_far_out], axis=0)
    early_1_other = lax.ppermute(after(early_1, cond_0), "feat", swap)
    far_out = lax.ppermute(far_mid, "ex", OUTWARD)
    cond_1 = condition(after(early_1, far_mid), early_1_other, *terms)

    base = score_call(
        first_pass_kernel, ex, (cond_0, cond_1, late, near, mid + mid_out, far_mid, grads), block_order,
        jax.ShapeDtypeStruct((ex * count, n), F32),
    )
    half = jax.ShapeDtypeStruct((ex * count // 2, n), F32)
    mine, send = score_call(
        last_pass_kernel, ex, (base, far_out, grads), block_order, (half, half),
        [pltpu.VMEM((ex * count, n), F32)],
    )
    scores = mine + lax.ppermute(send, "feat", swap)
    return scores.T[:, None, :]


def per_device_gather(train_grads, queries, left_factor, right_factor, block_order):
    row_count = train_grads.shape[0]
    part_rows = train_grads.shape[1]
    right_width = train_grads.shape[2]
    flat_grads = train_grads.reshape(row_count, part_rows * right_width)
    local_queries = queries[0]
    block_size = local_queries.shape[0]
    regrouped = lax.all_to_all(local_queries, "feat", split_axis=0, concat_axis=1, tiled=True)
    whole_mix = jnp.einsum(
        "ik,qkj->qij", left_factor, regrouped.astype(F32), precision=lax.Precision.HIGHEST
    )
    whole_cond = jnp.einsum(
        "qij,jl->qil", whole_mix, right_factor, precision=lax.Precision.HIGHEST
    ).astype(BF16)
    conditioned = lax.all_to_all(whole_cond, "feat", split_axis=1, concat_axis=0, tiled=True)
    conditioned = conditioned.reshape(block_size, part_rows * right_width)
    partials = lax.dot_general(
        flat_grads,
        lax.all_gather(conditioned, "ex", axis=0, tiled=True),
        (((1,), (1,)), ((), ())),
        preferred_element_type=F32,
    )
    block_count = lax.axis_size("ex")
    partials = jnp.take(partials.reshape(row_count, block_count, block_size), block_order, axis=1)
    partials = partials.reshape(row_count, block_count * block_size)
    owned_scores = lax.psum_scatter(partials, "feat", scatter_dimension=1, tiled=True)
    return owned_scores.reshape(row_count, 1, owned_scores.shape[1])


def solution(mesh):
    short_line = mesh.shape["ex"] == 4 and mesh.shape["feat"] == 2
    return jax.shard_map(
        per_device_line if short_line else per_device_gather,
        mesh=mesh,
        in_specs=(
            P(("grp", "ex"), "feat", None),
            P("pb", ("grp", "ex"), "feat", None),
            P("grp", None),
            P("grp", None),
            P("grp"),
        ),
        out_specs=P(("grp", "ex"), "pb", "feat"),
        check_vma=False,
    )
```

```python
import functools

import jax
import jax.numpy as jnp
from jax import lax
from jax.experimental import pallas as pl
from jax.experimental.pallas import tpu as pltpu
from jax.sharding import PartitionSpec as P

F32 = jnp.float32
BF16 = jnp.bfloat16
EARLY = 4
TILE = 16
EXAMPLES = 32
DEEP = 32
VMEM = pl.BlockSpec(memory_space=pltpu.VMEM)
SMEM = pl.BlockSpec(memory_space=pltpu.SMEM)


def parts_of(x, count):
    terms = []
    for _ in range(count):
        top = x.astype(BF16)
        terms.append(top)
        x = x - top.astype(F32)
    return terms


def factor_kernel(left_ref, right_ref, left_out, right_out):
    rows = left_out.shape[0] // 3
    side = lax.axis_index("feat")
    here = pl.ds(pl.multiple_of(side * rows, rows), rows)
    there = pl.ds(pl.multiple_of((1 - side) * rows, rows), rows)
    left = jnp.concatenate([left_ref[here, here], left_ref[here, there]], axis=1)
    left_out[...] = jnp.concatenate(parts_of(left, 3), axis=0)
    right_out[...] = jnp.concatenate(parts_of(right_ref[...], 2), axis=0)


def factor_terms(left, right, rows):
    wide, width = left.shape[1], right.shape[1]
    return pl.pallas_call(
        factor_kernel,
        out_shape=(
            jax.ShapeDtypeStruct((3 * rows, wide), BF16),
            jax.ShapeDtypeStruct((2 * width, width), BF16),
        ),
        in_specs=[VMEM] * 2,
        out_specs=(VMEM, VMEM),
        compiler_params=pltpu.CompilerParams(vmem_limit_bytes=16 << 20),
    )(left, right)


def condition_kernel(own_ref, far_ref, left_ref, right_ref, out_ref, wide_ref):
    count, rows, width = own_ref.shape
    left_terms = left_ref[...]
    right_0, right_1 = right_ref[:width], right_ref[width:]
    for q in range(count):
        query = jnp.concatenate([own_ref[q], far_ref[q]], axis=0)
        mixed = jnp.dot(left_terms, query, preferred_element_type=F32)
        mixed = mixed[:rows] + (mixed[rows : 2 * rows] + mixed[2 * rows :])
        mixed_0, mixed_1 = parts_of(mixed, 2)
        both = jnp.dot(jnp.concatenate([mixed_0, mixed_1], axis=0), right_0, preferred_element_type=F32)
        cross = jnp.dot(mixed_0, right_1, preferred_element_type=F32)
        wide_ref[:, q, :] = both[:rows] + (both[rows:] + cross)
    out_ref[...] = wide_ref[...].astype(BF16)


def condition(own, far, left_terms, right_terms):
    count, rows, width = own.shape
    return pl.pallas_call(
        condition_kernel,
        out_shape=jax.ShapeDtypeStruct((rows, count, width), BF16),
        in_specs=[VMEM] * 4,
        out_specs=VMEM,
        scratch_shapes=[pltpu.VMEM((rows, count, width), F32)],
        compiler_params=pltpu.CompilerParams(vmem_limit_bytes=24 << 20),
        cost_estimate=pl.CostEstimate(flops=count * 3_000_000 * 40, bytes_accessed=8 * count * rows * width, transcendentals=0),
    )(own, far, left_terms, right_terms)


def regroup_kernel(grads_ref, out_ref, held_ref, sems):
    examples, rows, width = held_ref.shape
    blocks = examples // EXAMPLES
    copies = []
    for b in range(blocks):
        part = pl.ds(b * EXAMPLES, EXAMPLES)
        copies.append(pltpu.make_async_copy(grads_ref.at[part], held_ref.at[part], sems.at[b]))
        copies[-1].start()
    i = lax.broadcasted_iota(jnp.int32, (TILE * TILE, TILE * TILE), 0)
    j = lax.broadcasted_iota(jnp.int32, (TILE * TILE, TILE * TILE), 1)
    swap = jnp.where((i // TILE == j % TILE) & (i % TILE == j // TILE), 1.0, 0.0).astype(BF16)
    for b in range(blocks):
        copies[b].wait()

        @pl.loop(b * EXAMPLES // TILE, (b + 1) * EXAMPLES // TILE)
        def _(step):
            n = pl.ds(pl.multiple_of(step * TILE, TILE), TILE)
            for r in range(0, rows, TILE):
                tile = held_ref[n, r : r + TILE, :].reshape(TILE * TILE, width)
                turned = jnp.dot(swap, tile, preferred_element_type=F32).astype(BF16)
                out_ref[r : r + TILE, n, :] = turned.reshape(TILE, TILE, width)


def regroup(grads):
    n, rows, width = grads.shape
    return pl.pallas_call(
        regroup_kernel,
        out_shape=jax.ShapeDtypeStruct((rows, n, width), BF16),
        in_specs=[pl.BlockSpec(memory_space=pltpu.HBM)],
        out_specs=VMEM,
        scratch_shapes=[pltpu.VMEM((n, rows, width), BF16), pltpu.SemaphoreType.DMA((n // EXAMPLES,))],
        compiler_params=pltpu.CompilerParams(vmem_limit_bytes=48 << 20),
        cost_estimate=pl.CostEstimate(flops=6_000_000_000, bytes_accessed=16_000_000, transcendentals=0),
    )(grads)


def inner_products(query_refs, grad_ref):
    total = sum(ref.shape[1] for ref in query_refs)

    def body(i, acc):
        at = [i * DEEP + j for j in range(DEEP)]
        queries = [jnp.concatenate([ref[r] for ref in query_refs], axis=0) for r in at]
        return acc + lax.dot_general(
            jnp.concatenate(queries, axis=1),
            jnp.concatenate([grad_ref[r] for r in at], axis=1),
            (((1,), (1,)), ((), ())),
            preferred_element_type=F32,
        )

    start = jnp.zeros((total, grad_ref.shape[1]), F32)
    return lax.fori_loop(0, grad_ref.shape[0] // DEEP, body, start)


def first_pass_kernel(ex, early_0, early_1, own_ref, near, mid, far_in, grad_ref, order_ref, out_ref):
    late = own_ref.shape[1]
    acc = inner_products((early_0, early_1, own_ref, near, mid, far_in), grad_ref)
    me = lax.axis_index("ex")
    sources = slot_sources(me)
    early = [acc[EARLY * s : EARLY * (s + 1)] for s in range(ex)]
    base = EARLY * ex
    slots = [acc[base + late * s : base + late * (s + 1)] for s in range(4)]
    for b in range(ex):
        block = order_ref[b]
        low = jnp.zeros_like(early[0])
        high = jnp.zeros_like(slots[0])
        for s in range(ex):
            hit = sources[s] == block
            low = low + jnp.where(hit, early[s], 0.0)
            high = high + jnp.where(hit, slots[s], 0.0)
        at = b * (EARLY + late)
        out_ref[at : at + EARLY, :] = low
        out_ref[at + EARLY : at + EARLY + late, :] = high


def slot_sources(me):
    low_pair = me < 2
    near = jnp.where(low_pair, 1 - me, 5 - me)
    return [me, near, jnp.where(low_pair, 2, 1), jnp.where(low_pair, 3, 0)]


def last_pass_kernel(ex, base_ref, far_out, grad_ref, order_ref, mine_ref, send_ref, full_ref):
    late = far_out.shape[1]
    acc = inner_products((far_out,), grad_ref)
    far = slot_sources(lax.axis_index("ex"))[3]
    full_ref[...] = base_ref[...]
    for b in range(ex):
        at = b * (EARLY + late) + EARLY
        full_ref[at : at + late, :] = full_ref[at : at + late, :] + jnp.where(order_ref[b] == far, acc, 0.0)
    half = mine_ref.shape[0]
    side = lax.axis_index("feat")
    mine_ref[...] = full_ref[pl.ds(pl.multiple_of(side * half, half), half), :]
    send_ref[...] = full_ref[pl.ds(pl.multiple_of((1 - side) * half, half), half), :]


def score_call(kernel, ex, arrays, order, out_shape, scratch=()):
    return pl.pallas_call(
        functools.partial(kernel, ex),
        out_shape=out_shape,
        in_specs=[VMEM] * len(arrays) + [SMEM],
        out_specs=jax.tree.map(lambda _: VMEM, out_shape),
        scratch_shapes=scratch,
        compiler_params=pltpu.CompilerParams(vmem_limit_bytes=40 << 20),
        cost_estimate=pl.CostEstimate(flops=3_000_000_000, bytes_accessed=12_000_000, transcendentals=0),
    )(*arrays, order)


def after(x, *others):
    return lax.optimization_barrier((x, *others))[0]


PAIRS = [(0, 1), (1, 0), (2, 3), (3, 2)]
MIDDLE = [(1, 2), (2, 1)]
OUTWARD = [(1, 0), (2, 3)]


def per_device_line(train_grads, queries, left_factor, right_factor, block_order):
    ex = lax.axis_size("ex")
    swap = [(0, 1), (1, 0)]
    count = queries.shape[1]
    n = train_grads.shape[0]
    late_raw = queries[0, EARLY:]
    late_other = lax.ppermute(late_raw, "feat", swap)
    raw = after(queries, late_raw)[0, :EARLY]
    terms = factor_terms(left_factor, after(right_factor, raw), train_grads.shape[1])
    raw_near = lax.ppermute(raw, "ex", PAIRS)
    raw_mid = lax.ppermute(raw, "ex", MIDDLE)
    raw_far_mid = lax.ppermute(after(raw_near, *terms), "ex", MIDDLE)
    raw_mid_out = lax.ppermute(raw_mid, "ex", OUTWARD)

    late = condition(after(late_raw, raw_near, raw_mid), late_other, *terms)
    near = lax.ppermute(late, "ex", PAIRS)
    mid = lax.ppermute(late, "ex", MIDDLE)
    grads = regroup(after(train_grads, late))
    early_0 = jnp.concatenate([raw, after(raw_near, late)], axis=0)
    early_0_other = lax.ppermute(early_0, "feat", swap)
    raw_far_out = lax.ppermute(after(raw_far_mid, grads), "ex", OUTWARD)
    far_mid = lax.ppermute(after(near, grads), "ex", MIDDLE)
    mid_out = lax.ppermute(after(mid, near, grads), "ex", OUTWARD)
    cond_0 = condition(after(early_0, near, mid), early_0_other, *terms)
    early_1 = jnp.concatenate([raw_mid + raw_mid_out, after(raw_far_mid, near, mid) + raw_far_out], axis=0)
    early_1_other = lax.ppermute(after(early_1, cond_0), "feat", swap)
    far_out = lax.ppermute(far_mid, "ex", OUTWARD)
    cond_1 = condition(after(early_1, far_mid), early_1_other, *terms)

    base = score_call(
        first_pass_kernel, ex, (cond_0, cond_1, late, near, mid + mid_out, far_mid, grads), block_order,
        jax.ShapeDtypeStruct((ex * count, n), F32),
    )
    half = jax.ShapeDtypeStruct((ex * count // 2, n), F32)
    mine, send = score_call(
        last_pass_kernel, ex, (base, far_out, grads), block_order, (half, half),
        [pltpu.VMEM((ex * count, n), F32)],
    )
    scores = mine + lax.ppermute(send, "feat", swap)
    return scores.T[:, None, :]


def per_device_gather(train_grads, queries, left_factor, right_factor, block_order):
    row_count = train_grads.shape[0]
    part_rows = train_grads.shape[1]
    right_width = train_grads.shape[2]
    flat_grads = train_grads.reshape(row_count, part_rows * right_width)
    local_queries = queries[0]
    block_size = local_queries.shape[0]
    regrouped = lax.all_to_all(local_queries, "feat", split_axis=0, concat_axis=1, tiled=True)
    whole_mix = jnp.einsum(
        "ik,qkj->qij", left_factor, regrouped.astype(F32), precision=lax.Precision.HIGHEST
    )
    whole_cond = jnp.einsum(
        "qij,jl->qil", whole_mix, right_factor, precision=lax.Precision.HIGHEST
    ).astype(BF16)
    conditioned = lax.all_to_all(whole_cond, "feat", split_axis=1, concat_axis=0, tiled=True)
    conditioned = conditioned.reshape(block_size, part_rows * right_width)
    partials = lax.dot_general(
        flat_grads,
        lax.all_gather(conditioned, "ex", axis=0, tiled=True),
        (((1,), (1,)), ((), ())),
        preferred_element_type=F32,
    )
    block_count = lax.axis_size("ex")
    partials = jnp.take(partials.reshape(row_count, block_count, block_size), block_order, axis=1)
    partials = partials.reshape(row_count, block_count * block_size)
    owned_scores = lax.psum_scatter(partials, "feat", scatter_dimension=1, tiled=True)
    return owned_scores.reshape(row_count, 1, owned_scores.shape[1])


def solution(mesh):
    short_line = mesh.shape["ex"] == 4 and mesh.shape["feat"] == 2
    return jax.shard_map(
        per_device_line if short_line else per_device_gather,
        mesh=mesh,
        in_specs=(
            P(("grp", "ex"), "feat", None),
            P("pb", ("grp", "ex"), "feat", None),
            P("grp", None),
            P("grp", None),
            P("grp"),
        ),
        out_specs=P(("grp", "ex"), "pb", "feat"),
        check_vma=False,
    )
```

```python
import functools

import jax
import jax.numpy as jnp
from jax import lax
from jax.experimental import pallas as pl
from jax.experimental.pallas import tpu as pltpu
from jax.sharding import PartitionSpec as P

F32 = jnp.float32
BF16 = jnp.bfloat16
EARLY = 4
TILE = 16
EXAMPLES = 32
DEEP = 32
VMEM = pl.BlockSpec(memory_space=pltpu.VMEM)
SMEM = pl.BlockSpec(memory_space=pltpu.SMEM)


def parts_of(x, count):
    terms = []
    for _ in range(count):
        top = x.astype(BF16)
        terms.append(top)
        x = x - top.astype(F32)
    return terms


def factor_kernel(left_ref, right_ref, left_out, right_out):
    rows = left_out.shape[0] // 3
    side = lax.axis_index("feat")
    here = pl.ds(pl.multiple_of(side * rows, rows), rows)
    there = pl.ds(pl.multiple_of((1 - side) * rows, rows), rows)
    left = jnp.concatenate([left_ref[here, here], left_ref[here, there]], axis=1)
    left_out[...] = jnp.concatenate(parts_of(left, 3), axis=0)
    right_out[...] = jnp.concatenate(parts_of(right_ref[...], 2), axis=0)


def factor_terms(left, right, rows):
    wide, width = left.shape[1], right.shape[1]
    return pl.pallas_call(
        factor_kernel,
        out_shape=(
            jax.ShapeDtypeStruct((3 * rows, wide), BF16),
            jax.ShapeDtypeStruct((2 * width, width), BF16),
        ),
        in_specs=[VMEM] * 2,
        out_specs=(VMEM, VMEM),
        compiler_params=pltpu.CompilerParams(vmem_limit_bytes=16 << 20),
    )(left, right)


def condition_kernel(own_ref, far_ref, left_ref, right_ref, out_ref, wide_ref):
    count, rows, width = own_ref.shape
    left_terms = left_ref[...]
    right_0, right_1 = right_ref[:width], right_ref[width:]
    for q in range(count):
        query = jnp.concatenate([own_ref[q], far_ref[q]], axis=0)
        mixed = jnp.dot(left_terms, query, preferred_element_type=F32)
        mixed = mixed[:rows] + (mixed[rows : 2 * rows] + mixed[2 * rows :])
        mixed_0, mixed_1 = parts_of(mixed, 2)
        both = jnp.dot(jnp.concatenate([mixed_0, mixed_1], axis=0), right_0, preferred_element_type=F32)
        cross = jnp.dot(mixed_0, right_1, preferred_element_type=F32)
        wide_ref[:, q, :] = both[:rows] + (both[rows:] + cross)
    out_ref[...] = wide_ref[...].astype(BF16)


def condition(own, far, left_terms, right_terms):
    count, rows, width = own.shape
    return pl.pallas_call(
        condition_kernel,
        out_shape=jax.ShapeDtypeStruct((rows, count, width), BF16),
        in_specs=[VMEM] * 4,
        out_specs=VMEM,
        scratch_shapes=[pltpu.VMEM((rows, count, width), F32)],
        compiler_params=pltpu.CompilerParams(vmem_limit_bytes=24 << 20),
        cost_estimate=pl.CostEstimate(flops=count * 3_000_000 * 40, bytes_accessed=8 * count * rows * width, transcendentals=0),
    )(own, far, left_terms, right_terms)


def regroup_kernel(grads_ref, out_ref, held_ref, sems):
    examples, rows, width = held_ref.shape
    blocks = examples // EXAMPLES
    copies = []
    for b in range(blocks):
        part = pl.ds(b * EXAMPLES, EXAMPLES)
        copies.append(pltpu.make_async_copy(grads_ref.at[part], held_ref.at[part], sems.at[b]))
        copies[-1].start()
    i = lax.broadcasted_iota(jnp.int32, (TILE * TILE, TILE * TILE), 0)
    j = lax.broadcasted_iota(jnp.int32, (TILE * TILE, TILE * TILE), 1)
    swap = jnp.where((i // TILE == j % TILE) & (i % TILE == j // TILE), 1.0, 0.0).astype(BF16)
    for b in range(blocks):
        copies[b].wait()

        @pl.loop(b * EXAMPLES // TILE, (b + 1) * EXAMPLES // TILE)
        def _(step):
            n = pl.ds(pl.multiple_of(step * TILE, TILE), TILE)
            for r in range(0, rows, TILE):
                tile = held_ref[n, r : r + TILE, :].reshape(TILE * TILE, width)
                turned = jnp.dot(swap, tile, preferred_element_type=F32).astype(BF16)
                out_ref[r : r + TILE, n, :] = turned.reshape(TILE, TILE, width)


def regroup(grads):
    n, rows, width = grads.shape
    return pl.pallas_call(
        regroup_kernel,
        out_shape=jax.ShapeDtypeStruct((rows, n, width), BF16),
        in_specs=[pl.BlockSpec(memory_space=pltpu.HBM)],
        out_specs=VMEM,
        scratch_shapes=[pltpu.VMEM((n, rows, width), BF16), pltpu.SemaphoreType.DMA((n // EXAMPLES,))],
        compiler_params=pltpu.CompilerParams(vmem_limit_bytes=48 << 20),
        cost_estimate=pl.CostEstimate(flops=6_000_000_000, bytes_accessed=16_000_000, transcendentals=0),
    )(grads)


def inner_products(query_refs, grad_ref):
    total = sum(ref.shape[1] for ref in query_refs)

    def body(i, acc):
        at = [i * DEEP + j for j in range(DEEP)]
        queries = [jnp.concatenate([ref[r] for ref in query_refs], axis=0) for r in at]
        return acc + lax.dot_general(
            jnp.concatenate(queries, axis=1),
            jnp.concatenate([grad_ref[r] for r in at], axis=1),
            (((1,), (1,)), ((), ())),
            preferred_element_type=F32,
        )

    start = jnp.zeros((total, grad_ref.shape[1]), F32)
    return lax.fori_loop(0, grad_ref.shape[0] // DEEP, body, start)


def first_pass_kernel(ex, early_0, early_1, own_ref, near, mid, far_in, grad_ref, order_ref, out_ref):
    late = own_ref.shape[1]
    acc = inner_products((early_0, early_1, own_ref, near, mid, far_in), grad_ref)
    me = lax.axis_index("ex")
    sources = slot_sources(me)
    early = [acc[EARLY * s : EARLY * (s + 1)] for s in range(ex)]
    base = EARLY * ex
    slots = [acc[base + late * s : base + late * (s + 1)] for s in range(4)]
    for b in range(ex):
        block = order_ref[b]
        low = jnp.zeros_like(early[0])
        high = jnp.zeros_like(slots[0])
        for s in range(ex):
            hit = sources[s] == block
            low = low + jnp.where(hit, early[s], 0.0)
            high = high + jnp.where(hit, slots[s], 0.0)
        at = b * (EARLY + late)
        out_ref[at : at + EARLY, :] = low
        out_ref[at + EARLY : at + EARLY + late, :] = high


def slot_sources(me):
    low_pair = me < 2
    near = jnp.where(low_pair, 1 - me, 5 - me)
    return [me, near, jnp.where(low_pair, 2, 1), jnp.where(low_pair, 3, 0)]


def last_pass_kernel(ex, base_ref, far_out, grad_ref, order_ref, mine_ref, send_ref, full_ref):
    late = far_out.shape[1]
    acc = inner_products((far_out,), grad_ref)
    far = slot_sources(lax.axis_index("ex"))[3]
    full_ref[...] = base_ref[...]
    for b in range(ex):
        at = b * (EARLY + late) + EARLY
        full_ref[at : at + late, :] = full_ref[at : at + late, :] + jnp.where(order_ref[b] == far, acc, 0.0)
    half = mine_ref.shape[0]
    side = lax.axis_index("feat")
    mine_ref[...] = full_ref[pl.ds(pl.multiple_of(side * half, half), half), :]
    send_ref[...] = full_ref[pl.ds(pl.multiple_of((1 - side) * half, half), half), :]


def score_call(kernel, ex, arrays, order, out_shape, scratch=()):
    return pl.pallas_call(
        functools.partial(kernel, ex),
        out_shape=out_shape,
        in_specs=[VMEM] * len(arrays) + [SMEM],
        out_specs=jax.tree.map(lambda _: VMEM, out_shape),
        scratch_shapes=scratch,
        compiler_params=pltpu.CompilerParams(vmem_limit_bytes=40 << 20),
        cost_estimate=pl.CostEstimate(flops=3_000_000_000, bytes_accessed=12_000_000, transcendentals=0),
    )(*arrays, order)


def after(x, *others):
    return lax.optimization_barrier((x, *others))[0]


PAIRS = [(0, 1), (1, 0), (2, 3), (3, 2)]
MIDDLE = [(1, 2), (2, 1)]
OUTWARD = [(1, 0), (2, 3)]


def per_device_line(train_grads, queries, left_factor, right_factor, block_order):
    ex = lax.axis_size("ex")
    swap = [(0, 1), (1, 0)]
    count = queries.shape[1]
    n = train_grads.shape[0]
    late_raw = queries[0, EARLY:]
    late_other = lax.ppermute(late_raw, "feat", swap)
    raw = after(queries, late_raw)[0, :EARLY]
    terms = factor_terms(left_factor, after(right_factor, raw), train_grads.shape[1])
    raw_mid = lax.ppermute(raw, "ex", MIDDLE)
    raw_near = lax.ppermute(raw, "ex", PAIRS)
    raw_far_mid = lax.ppermute(after(raw_near, late_other), "ex", MIDDLE)
    raw_mid_out = lax.ppermute(after(raw_mid, *terms), "ex", OUTWARD)

    late = condition(after(late_raw, raw_near, raw_mid), late_other, *terms)
    near = lax.ppermute(late, "ex", PAIRS)
    mid = lax.ppermute(late, "ex", MIDDLE)
    grads = regroup(after(train_grads, late))
    early_0 = jnp.concatenate([raw, after(raw_near, late)], axis=0)
    early_0_other = lax.ppermute(early_0, "feat", swap)
    raw_far_out = lax.ppermute(after(raw_far_mid, grads), "ex", OUTWARD)
    far_mid = lax.ppermute(after(near, grads), "ex", MIDDLE)
    mid_out = lax.ppermute(after(mid, near, grads), "ex", OUTWARD)
    cond_0 = condition(after(early_0, near, mid), early_0_other, *terms)
    early_1 = jnp.concatenate([raw_mid + raw_mid_out, after(raw_far_mid, near, mid) + raw_far_out], axis=0)
    early_1_other = lax.ppermute(after(early_1, cond_0), "feat", swap)
    far_out = lax.ppermute(far_mid, "ex", OUTWARD)
    cond_1 = condition(after(early_1, far_mid), early_1_other, *terms)

    base = score_call(
        first_pass_kernel, ex, (cond_0, cond_1, late, near, mid + mid_out, far_mid, grads), block_order,
        jax.ShapeDtypeStruct((ex * count, n), F32),
    )
    half = jax.ShapeDtypeStruct((ex * count // 2, n), F32)
    mine, send = score_call(
        last_pass_kernel, ex, (base, far_out, grads), block_order, (half, half),
        [pltpu.VMEM((ex * count, n), F32)],
    )
    scores = mine + lax.ppermute(send, "feat", swap)
    return scores.T[:, None, :]


def per_device_gather(train_grads, queries, left_factor, right_factor, block_order):
    row_count = train_grads.shape[0]
    part_rows = train_grads.shape[1]
    right_width = train_grads.shape[2]
    flat_grads = train_grads.reshape(row_count, part_rows * right_width)
    local_queries = queries[0]
    block_size = local_queries.shape[0]
    regrouped = lax.all_to_all(local_queries, "feat", split_axis=0, concat_axis=1, tiled=True)
    whole_mix = jnp.einsum(
        "ik,qkj->qij", left_factor, regrouped.astype(F32), precision=lax.Precision.HIGHEST
    )
    whole_cond = jnp.einsum(
        "qij,jl->qil", whole_mix, right_factor, precision=lax.Precision.HIGHEST
    ).astype(BF16)
    conditioned = lax.all_to_all(whole_cond, "feat", split_axis=1, concat_axis=0, tiled=True)
    conditioned = conditioned.reshape(block_size, part_rows * right_width)
    partials = lax.dot_general(
        flat_grads,
        lax.all_gather(conditioned, "ex", axis=0, tiled=True),
        (((1,), (1,)), ((), ())),
        preferred_element_type=F32,
    )
    block_count = lax.axis_size("ex")
    partials = jnp.take(partials.reshape(row_count, block_count, block_size), block_order, axis=1)
    partials = partials.reshape(row_count, block_count * block_size)
    owned_scores = lax.psum_scatter(partials, "feat", scatter_dimension=1, tiled=True)
    return owned_scores.reshape(row_count, 1, owned_scores.shape[1])


def solution(mesh):
    short_line = mesh.shape["ex"] == 4 and mesh.shape["feat"] == 2
    return jax.shard_map(
        per_device_line if short_line else per_device_gather,
        mesh=mesh,
        in_specs=(
            P(("grp", "ex"), "feat", None),
            P("pb", ("grp", "ex"), "feat", None),
            P("grp", None),
            P("grp", None),
            P("grp"),
        ),
        out_specs=P(("grp", "ex"), "pb", "feat"),
        check_vma=False,
    )
```

```python
import functools

import jax
import jax.numpy as jnp
from jax import lax
from jax.experimental import pallas as pl
from jax.experimental.pallas import tpu as pltpu
from jax.sharding import PartitionSpec as P

F32 = jnp.float32
BF16 = jnp.bfloat16
EARLY = 4
TILE = 16
EXAMPLES = 32
DEEP = 32
VMEM = pl.BlockSpec(memory_space=pltpu.VMEM)
SMEM = pl.BlockSpec(memory_space=pltpu.SMEM)


def parts_of(x, count):
    terms = []
    for _ in range(count):
        top = x.astype(BF16)
        terms.append(top)
        x = x - top.astype(F32)
    return terms


def factor_kernel(left_ref, right_ref, left_out, right_out):
    rows = left_out.shape[0] // 3
    side = lax.axis_index("feat")
    here = pl.ds(pl.multiple_of(side * rows, rows), rows)
    there = pl.ds(pl.multiple_of((1 - side) * rows, rows), rows)
    left = jnp.concatenate([left_ref[here, here], left_ref[here, there]], axis=1)
    left_out[...] = jnp.concatenate(parts_of(left, 3), axis=0)
    right_out[...] = jnp.concatenate(parts_of(right_ref[...], 2), axis=0)


def factor_terms(left, right, rows):
    wide, width = left.shape[1], right.shape[1]
    return pl.pallas_call(
        factor_kernel,
        out_shape=(
            jax.ShapeDtypeStruct((3 * rows, wide), BF16),
            jax.ShapeDtypeStruct((2 * width, width), BF16),
        ),
        in_specs=[VMEM] * 2,
        out_specs=(VMEM, VMEM),
        compiler_params=pltpu.CompilerParams(vmem_limit_bytes=16 << 20),
    )(left, right)


def condition_kernel(own_ref, far_ref, left_ref, right_ref, out_ref, wide_ref):
    count, rows, width = own_ref.shape
    left_terms = left_ref[...]
    right_0, right_1 = right_ref[:width], right_ref[width:]
    for q in range(count):
        query = jnp.concatenate([own_ref[q], far_ref[q]], axis=0)
        mixed = jnp.dot(left_terms, query, preferred_element_type=F32)
        mixed = mixed[:rows] + (mixed[rows : 2 * rows] + mixed[2 * rows :])
        mixed_0, mixed_1 = parts_of(mixed, 2)
        both = jnp.dot(jnp.concatenate([mixed_0, mixed_1], axis=0), right_0, preferred_element_type=F32)
        cross = jnp.dot(mixed_0, right_1, preferred_element_type=F32)
        wide_ref[:, q, :] = both[:rows] + (both[rows:] + cross)
    out_ref[...] = wide_ref[...].astype(BF16)


def condition(own, far, left_terms, right_terms):
    count, rows, width = own.shape
    return pl.pallas_call(
        condition_kernel,
        out_shape=jax.ShapeDtypeStruct((rows, count, width), BF16),
        in_specs=[VMEM] * 4,
        out_specs=VMEM,
        scratch_shapes=[pltpu.VMEM((rows, count, width), F32)],
        compiler_params=pltpu.CompilerParams(vmem_limit_bytes=24 << 20),
        cost_estimate=pl.CostEstimate(flops=count * 3_000_000 * 40, bytes_accessed=8 * count * rows * width, transcendentals=0),
    )(own, far, left_terms, right_terms)


def regroup_kernel(grads_ref, out_ref, held_ref, sems):
    examples, rows, width = held_ref.shape
    blocks = examples // EXAMPLES
    copies = []
    for b in range(blocks):
        part = pl.ds(b * EXAMPLES, EXAMPLES)
        copies.append(pltpu.make_async_copy(grads_ref.at[part], held_ref.at[part], sems.at[b]))
        copies[-1].start()
    i = lax.broadcasted_iota(jnp.int32, (TILE * TILE, TILE * TILE), 0)
    j = lax.broadcasted_iota(jnp.int32, (TILE * TILE, TILE * TILE), 1)
    swap = jnp.where((i // TILE == j % TILE) & (i % TILE == j // TILE), 1.0, 0.0).astype(BF16)
    for b in range(blocks):
        copies[b].wait()

        @pl.loop(b * EXAMPLES // TILE, (b + 1) * EXAMPLES // TILE)
        def _(step):
            n = pl.ds(pl.multiple_of(step * TILE, TILE), TILE)
            for r in range(0, rows, TILE):
                tile = held_ref[n, r : r + TILE, :].reshape(TILE * TILE, width)
                turned = jnp.dot(swap, tile, preferred_element_type=F32).astype(BF16)
                out_ref[r : r + TILE, n, :] = turned.reshape(TILE, TILE, width)


def regroup(grads):
    n, rows, width = grads.shape
    return pl.pallas_call(
        regroup_kernel,
        out_shape=jax.ShapeDtypeStruct((rows, n, width), BF16),
        in_specs=[pl.BlockSpec(memory_space=pltpu.HBM)],
        out_specs=VMEM,
        scratch_shapes=[pltpu.VMEM((n, rows, width), BF16), pltpu.SemaphoreType.DMA((n // EXAMPLES,))],
        compiler_params=pltpu.CompilerParams(vmem_limit_bytes=48 << 20),
        cost_estimate=pl.CostEstimate(flops=6_000_000_000, bytes_accessed=16_000_000, transcendentals=0),
    )(grads)


def inner_products(query_refs, grad_ref, first=0):
    total = sum(ref.shape[1] for ref in query_refs)

    def body(i, acc):
        at = [i * DEEP + j for j in range(DEEP)]
        queries = [jnp.concatenate([ref[r] for ref in query_refs], axis=0) for r in at]
        return acc + lax.dot_general(
            jnp.concatenate(queries, axis=1),
            jnp.concatenate([grad_ref[first + r] for r in at], axis=1),
            (((1,), (1,)), ((), ())),
            preferred_element_type=F32,
        )

    start = jnp.zeros((total, grad_ref.shape[1]), F32)
    return lax.fori_loop(0, query_refs[0].shape[0] // DEEP, body, start)


def first_pass_kernel(ex, early_0, early_1, own_ref, near, mid, far_in, grad_ref, order_ref, out_ref):
    late = own_ref.shape[1]
    acc = inner_products((early_0, early_1, own_ref, near, mid, far_in), grad_ref)
    me = lax.axis_index("ex")
    sources = slot_sources(me)
    early = [acc[EARLY * s : EARLY * (s + 1)] for s in range(ex)]
    base = EARLY * ex
    slots = [acc[base + late * s : base + late * (s + 1)] for s in range(4)]
    for b in range(ex):
        block = order_ref[b]
        low = jnp.zeros_like(early[0])
        high = jnp.zeros_like(slots[0])
        for s in range(ex):
            hit = sources[s] == block
            low = low + jnp.where(hit, early[s], 0.0)
            high = high + jnp.where(hit, slots[s], 0.0)
        at = b * (EARLY + late)
        out_ref[at : at + EARLY, :] = low
        out_ref[at + EARLY : at + EARLY + late, :] = high


def slot_sources(me):
    low_pair = me < 2
    near = jnp.where(low_pair, 1 - me, 5 - me)
    return [me, near, jnp.where(low_pair, 2, 1), jnp.where(low_pair, 3, 0)]


def far_pass_kernel(ex, far_out, grad_ref, order_ref, out_ref):
    out_ref[...] = inner_products((far_out,), grad_ref)


def last_pass_kernel(ex, base_ref, far_ref, far_out, grad_ref, order_ref, mine_ref, send_ref, full_ref):
    late = far_out.shape[1]
    acc = far_ref[...] + inner_products((far_out,), grad_ref, far_out.shape[0])
    far = slot_sources(lax.axis_index("ex"))[3]
    full_ref[...] = base_ref[...]
    for b in range(ex):
        at = b * (EARLY + late) + EARLY
        full_ref[at : at + late, :] = full_ref[at : at + late, :] + jnp.where(order_ref[b] == far, acc, 0.0)
    half = mine_ref.shape[0]
    side = lax.axis_index("feat")
    mine_ref[...] = full_ref[pl.ds(pl.multiple_of(side * half, half), half), :]
    send_ref[...] = full_ref[pl.ds(pl.multiple_of((1 - side) * half, half), half), :]


def score_call(kernel, ex, arrays, order, out_shape, scratch=()):
    return pl.pallas_call(
        functools.partial(kernel, ex),
        out_shape=out_shape,
        in_specs=[VMEM] * len(arrays) + [SMEM],
        out_specs=jax.tree.map(lambda _: VMEM, out_shape),
        scratch_shapes=scratch,
        compiler_params=pltpu.CompilerParams(vmem_limit_bytes=40 << 20),
        cost_estimate=pl.CostEstimate(flops=3_000_000_000, bytes_accessed=12_000_000, transcendentals=0),
    )(*arrays, order)


def after(x, *others):
    return lax.optimization_barrier((x, *others))[0]


PAIRS = [(0, 1), (1, 0), (2, 3), (3, 2)]
MIDDLE = [(1, 2), (2, 1)]
OUTWARD = [(1, 0), (2, 3)]


def per_device_line(train_grads, queries, left_factor, right_factor, block_order):
    ex = lax.axis_size("ex")
    swap = [(0, 1), (1, 0)]
    count = queries.shape[1]
    n = train_grads.shape[0]
    late_raw = queries[0, EARLY:]
    late_other = lax.ppermute(late_raw, "feat", swap)
    raw = after(queries, late_raw)[0, :EARLY]
    terms = factor_terms(left_factor, after(right_factor, raw), train_grads.shape[1])
    raw_near = lax.ppermute(raw, "ex", PAIRS)
    raw_mid = lax.ppermute(raw, "ex", MIDDLE)
    raw_mid_out = lax.ppermute(after(raw_mid, *terms), "ex", OUTWARD)
    early_0 = jnp.concatenate([raw, after(raw_near, raw_mid)], axis=0)
    raw_far_mid = lax.ppermute(after(raw_near, early_0), "ex", MIDDLE)

    late = condition(after(late_raw, raw_near, raw_mid), late_other, *terms)
    near = lax.ppermute(late, "ex", PAIRS)
    mid = lax.ppermute(late, "ex", MIDDLE)
    grads = regroup(after(train_grads, late))
    early_0_other = lax.ppermute(after(early_0, late), "feat", swap)
    raw_far_out = lax.ppermute(after(raw_far_mid, grads), "ex", OUTWARD)
    far_mid = lax.ppermute(after(near, grads), "ex", MIDDLE)
    mid_out = lax.ppermute(after(mid, near, grads), "ex", OUTWARD)
    cond_0 = condition(after(early_0, near, mid), early_0_other, *terms)
    early_1 = jnp.concatenate([raw_mid + raw_mid_out, after(raw_far_mid, near, mid) + raw_far_out], axis=0)
    early_1_other = lax.ppermute(after(early_1, cond_0), "feat", swap)
    part = far_mid.shape[0] // 2
    far_out_0 = lax.ppermute(far_mid[:part], "ex", OUTWARD)
    far_out_1 = lax.ppermute(far_mid[part:], "ex", OUTWARD)
    cond_1 = condition(after(early_1, far_mid), early_1_other, *terms)

    base = score_call(
        first_pass_kernel, ex, (cond_0, cond_1, late, near, mid + mid_out, far_mid, grads), block_order,
        jax.ShapeDtypeStruct((ex * count, n), F32),
    )
    far_0 = score_call(
        far_pass_kernel, ex, (far_out_0, after(grads, base)), block_order,
        jax.ShapeDtypeStruct((count - EARLY, n), F32),
    )
    half = jax.ShapeDtypeStruct((ex * count // 2, n), F32)
    mine, send = score_call(
        last_pass_kernel, ex, (base, far_0, far_out_1, grads), block_order, (half, half),
        [pltpu.VMEM((ex * count, n), F32)],
    )
    scores = mine + lax.ppermute(send, "feat", swap)
    return scores.T[:, None, :]


def per_device_gather(train_grads, queries, left_factor, right_factor, block_order):
    row_count = train_grads.shape[0]
    part_rows = train_grads.shape[1]
    right_width = train_grads.shape[2]
    flat_grads = train_grads.reshape(row_count, part_rows * right_width)
    local_queries = queries[0]
    block_size = local_queries.shape[0]
    regrouped = lax.all_to_all(local_queries, "feat", split_axis=0, concat_axis=1, tiled=True)
    whole_mix = jnp.einsum(
        "ik,qkj->qij", left_factor, regrouped.astype(F32), precision=lax.Precision.HIGHEST
    )
    whole_cond = jnp.einsum(
        "qij,jl->qil", whole_mix, right_factor, precision=lax.Precision.HIGHEST
    ).astype(BF16)
    conditioned = lax.all_to_all(whole_cond, "feat", split_axis=1, concat_axis=0, tiled=True)
    conditioned = conditioned.reshape(block_size, part_rows * right_width)
    partials = lax.dot_general(
        flat_grads,
        lax.all_gather(conditioned, "ex", axis=0, tiled=True),
        (((1,), (1,)), ((), ())),
        preferred_element_type=F32,
    )
    block_count = lax.axis_size("ex")
    partials = jnp.take(partials.reshape(row_count, block_count, block_size), block_order, axis=1)
    partials = partials.reshape(row_count, block_count * block_size)
    owned_scores = lax.psum_scatter(partials, "feat", scatter_dimension=1, tiled=True)
    return owned_scores.reshape(row_count, 1, owned_scores.shape[1])


def solution(mesh):
    short_line = mesh.shape["ex"] == 4 and mesh.shape["feat"] == 2
    return jax.shard_map(
        per_device_line if short_line else per_device_gather,
        mesh=mesh,
        in_specs=(
            P(("grp", "ex"), "feat", None),
            P("pb", ("grp", "ex"), "feat", None),
            P("grp", None),
            P("grp", None),
            P("grp"),
        ),
        out_specs=P(("grp", "ex"), "pb", "feat"),
        check_vma=False,
    )
```

```python
import functools

import jax
import jax.numpy as jnp
from jax import lax
from jax.experimental import pallas as pl
from jax.experimental.pallas import tpu as pltpu
from jax.sharding import PartitionSpec as P

F32 = jnp.float32
BF16 = jnp.bfloat16
EARLY = 4
TILE = 16
EXAMPLES = 32
DEEP = 32
VMEM = pl.BlockSpec(memory_space=pltpu.VMEM)
SMEM = pl.BlockSpec(memory_space=pltpu.SMEM)


def parts_of(x, count):
    terms = []
    for _ in range(count):
        top = x.astype(BF16)
        terms.append(top)
        x = x - top.astype(F32)
    return terms


def factor_kernel(left_ref, right_ref, left_out, right_out):
    rows = left_out.shape[0] // 3
    side = lax.axis_index("feat")
    here = pl.ds(pl.multiple_of(side * rows, rows), rows)
    there = pl.ds(pl.multiple_of((1 - side) * rows, rows), rows)
    left = jnp.concatenate([left_ref[here, here], left_ref[here, there]], axis=1)
    left_out[...] = jnp.concatenate(parts_of(left, 3), axis=0)
    right_out[...] = jnp.concatenate(parts_of(right_ref[...], 2), axis=0)


def factor_terms(left, right, rows):
    wide, width = left.shape[1], right.shape[1]
    return pl.pallas_call(
        factor_kernel,
        out_shape=(
            jax.ShapeDtypeStruct((3 * rows, wide), BF16),
            jax.ShapeDtypeStruct((2 * width, width), BF16),
        ),
        in_specs=[VMEM] * 2,
        out_specs=(VMEM, VMEM),
        compiler_params=pltpu.CompilerParams(vmem_limit_bytes=16 << 20),
    )(left, right)


def condition_kernel(own_ref, far_ref, left_ref, right_ref, out_ref, wide_ref):
    count, rows, width = own_ref.shape
    left_terms = left_ref[...]
    right_0, right_1 = right_ref[:width], right_ref[width:]
    for q in range(count):
        query = jnp.concatenate([own_ref[q], far_ref[q]], axis=0)
        mixed = jnp.dot(left_terms, query, preferred_element_type=F32)
        mixed = mixed[:rows] + (mixed[rows : 2 * rows] + mixed[2 * rows :])
        mixed_0, mixed_1 = parts_of(mixed, 2)
        both = jnp.dot(jnp.concatenate([mixed_0, mixed_1], axis=0), right_0, preferred_element_type=F32)
        cross = jnp.dot(mixed_0, right_1, preferred_element_type=F32)
        wide_ref[:, q, :] = both[:rows] + (both[rows:] + cross)
    out_ref[...] = wide_ref[...].astype(BF16)


def condition(own, far, left_terms, right_terms):
    count, rows, width = own.shape
    return pl.pallas_call(
        condition_kernel,
        out_shape=jax.ShapeDtypeStruct((rows, count, width), BF16),
        in_specs=[VMEM] * 4,
        out_specs=VMEM,
        scratch_shapes=[pltpu.VMEM((rows, count, width), F32)],
        compiler_params=pltpu.CompilerParams(vmem_limit_bytes=24 << 20),
        cost_estimate=pl.CostEstimate(flops=count * 3_000_000 * 40, bytes_accessed=8 * count * rows * width, transcendentals=0),
    )(own, far, left_terms, right_terms)


def regroup_kernel(grads_ref, out_ref, held_ref, sems):
    examples, rows, width = held_ref.shape
    blocks = examples // EXAMPLES
    copies = []
    for b in range(blocks):
        part = pl.ds(b * EXAMPLES, EXAMPLES)
        copies.append(pltpu.make_async_copy(grads_ref.at[part], held_ref.at[part], sems.at[b]))
        copies[-1].start()
    i = lax.broadcasted_iota(jnp.int32, (TILE * TILE, TILE * TILE), 0)
    j = lax.broadcasted_iota(jnp.int32, (TILE * TILE, TILE * TILE), 1)
    swap = jnp.where((i // TILE == j % TILE) & (i % TILE == j // TILE), 1.0, 0.0).astype(BF16)
    for b in range(blocks):
        copies[b].wait()

        @pl.loop(b * EXAMPLES // TILE, (b + 1) * EXAMPLES // TILE)
        def _(step):
            n = pl.ds(pl.multiple_of(step * TILE, TILE), TILE)
            for r in range(0, rows, TILE):
                tile = held_ref[n, r : r + TILE, :].reshape(TILE * TILE, width)
                turned = jnp.dot(swap, tile, preferred_element_type=F32).astype(BF16)
                out_ref[r : r + TILE, n, :] = turned.reshape(TILE, TILE, width)


def regroup(grads):
    n, rows, width = grads.shape
    return pl.pallas_call(
        regroup_kernel,
        out_shape=jax.ShapeDtypeStruct((rows, n, width), BF16),
        in_specs=[pl.BlockSpec(memory_space=pltpu.HBM)],
        out_specs=VMEM,
        scratch_shapes=[pltpu.VMEM((n, rows, width), BF16), pltpu.SemaphoreType.DMA((n // EXAMPLES,))],
        compiler_params=pltpu.CompilerParams(vmem_limit_bytes=48 << 20),
        cost_estimate=pl.CostEstimate(flops=6_000_000_000, bytes_accessed=16_000_000, transcendentals=0),
    )(grads)


def inner_products(query_refs, grad_ref, first=0):
    total = sum(ref.shape[1] for ref in query_refs)

    def body(i, acc):
        at = [i * DEEP + j for j in range(DEEP)]
        queries = [jnp.concatenate([ref[r] for ref in query_refs], axis=0) for r in at]
        return acc + lax.dot_general(
            jnp.concatenate(queries, axis=1),
            jnp.concatenate([grad_ref[first + r] for r in at], axis=1),
            (((1,), (1,)), ((), ())),
            preferred_element_type=F32,
        )

    start = jnp.zeros((total, grad_ref.shape[1]), F32)
    return lax.fori_loop(0, query_refs[0].shape[0] // DEEP, body, start)


def first_pass_kernel(ex, early_0, early_1, own_ref, near, mid, far_in, grad_ref, order_ref, out_ref):
    late = own_ref.shape[1]
    acc = inner_products((early_0, early_1, own_ref, near, mid, far_in), grad_ref)
    me = lax.axis_index("ex")
    sources = slot_sources(me)
    early = [acc[EARLY * s : EARLY * (s + 1)] for s in range(ex)]
    base = EARLY * ex
    slots = [acc[base + late * s : base + late * (s + 1)] for s in range(4)]
    for b in range(ex):
        block = order_ref[b]
        low = jnp.zeros_like(early[0])
        high = jnp.zeros_like(slots[0])
        for s in range(ex):
            hit = sources[s] == block
            low = low + jnp.where(hit, early[s], 0.0)
            high = high + jnp.where(hit, slots[s], 0.0)
        at = b * (EARLY + late)
        out_ref[at : at + EARLY, :] = low
        out_ref[at + EARLY : at + EARLY + late, :] = high


def slot_sources(me):
    low_pair = me < 2
    near = jnp.where(low_pair, 1 - me, 5 - me)
    return [me, near, jnp.where(low_pair, 2, 1), jnp.where(low_pair, 3, 0)]


def far_pass_kernel(ex, far_out, grad_ref, order_ref, out_ref):
    out_ref[...] = inner_products((far_out,), grad_ref)


def last_pass_kernel(ex, base_ref, far_ref, far_out, grad_ref, order_ref, mine_ref, send_ref, full_ref):
    late = far_out.shape[1]
    acc = far_ref[...] + inner_products((far_out,), grad_ref, far_out.shape[0])
    far = slot_sources(lax.axis_index("ex"))[3]
    full_ref[...] = base_ref[...]
    for b in range(ex):
        at = b * (EARLY + late) + EARLY
        full_ref[at : at + late, :] = full_ref[at : at + late, :] + jnp.where(order_ref[b] == far, acc, 0.0)
    half = mine_ref.shape[0]
    side = lax.axis_index("feat")
    mine_ref[...] = full_ref[pl.ds(pl.multiple_of(side * half, half), half), :]
    send_ref[...] = full_ref[pl.ds(pl.multiple_of((1 - side) * half, half), half), :]


def score_call(kernel, ex, arrays, order, out_shape, scratch=()):
    return pl.pallas_call(
        functools.partial(kernel, ex),
        out_shape=out_shape,
        in_specs=[VMEM] * len(arrays) + [SMEM],
        out_specs=jax.tree.map(lambda _: VMEM, out_shape),
        scratch_shapes=scratch,
        compiler_params=pltpu.CompilerParams(vmem_limit_bytes=40 << 20),
        cost_estimate=pl.CostEstimate(flops=1000, bytes_accessed=1000, transcendentals=0),
    )(*arrays, order)


def after(x, *others):
    return lax.optimization_barrier((x, *others))[0]


PAIRS = [(0, 1), (1, 0), (2, 3), (3, 2)]
MIDDLE = [(1, 2), (2, 1)]
OUTWARD = [(1, 0), (2, 3)]


def per_device_line(train_grads, queries, left_factor, right_factor, block_order):
    ex = lax.axis_size("ex")
    swap = [(0, 1), (1, 0)]
    count = queries.shape[1]
    n = train_grads.shape[0]
    late_raw = queries[0, EARLY:]
    late_other = lax.ppermute(late_raw, "feat", swap)
    raw = after(queries, late_raw)[0, :EARLY]
    terms = factor_terms(left_factor, after(right_factor, raw), train_grads.shape[1])
    raw_near = lax.ppermute(raw, "ex", PAIRS)
    raw_mid = lax.ppermute(raw, "ex", MIDDLE)
    raw_mid_out = lax.ppermute(after(raw_mid, *terms), "ex", OUTWARD)
    early_0 = jnp.concatenate([raw, after(raw_near, raw_mid)], axis=0)
    raw_far_mid = lax.ppermute(after(raw_near, early_0), "ex", MIDDLE)

    late = condition(after(late_raw, raw_near, raw_mid), late_other, *terms)
    near = lax.ppermute(late, "ex", PAIRS)
    mid = lax.ppermute(late, "ex", MIDDLE)
    grads = regroup(after(train_grads, late))
    early_0_other = lax.ppermute(after(early_0, late), "feat", swap)
    raw_far_out = lax.ppermute(after(raw_far_mid, grads), "ex", OUTWARD)
    far_mid = lax.ppermute(after(near, grads), "ex", MIDDLE)
    mid_out = lax.ppermute(after(mid, near, grads), "ex", OUTWARD)
    cond_0 = condition(after(early_0, near, mid), early_0_other, *terms)
    early_1 = jnp.concatenate([raw_mid + raw_mid_out, after(raw_far_mid, near, mid) + raw_far_out], axis=0)
    early_1_other = lax.ppermute(after(early_1, cond_0), "feat", swap)
    part = far_mid.shape[0] // 2
    far_out_0 = lax.ppermute(far_mid[:part], "ex", OUTWARD)
    far_out_1 = lax.ppermute(far_mid[part:], "ex", OUTWARD)
    cond_1 = condition(after(early_1, far_mid), early_1_other, *terms)

    base = score_call(
        first_pass_kernel, ex, (cond_0, cond_1, late, near, mid + mid_out, far_mid, grads), block_order,
        jax.ShapeDtypeStruct((ex * count, n), F32),
    )
    far_0 = score_call(
        far_pass_kernel, ex, (far_out_0, after(grads, base)), block_order,
        jax.ShapeDtypeStruct((count - EARLY, n), F32),
    )
    half = jax.ShapeDtypeStruct((ex * count // 2, n), F32)
    mine, send = score_call(
        last_pass_kernel, ex, (base, far_0, far_out_1, grads), block_order, (half, half),
        [pltpu.VMEM((ex * count, n), F32)],
    )
    scores = mine + lax.ppermute(send, "feat", swap)
    return scores.T[:, None, :]


def per_device_gather(train_grads, queries, left_factor, right_factor, block_order):
    row_count = train_grads.shape[0]
    part_rows = train_grads.shape[1]
    right_width = train_grads.shape[2]
    flat_grads = train_grads.reshape(row_count, part_rows * right_width)
    local_queries = queries[0]
    block_size = local_queries.shape[0]
    regrouped = lax.all_to_all(local_queries, "feat", split_axis=0, concat_axis=1, tiled=True)
    whole_mix = jnp.einsum(
        "ik,qkj->qij", left_factor, regrouped.astype(F32), precision=lax.Precision.HIGHEST
    )
    whole_cond = jnp.einsum(
        "qij,jl->qil", whole_mix, right_factor, precision=lax.Precision.HIGHEST
    ).astype(BF16)
    conditioned = lax.all_to_all(whole_cond, "feat", split_axis=1, concat_axis=0, tiled=True)
    conditioned = conditioned.reshape(block_size, part_rows * right_width)
    partials = lax.dot_general(
        flat_grads,
        lax.all_gather(conditioned, "ex", axis=0, tiled=True),
        (((1,), (1,)), ((), ())),
        preferred_element_type=F32,
    )
    block_count = lax.axis_size("ex")
    partials = jnp.take(partials.reshape(row_count, block_count, block_size), block_order, axis=1)
    partials = partials.reshape(row_count, block_count * block_size)
    owned_scores = lax.psum_scatter(partials, "feat", scatter_dimension=1, tiled=True)
    return owned_scores.reshape(row_count, 1, owned_scores.shape[1])


def solution(mesh):
    short_line = mesh.shape["ex"] == 4 and mesh.shape["feat"] == 2
    return jax.shard_map(
        per_device_line if short_line else per_device_gather,
        mesh=mesh,
        in_specs=(
            P(("grp", "ex"), "feat", None),
            P("pb", ("grp", "ex"), "feat", None),
            P("grp", None),
            P("grp", None),
            P("grp"),
        ),
        out_specs=P(("grp", "ex"), "pb", "feat"),
        check_vma=False,
    )
```

```python
import functools

import jax
import jax.numpy as jnp
from jax import lax
from jax.experimental import pallas as pl
from jax.experimental.pallas import tpu as pltpu
from jax.sharding import PartitionSpec as P

F32 = jnp.float32
BF16 = jnp.bfloat16
EARLY = 4
SHARED = 16
TILE = 16
EXAMPLES = 32
DEEP = 32
VMEM = pl.BlockSpec(memory_space=pltpu.VMEM)
SMEM = pl.BlockSpec(memory_space=pltpu.SMEM)


def parts_of(x, count):
    terms = []
    for _ in range(count):
        top = x.astype(BF16)
        terms.append(top)
        x = x - top.astype(F32)
    return terms


def factor_kernel(left_ref, right_ref, left_out, right_out):
    rows = left_out.shape[0] // 3
    side = lax.axis_index("feat")
    here = pl.ds(pl.multiple_of(side * rows, rows), rows)
    there = pl.ds(pl.multiple_of((1 - side) * rows, rows), rows)
    left = jnp.concatenate([left_ref[here, here], left_ref[here, there]], axis=1)
    left_out[...] = jnp.concatenate(parts_of(left, 3), axis=0)
    right_out[...] = jnp.concatenate(parts_of(right_ref[...], 2), axis=0)


def factor_terms(left, right, rows):
    wide, width = left.shape[1], right.shape[1]
    return pl.pallas_call(
        factor_kernel,
        out_shape=(
            jax.ShapeDtypeStruct((3 * rows, wide), BF16),
            jax.ShapeDtypeStruct((2 * width, width), BF16),
        ),
        in_specs=[VMEM] * 2,
        out_specs=(VMEM, VMEM),
        compiler_params=pltpu.CompilerParams(vmem_limit_bytes=16 << 20),
    )(left, right)


def condition_kernel(own_ref, far_ref, left_ref, right_ref, out_ref, wide_ref):
    count, rows, width = own_ref.shape
    left_terms = left_ref[...]
    right_0, right_1 = right_ref[:width], right_ref[width:]
    for q in range(count):
        query = jnp.concatenate([own_ref[q], far_ref[q]], axis=0)
        mixed = jnp.dot(left_terms, query, preferred_element_type=F32)
        mixed = mixed[:rows] + (mixed[rows : 2 * rows] + mixed[2 * rows :])
        mixed_0, mixed_1 = parts_of(mixed, 2)
        both = jnp.dot(jnp.concatenate([mixed_0, mixed_1], axis=0), right_0, preferred_element_type=F32)
        cross = jnp.dot(mixed_0, right_1, preferred_element_type=F32)
        wide_ref[:, q, :] = both[:rows] + (both[rows:] + cross)
    out_ref[...] = wide_ref[...].astype(BF16)


def condition(own, far, left_terms, right_terms):
    count, rows, width = own.shape
    return pl.pallas_call(
        condition_kernel,
        out_shape=jax.ShapeDtypeStruct((rows, count, width), BF16),
        in_specs=[VMEM] * 4,
        out_specs=VMEM,
        scratch_shapes=[pltpu.VMEM((rows, count, width), F32)],
        compiler_params=pltpu.CompilerParams(vmem_limit_bytes=24 << 20),
        cost_estimate=pl.CostEstimate(flops=count * 3_000_000 * 40, bytes_accessed=8 * count * rows * width, transcendentals=0),
    )(own, far, left_terms, right_terms)


def regroup_kernel(grads_ref, out_ref, held_ref, sems):
    examples, rows, width = held_ref.shape
    blocks = examples // EXAMPLES
    copies = []
    for b in range(blocks):
        part = pl.ds(b * EXAMPLES, EXAMPLES)
        copies.append(pltpu.make_async_copy(grads_ref.at[part], held_ref.at[part], sems.at[b]))
        copies[-1].start()
    i = lax.broadcasted_iota(jnp.int32, (TILE * TILE, TILE * TILE), 0)
    j = lax.broadcasted_iota(jnp.int32, (TILE * TILE, TILE * TILE), 1)
    swap = jnp.where((i // TILE == j % TILE) & (i % TILE == j // TILE), 1.0, 0.0).astype(BF16)
    for b in range(blocks):
        copies[b].wait()

        @pl.loop(b * EXAMPLES // TILE, (b + 1) * EXAMPLES // TILE)
        def _(step):
            n = pl.ds(pl.multiple_of(step * TILE, TILE), TILE)
            for r in range(0, rows, TILE):
                tile = held_ref[n, r : r + TILE, :].reshape(TILE * TILE, width)
                turned = jnp.dot(swap, tile, preferred_element_type=F32).astype(BF16)
                out_ref[r : r + TILE, n, :] = turned.reshape(TILE, TILE, width)


def regroup(grads):
    n, rows, width = grads.shape
    return pl.pallas_call(
        regroup_kernel,
        out_shape=jax.ShapeDtypeStruct((rows, n, width), BF16),
        in_specs=[pl.BlockSpec(memory_space=pltpu.HBM)],
        out_specs=VMEM,
        scratch_shapes=[pltpu.VMEM((n, rows, width), BF16), pltpu.SemaphoreType.DMA((n // EXAMPLES,))],
        compiler_params=pltpu.CompilerParams(vmem_limit_bytes=48 << 20),
        cost_estimate=pl.CostEstimate(flops=6_000_000_000, bytes_accessed=16_000_000, transcendentals=0),
    )(grads)


def inner_products(query_refs, grad_ref, first=0, rows=None):
    total = sum(ref.shape[1] for ref in query_refs)

    rows = rows or query_refs[0].shape[0]
    deep = next(d for d in range(DEEP, 0, -1) if rows % d == 0)

    def body(i, acc):
        at = [i * deep + j for j in range(deep)]
        queries = [jnp.concatenate([ref[r] for ref in query_refs], axis=0) for r in at]
        return acc + lax.dot_general(
            jnp.concatenate(queries, axis=1),
            jnp.concatenate([grad_ref[first + r] for r in at], axis=1),
            (((1,), (1,)), ((), ())),
            preferred_element_type=F32,
        )

    start = jnp.zeros((total, grad_ref.shape[1]), F32)
    return lax.fori_loop(0, rows // deep, body, start)


def first_pass_kernel(ex, early_0, early_1, own_ref, near, mid, far_in, grad_ref, order_ref, out_ref):
    late = own_ref.shape[1]
    acc = inner_products((early_0, early_1, own_ref, near, mid, far_in), grad_ref)
    me = lax.axis_index("ex")
    sources = slot_sources(me)
    early = [acc[EARLY * s : EARLY * (s + 1)] for s in range(ex)]
    base = EARLY * ex
    slots = [acc[base + late * s : base + late * (s + 1)] for s in range(4)]
    for b in range(ex):
        block = order_ref[b]
        low = jnp.zeros_like(early[0])
        high = jnp.zeros_like(slots[0])
        for s in range(ex):
            hit = sources[s] == block
            low = low + jnp.where(hit, early[s], 0.0)
            high = high + jnp.where(hit, slots[s], 0.0)
        at = b * (EARLY + late)
        out_ref[at : at + EARLY, :] = low
        out_ref[at + EARLY : at + EARLY + late, :] = high


def slot_sources(me):
    low_pair = me < 2
    near = jnp.where(low_pair, 1 - me, 5 - me)
    return [me, near, jnp.where(low_pair, 2, 1), jnp.where(low_pair, 3, 0)]


def shared_kernel(own_ref, mid_ref, far_ref, mine_ref, other_ref, out_ref):
    queries = (own_ref, mid_ref, far_ref)
    mine = inner_products(queries, mine_ref, 0, mine_ref.shape[0])
    other = inner_products(queries, other_ref, 0, mine_ref.shape[0])
    lower = lax.axis_index("pb") == 0
    out_ref[...] = jnp.concatenate([jnp.where(lower, mine, other), jnp.where(lower, other, mine)], axis=1)


def shared_products(own, mid, far, mine, other):
    return pl.pallas_call(
        shared_kernel,
        out_shape=jax.ShapeDtypeStruct((3 * own.shape[1], 2 * mine.shape[1]), F32),
        in_specs=[VMEM] * 5,
        out_specs=VMEM,
        compiler_params=pltpu.CompilerParams(vmem_limit_bytes=24 << 20),
        cost_estimate=pl.CostEstimate(flops=1000, bytes_accessed=1000, transcendentals=0),
    )(own, mid, far, mine, other)


def far_pass_kernel(ex, far_out, grad_ref, order_ref, out_ref):
    out_ref[...] = inner_products((far_out,), grad_ref, SHARED)


def last_pass_kernel(ex, base_ref, far_ref, shared_ref, far_out, grad_ref, order_ref, mine_ref, send_ref, full_ref):
    late = far_out.shape[1]
    acc = far_ref[...] + inner_products((far_out,), grad_ref, SHARED + far_out.shape[0])
    slots = [shared_ref[:late], shared_ref[late : 2 * late], shared_ref[2 * late :] + acc]
    sources = slot_sources(lax.axis_index("ex"))[1:]
    full_ref[...] = base_ref[...]
    for b in range(ex):
        at = b * (EARLY + late) + EARLY
        high = full_ref[at : at + late, :]
        for source, slot in zip(sources, slots):
            high = high + jnp.where(order_ref[b] == source, slot, 0.0)
        full_ref[at : at + late, :] = high
    half = mine_ref.shape[0]
    side = lax.axis_index("feat")
    mine_ref[...] = full_ref[pl.ds(pl.multiple_of(side * half, half), half), :]
    send_ref[...] = full_ref[pl.ds(pl.multiple_of((1 - side) * half, half), half), :]


def score_call(kernel, ex, arrays, order, out_shape, scratch=()):
    return pl.pallas_call(
        functools.partial(kernel, ex),
        out_shape=out_shape,
        in_specs=[VMEM] * len(arrays) + [SMEM],
        out_specs=jax.tree.map(lambda _: VMEM, out_shape),
        scratch_shapes=scratch,
        compiler_params=pltpu.CompilerParams(vmem_limit_bytes=40 << 20),
        cost_estimate=pl.CostEstimate(flops=1000, bytes_accessed=1000, transcendentals=0),
    )(*arrays, order)


def after(x, *others):
    return lax.optimization_barrier((x, *others))[0]


PAIRS = [(0, 1), (1, 0), (2, 3), (3, 2)]
MIDDLE = [(1, 2), (2, 1)]
OUTWARD = [(1, 0), (2, 3)]
INWARD = [(0, 1), (3, 2)]


def per_device_line(train_grads, queries, left_factor, right_factor, block_order):
    ex = lax.axis_size("ex")
    swap = [(0, 1), (1, 0)]
    count = queries.shape[1]
    n = train_grads.shape[0]
    late_raw = queries[0, EARLY:]
    late_other = lax.ppermute(late_raw, "feat", swap)
    raw = after(queries, late_raw)[0, :EARLY]
    terms = factor_terms(left_factor, after(right_factor, raw), train_grads.shape[1])
    raw_near = lax.ppermute(raw, "ex", PAIRS)
    raw_mid = lax.ppermute(raw, "ex", MIDDLE)
    raw_mid_out = lax.ppermute(after(raw_mid, *terms), "ex", OUTWARD)
    early_0 = jnp.concatenate([raw, after(raw_near, raw_mid)], axis=0)
    raw_far_mid = lax.ppermute(after(raw_near, early_0), "ex", MIDDLE)

    late = condition(after(late_raw, raw_near, raw_mid), late_other, *terms)
    near_in = lax.ppermute(late, "ex", INWARD)
    near_out = lax.ppermute(late[SHARED:], "ex", OUTWARD)
    mid_in = lax.ppermute(late, "ex", MIDDLE)
    grads = regroup(after(train_grads, late, raw_mid_out, raw_far_mid))
    early_0_other = lax.ppermute(after(early_0, late), "feat", swap)
    raw_far_out = lax.ppermute(after(raw_far_mid, grads), "ex", OUTWARD)
    far_mid = lax.ppermute(after(near_in, near_out, grads), "ex", MIDDLE)
    mid_out = lax.ppermute(after(mid_in, grads)[SHARED:], "ex", OUTWARD)
    lot = n // lax.axis_size("pb")
    share = lax.dynamic_slice_in_dim(grads[:SHARED], lax.axis_index("pb") * lot, lot, axis=1)
    cond_0 = condition(after(early_0, near_in, mid_in, near_out), early_0_other, *terms)
    share_mine = lax.ppermute(after(share, near_in, near_out, mid_in), "ex", INWARD)
    share_other = lax.ppermute(after(share_mine, mid_out), "pb", swap)
    early_1 = jnp.concatenate([raw_mid + raw_mid_out, after(raw_far_mid, near_in, mid_in) + raw_far_out], axis=0)
    early_1_other = lax.ppermute(after(early_1, cond_0), "feat", swap)
    part = (far_mid.shape[0] - SHARED) // 2
    far_out_0 = lax.ppermute(far_mid[SHARED : SHARED + part], "ex", OUTWARD)
    far_out_1 = lax.ppermute(far_mid[SHARED + part :], "ex", OUTWARD)
    near = jnp.concatenate([near_in[:SHARED], near_in[SHARED:] + near_out], axis=0)
    mid = jnp.concatenate([mid_in[:SHARED], mid_in[SHARED:] + mid_out], axis=0)
    shared = lax.ppermute(shared_products(late, mid_in, far_mid, share_mine, share_other), "ex", OUTWARD)
    cond_1 = condition(after(early_1, far_mid), early_1_other, *terms)

    base = score_call(
        first_pass_kernel, ex, (cond_0, cond_1, late, near, mid, far_mid, grads), block_order,
        jax.ShapeDtypeStruct((ex * count, n), F32),
    )
    far_0 = score_call(
        far_pass_kernel, ex, (far_out_0, after(grads, base)), block_order,
        jax.ShapeDtypeStruct((count - EARLY, n), F32),
    )
    half = jax.ShapeDtypeStruct((ex * count // 2, n), F32)
    mine, send = score_call(
        last_pass_kernel, ex, (base, far_0, shared, far_out_1, grads), block_order, (half, half),
        [pltpu.VMEM((ex * count, n), F32)],
    )
    scores = mine + lax.ppermute(send, "feat", swap)
    return scores.T[:, None, :]


def per_device_gather(train_grads, queries, left_factor, right_factor, block_order):
    row_count = train_grads.shape[0]
    part_rows = train_grads.shape[1]
    right_width = train_grads.shape[2]
    flat_grads = train_grads.reshape(row_count, part_rows * right_width)
    local_queries = queries[0]
    block_size = local_queries.shape[0]
    regrouped = lax.all_to_all(local_queries, "feat", split_axis=0, concat_axis=1, tiled=True)
    whole_mix = jnp.einsum(
        "ik,qkj->qij", left_factor, regrouped.astype(F32), precision=lax.Precision.HIGHEST
    )
    whole_cond = jnp.einsum(
        "qij,jl->qil", whole_mix, right_factor, precision=lax.Precision.HIGHEST
    ).astype(BF16)
    conditioned = lax.all_to_all(whole_cond, "feat", split_axis=1, concat_axis=0, tiled=True)
    conditioned = conditioned.reshape(block_size, part_rows * right_width)
    partials = lax.dot_general(
        flat_grads,
        lax.all_gather(conditioned, "ex", axis=0, tiled=True),
        (((1,), (1,)), ((), ())),
        preferred_element_type=F32,
    )
    block_count = lax.axis_size("ex")
    partials = jnp.take(partials.reshape(row_count, block_count, block_size), block_order, axis=1)
    partials = partials.reshape(row_count, block_count * block_size)
    owned_scores = lax.psum_scatter(partials, "feat", scatter_dimension=1, tiled=True)
    return owned_scores.reshape(row_count, 1, owned_scores.shape[1])


def solution(mesh):
    short_line = mesh.shape["ex"] == 4 and mesh.shape["feat"] == 2
    return jax.shard_map(
        per_device_line if short_line else per_device_gather,
        mesh=mesh,
        in_specs=(
            P(("grp", "ex"), "feat", None),
            P("pb", ("grp", "ex"), "feat", None),
            P("grp", None),
            P("grp", None),
            P("grp"),
        ),
        out_specs=P(("grp", "ex"), "pb", "feat"),
        check_vma=False,
    )
```

```python
import functools

import jax
import jax.numpy as jnp
from jax import lax
from jax.experimental import pallas as pl
from jax.experimental.pallas import tpu as pltpu
from jax.sharding import PartitionSpec as P

F32 = jnp.float32
BF16 = jnp.bfloat16
EARLY = 4
TILE = 16
EXAMPLES = 32
DEEP = 32
VMEM = pl.BlockSpec(memory_space=pltpu.VMEM)
SMEM = pl.BlockSpec(memory_space=pltpu.SMEM)


def parts_of(x, count):
    terms = []
    for _ in range(count):
        top = x.astype(BF16)
        terms.append(top)
        x = x - top.astype(F32)
    return terms


def factor_kernel(left_ref, right_ref, left_out, right_out):
    rows = left_out.shape[0] // 3
    side = lax.axis_index("feat")
    here = pl.ds(pl.multiple_of(side * rows, rows), rows)
    there = pl.ds(pl.multiple_of((1 - side) * rows, rows), rows)
    left = jnp.concatenate([left_ref[here, here], left_ref[here, there]], axis=1)
    left_out[...] = jnp.concatenate(parts_of(left, 3), axis=0)
    right_out[...] = jnp.concatenate(parts_of(right_ref[...], 2), axis=0)


def factor_terms(left, right, rows):
    wide, width = left.shape[1], right.shape[1]
    return pl.pallas_call(
        factor_kernel,
        out_shape=(
            jax.ShapeDtypeStruct((3 * rows, wide), BF16),
            jax.ShapeDtypeStruct((2 * width, width), BF16),
        ),
        in_specs=[VMEM] * 2,
        out_specs=(VMEM, VMEM),
        compiler_params=pltpu.CompilerParams(vmem_limit_bytes=16 << 20),
    )(left, right)


def condition_kernel(own_ref, far_ref, left_ref, right_ref, out_ref, wide_ref):
    count, rows, width = own_ref.shape
    left_terms = left_ref[...]
    right_0, right_1 = right_ref[:width], right_ref[width:]
    for q in range(count):
        query = jnp.concatenate([own_ref[q], far_ref[q]], axis=0)
        mixed = jnp.dot(left_terms, query, preferred_element_type=F32)
        mixed = mixed[:rows] + (mixed[rows : 2 * rows] + mixed[2 * rows :])
        mixed_0, mixed_1 = parts_of(mixed, 2)
        both = jnp.dot(jnp.concatenate([mixed_0, mixed_1], axis=0), right_0, preferred_element_type=F32)
        cross = jnp.dot(mixed_0, right_1, preferred_element_type=F32)
        wide_ref[:, q, :] = both[:rows] + (both[rows:] + cross)
    out_ref[...] = wide_ref[...].astype(BF16)


def condition(own, far, left_terms, right_terms):
    count, rows, width = own.shape
    return pl.pallas_call(
        condition_kernel,
        out_shape=jax.ShapeDtypeStruct((rows, count, width), BF16),
        in_specs=[VMEM] * 4,
        out_specs=VMEM,
        scratch_shapes=[pltpu.VMEM((rows, count, width), F32)],
        compiler_params=pltpu.CompilerParams(vmem_limit_bytes=24 << 20),
        cost_estimate=pl.CostEstimate(flops=count * 3_000_000 * 40, bytes_accessed=8 * count * rows * width, transcendentals=0),
    )(own, far, left_terms, right_terms)


def regroup_kernel(grads_ref, out_ref, held_ref, sems):
    examples, rows, width = held_ref.shape
    blocks = examples // EXAMPLES
    copies = []
    for b in range(blocks):
        part = pl.ds(b * EXAMPLES, EXAMPLES)
        copies.append(pltpu.make_async_copy(grads_ref.at[part], held_ref.at[part], sems.at[b]))
        copies[-1].start()
    i = lax.broadcasted_iota(jnp.int32, (TILE * TILE, TILE * TILE), 0)
    j = lax.broadcasted_iota(jnp.int32, (TILE * TILE, TILE * TILE), 1)
    swap = jnp.where((i // TILE == j % TILE) & (i % TILE == j // TILE), 1.0, 0.0).astype(BF16)
    for b in range(blocks):
        copies[b].wait()

        @pl.loop(b * EXAMPLES // TILE, (b + 1) * EXAMPLES // TILE)
        def _(step):
            n = pl.ds(pl.multiple_of(step * TILE, TILE), TILE)
            for r in range(0, rows, TILE):
                tile = held_ref[n, r : r + TILE, :].reshape(TILE * TILE, width)
                turned = jnp.dot(swap, tile, preferred_element_type=F32).astype(BF16)
                out_ref[r : r + TILE, n, :] = turned.reshape(TILE, TILE, width)


def regroup(grads):
    n, rows, width = grads.shape
    return pl.pallas_call(
        regroup_kernel,
        out_shape=jax.ShapeDtypeStruct((rows, n, width), BF16),
        in_specs=[pl.BlockSpec(memory_space=pltpu.HBM)],
        out_specs=VMEM,
        scratch_shapes=[pltpu.VMEM((n, rows, width), BF16), pltpu.SemaphoreType.DMA((n // EXAMPLES,))],
        compiler_params=pltpu.CompilerParams(vmem_limit_bytes=44 << 20),
        cost_estimate=pl.CostEstimate(flops=1000, bytes_accessed=1000, transcendentals=0),
    )(grads)


def inner_products(query_refs, grad_ref, first=0):
    total = sum(ref.shape[1] for ref in query_refs)

    def body(i, acc):
        at = [i * DEEP + j for j in range(DEEP)]
        queries = [jnp.concatenate([ref[r] for ref in query_refs], axis=0) for r in at]
        return acc + lax.dot_general(
            jnp.concatenate(queries, axis=1),
            jnp.concatenate([grad_ref[first + r] for r in at], axis=1),
            (((1,), (1,)), ((), ())),
            preferred_element_type=F32,
        )

    start = jnp.zeros((total, grad_ref.shape[1]), F32)
    return lax.fori_loop(0, query_refs[0].shape[0] // DEEP, body, start)


def first_pass_kernel(ex, early_0, early_1, own_ref, near, mid, far_in, grad_ref, order_ref, out_ref):
    late = own_ref.shape[1]
    acc = inner_products((early_0, early_1, own_ref, near, mid, far_in), grad_ref)
    me = lax.axis_index("ex")
    sources = slot_sources(me)
    early = [acc[EARLY * s : EARLY * (s + 1)] for s in range(ex)]
    base = EARLY * ex
    slots = [acc[base + late * s : base + late * (s + 1)] for s in range(4)]
    for b in range(ex):
        block = order_ref[b]
        low = jnp.zeros_like(early[0])
        high = jnp.zeros_like(slots[0])
        for s in range(ex):
            hit = sources[s] == block
            low = low + jnp.where(hit, early[s], 0.0)
            high = high + jnp.where(hit, slots[s], 0.0)
        at = b * (EARLY + late)
        out_ref[at : at + EARLY, :] = low
        out_ref[at + EARLY : at + EARLY + late, :] = high


def slot_sources(me):
    low_pair = me < 2
    near = jnp.where(low_pair, 1 - me, 5 - me)
    return [me, near, jnp.where(low_pair, 2, 1), jnp.where(low_pair, 3, 0)]


def far_pass_kernel(ex, far_out, grad_ref, order_ref, out_ref):
    out_ref[...] = inner_products((far_out,), grad_ref)


def last_pass_kernel(ex, base_ref, far_ref, far_out, grad_ref, order_ref, mine_ref, send_ref, full_ref):
    late = far_out.shape[1]
    acc = far_ref[...] + inner_products((far_out,), grad_ref, far_out.shape[0])
    far = slot_sources(lax.axis_index("ex"))[3]
    full_ref[...] = base_ref[...]
    for b in range(ex):
        at = b * (EARLY + late) + EARLY
        full_ref[at : at + late, :] = full_ref[at : at + late, :] + jnp.where(order_ref[b] == far, acc, 0.0)
    half = mine_ref.shape[0]
    side = lax.axis_index("feat")
    mine_ref[...] = full_ref[pl.ds(pl.multiple_of(side * half, half), half), :]
    send_ref[...] = full_ref[pl.ds(pl.multiple_of((1 - side) * half, half), half), :]


def score_call(kernel, ex, arrays, order, out_shape, scratch=()):
    return pl.pallas_call(
        functools.partial(kernel, ex),
        out_shape=out_shape,
        in_specs=[VMEM] * len(arrays) + [SMEM],
        out_specs=jax.tree.map(lambda _: VMEM, out_shape),
        scratch_shapes=scratch,
        compiler_params=pltpu.CompilerParams(vmem_limit_bytes=40 << 20),
        cost_estimate=pl.CostEstimate(flops=1000, bytes_accessed=1000, transcendentals=0),
    )(*arrays, order)


def after(x, *others):
    return lax.optimization_barrier((x, *others))[0]


PAIRS = [(0, 1), (1, 0), (2, 3), (3, 2)]
MIDDLE = [(1, 2), (2, 1)]
OUTWARD = [(1, 0), (2, 3)]


def per_device_line(train_grads, queries, left_factor, right_factor, block_order):
    ex = lax.axis_size("ex")
    swap = [(0, 1), (1, 0)]
    count = queries.shape[1]
    n = train_grads.shape[0]
    late_raw = queries[0, EARLY:]
    late_other = lax.ppermute(late_raw, "feat", swap)
    raw = after(queries, late_raw)[0, :EARLY]
    terms = factor_terms(left_factor, after(right_factor, raw), train_grads.shape[1])
    raw_near = lax.ppermute(raw, "ex", PAIRS)
    raw_mid = lax.ppermute(raw, "ex", MIDDLE)
    grads = regroup(after(train_grads, *terms))
    raw_mid_out = lax.ppermute(after(raw_mid, grads), "ex", OUTWARD)
    early_0 = jnp.concatenate([raw, after(raw_near, raw_mid, grads)], axis=0)
    raw_far_mid = lax.ppermute(after(raw_near, early_0), "ex", MIDDLE)

    late = condition(after(late_raw, raw_near, raw_mid, grads), late_other, *terms)
    near = lax.ppermute(late, "ex", PAIRS)
    mid = lax.ppermute(late, "ex", MIDDLE)
    early_0_other = lax.ppermute(after(early_0, late, raw_far_mid, raw_mid_out), "feat", swap)
    raw_far_out = lax.ppermute(after(raw_far_mid, near), "ex", OUTWARD)
    far_mid = lax.ppermute(near, "ex", MIDDLE)
    mid_out = lax.ppermute(mid, "ex", OUTWARD)
    cond_0 = condition(after(early_0, near, mid), early_0_other, *terms)
    early_1 = jnp.concatenate([raw_mid + raw_mid_out, after(raw_far_mid, near, mid) + raw_far_out], axis=0)
    early_1_other = lax.ppermute(after(early_1, cond_0), "feat", swap)
    part = far_mid.shape[0] // 2
    far_out_0 = lax.ppermute(far_mid[:part], "ex", OUTWARD)
    far_out_1 = lax.ppermute(far_mid[part:], "ex", OUTWARD)
    cond_1 = condition(after(early_1, far_mid), early_1_other, *terms)

    base = score_call(
        first_pass_kernel, ex, (cond_0, cond_1, late, near, mid + mid_out, far_mid, grads), block_order,
        jax.ShapeDtypeStruct((ex * count, n), F32),
    )
    far_0 = score_call(
        far_pass_kernel, ex, (far_out_0, after(grads, base)), block_order,
        jax.ShapeDtypeStruct((count - EARLY, n), F32),
    )
    half = jax.ShapeDtypeStruct((ex * count // 2, n), F32)
    mine, send = score_call(
        last_pass_kernel, ex, (base, far_0, far_out_1, grads), block_order, (half, half),
        [pltpu.VMEM((ex * count, n), F32)],
    )
    scores = mine + lax.ppermute(send, "feat", swap)
    return scores.T[:, None, :]


def per_device_gather(train_grads, queries, left_factor, right_factor, block_order):
    row_count = train_grads.shape[0]
    part_rows = train_grads.shape[1]
    right_width = train_grads.shape[2]
    flat_grads = train_grads.reshape(row_count, part_rows * right_width)
    local_queries = queries[0]
    block_size = local_queries.shape[0]
    regrouped = lax.all_to_all(local_queries, "feat", split_axis=0, concat_axis=1, tiled=True)
    whole_mix = jnp.einsum(
        "ik,qkj->qij", left_factor, regrouped.astype(F32), precision=lax.Precision.HIGHEST
    )
    whole_cond = jnp.einsum(
        "qij,jl->qil", whole_mix, right_factor, precision=lax.Precision.HIGHEST
    ).astype(BF16)
    conditioned = lax.all_to_all(whole_cond, "feat", split_axis=1, concat_axis=0, tiled=True)
    conditioned = conditioned.reshape(block_size, part_rows * right_width)
    partials = lax.dot_general(
        flat_grads,
        lax.all_gather(conditioned, "ex", axis=0, tiled=True),
        (((1,), (1,)), ((), ())),
        preferred_element_type=F32,
    )
    block_count = lax.axis_size("ex")
    partials = jnp.take(partials.reshape(row_count, block_count, block_size), block_order, axis=1)
    partials = partials.reshape(row_count, block_count * block_size)
    owned_scores = lax.psum_scatter(partials, "feat", scatter_dimension=1, tiled=True)
    return owned_scores.reshape(row_count, 1, owned_scores.shape[1])


def solution(mesh):
    short_line = mesh.shape["ex"] == 4 and mesh.shape["feat"] == 2
    return jax.shard_map(
        per_device_line if short_line else per_device_gather,
        mesh=mesh,
        in_specs=(
            P(("grp", "ex"), "feat", None),
            P("pb", ("grp", "ex"), "feat", None),
            P("grp", None),
            P("grp", None),
            P("grp"),
        ),
        out_specs=P(("grp", "ex"), "pb", "feat"),
        check_vma=False,
    )
```

```python
import functools

import jax
import jax.numpy as jnp
from jax import lax
from jax.experimental import pallas as pl
from jax.experimental.pallas import tpu as pltpu
from jax.sharding import PartitionSpec as P

F32 = jnp.float32
BF16 = jnp.bfloat16
EARLY = 4
TILE = 16
EXAMPLES = 32
DEEP = 32
VMEM = pl.BlockSpec(memory_space=pltpu.VMEM)
SMEM = pl.BlockSpec(memory_space=pltpu.SMEM)


def parts_of(x, count):
    terms = []
    for _ in range(count):
        top = x.astype(BF16)
        terms.append(top)
        x = x - top.astype(F32)
    return terms


def factor_kernel(left_ref, right_ref, left_out, right_out):
    rows = left_out.shape[0] // 3
    side = lax.axis_index("feat")
    here = pl.ds(pl.multiple_of(side * rows, rows), rows)
    there = pl.ds(pl.multiple_of((1 - side) * rows, rows), rows)
    left = jnp.concatenate([left_ref[here, here], left_ref[here, there]], axis=1)
    left_out[...] = jnp.concatenate(parts_of(left, 3), axis=0)
    right_out[...] = jnp.concatenate(parts_of(right_ref[...], 2), axis=0)


def factor_terms(left, right, rows):
    wide, width = left.shape[1], right.shape[1]
    return pl.pallas_call(
        factor_kernel,
        out_shape=(
            jax.ShapeDtypeStruct((3 * rows, wide), BF16),
            jax.ShapeDtypeStruct((2 * width, width), BF16),
        ),
        in_specs=[VMEM] * 2,
        out_specs=(VMEM, VMEM),
        compiler_params=pltpu.CompilerParams(vmem_limit_bytes=16 << 20),
    )(left, right)


def condition_kernel(own_ref, far_ref, left_ref, right_ref, out_ref, wide_ref):
    count, rows, width = own_ref.shape
    left_terms = left_ref[...]
    right_0, right_1 = right_ref[:width], right_ref[width:]
    for q in range(count):
        query = jnp.concatenate([own_ref[q], far_ref[q]], axis=0)
        mixed = jnp.dot(left_terms, query, preferred_element_type=F32)
        mixed = mixed[:rows] + (mixed[rows : 2 * rows] + mixed[2 * rows :])
        mixed_0, mixed_1 = parts_of(mixed, 2)
        both = jnp.dot(jnp.concatenate([mixed_0, mixed_1], axis=0), right_0, preferred_element_type=F32)
        cross = jnp.dot(mixed_0, right_1, preferred_element_type=F32)
        wide_ref[:, q, :] = both[:rows] + (both[rows:] + cross)
    for q in range(count, out_ref.shape[1]):
        wide_ref[:, q, :] = jnp.zeros((rows, width), F32)
    out_ref[...] = wide_ref[...].astype(BF16)


def condition(own, far, left_terms, right_terms):
    count, rows, width = own.shape
    padded = -(-count // 8) * 8
    return pl.pallas_call(
        condition_kernel,
        out_shape=jax.ShapeDtypeStruct((rows, padded, width), BF16),
        in_specs=[VMEM] * 4,
        out_specs=VMEM,
        scratch_shapes=[pltpu.VMEM((rows, padded, width), F32)],
        compiler_params=pltpu.CompilerParams(vmem_limit_bytes=24 << 20),
        cost_estimate=pl.CostEstimate(flops=count * 3_000_000 * 40, bytes_accessed=8 * count * rows * width, transcendentals=0),
    )(own, far, left_terms, right_terms)


def regroup_kernel(grads_ref, out_ref, held_ref, sems):
    examples, rows, width = held_ref.shape
    blocks = examples // EXAMPLES
    copies = []
    for b in range(blocks):
        part = pl.ds(b * EXAMPLES, EXAMPLES)
        copies.append(pltpu.make_async_copy(grads_ref.at[part], held_ref.at[part], sems.at[b]))
        copies[-1].start()
    i = lax.broadcasted_iota(jnp.int32, (TILE * TILE, TILE * TILE), 0)
    j = lax.broadcasted_iota(jnp.int32, (TILE * TILE, TILE * TILE), 1)
    swap = jnp.where((i // TILE == j % TILE) & (i % TILE == j // TILE), 1.0, 0.0).astype(BF16)
    for b in range(blocks):
        copies[b].wait()

        @pl.loop(b * EXAMPLES // TILE, (b + 1) * EXAMPLES // TILE)
        def _(step):
            n = pl.ds(pl.multiple_of(step * TILE, TILE), TILE)
            for r in range(0, rows, TILE):
                tile = held_ref[n, r : r + TILE, :].reshape(TILE * TILE, width)
                turned = jnp.dot(swap, tile, preferred_element_type=F32).astype(BF16)
                out_ref[r : r + TILE, n, :] = turned.reshape(TILE, TILE, width)


def regroup(grads):
    n, rows, width = grads.shape
    return pl.pallas_call(
        regroup_kernel,
        out_shape=jax.ShapeDtypeStruct((rows, n, width), BF16),
        in_specs=[pl.BlockSpec(memory_space=pltpu.HBM)],
        out_specs=VMEM,
        scratch_shapes=[pltpu.VMEM((n, rows, width), BF16), pltpu.SemaphoreType.DMA((n // EXAMPLES,))],
        compiler_params=pltpu.CompilerParams(vmem_limit_bytes=44 << 20),
        cost_estimate=pl.CostEstimate(flops=1000, bytes_accessed=1000, transcendentals=0),
    )(grads)


def inner_products(query_refs, grad_ref, first=0, rows=None):
    total = sum(ref.shape[1] for ref in query_refs)
    rows = rows or grad_ref.shape[0]
    starts = [0 if ref.shape[0] == rows else first for ref in query_refs]

    def body(i, acc):
        at = [i * DEEP + j for j in range(DEEP)]
        queries = [
            jnp.concatenate([ref[start + r] for ref, start in zip(query_refs, starts)], axis=0) for r in at
        ]
        return acc + lax.dot_general(
            jnp.concatenate(queries, axis=1),
            jnp.concatenate([grad_ref[first + r] for r in at], axis=1),
            (((1,), (1,)), ((), ())),
            preferred_element_type=F32,
        )

    start = jnp.zeros((total, grad_ref.shape[1]), F32)
    return lax.fori_loop(0, rows // DEEP, body, start)


def first_pass_kernel(ex, early_ref, own_ref, near, mid, far_in, grad_ref, order_ref, out_ref):
    late = own_ref.shape[1]
    acc = inner_products((early_ref, own_ref, near, mid, far_in), grad_ref)
    sources = slot_sources(lax.axis_index("ex"))
    early = [acc[EARLY * s : EARLY * (s + 1)] for s in range(ex - 1)]
    base = early_ref.shape[1]
    slots = [acc[base + late * s : base + late * (s + 1)] for s in range(ex)]
    for b in range(ex):
        block = order_ref[b]
        low = jnp.zeros_like(early[0])
        for source, slot in zip(sources, early):
            low = low + jnp.where(source == block, slot, 0.0)
        high = jnp.zeros_like(slots[0])
        for source, slot in zip(sources, slots):
            high = high + jnp.where(source == block, slot, 0.0)
        at = b * (EARLY + late)
        out_ref[at : at + EARLY, :] = low
        out_ref[at + EARLY : at + EARLY + late, :] = high


def slot_sources(me):
    low_pair = me < 2
    near = jnp.where(low_pair, 1 - me, 5 - me)
    return [me, near, jnp.where(low_pair, 2, 1), jnp.where(low_pair, 3, 0)]


def far_pass_kernel(ex, early_ref, far_out, grad_ref, order_ref, out_ref):
    out_ref[...] = inner_products((early_ref, far_out), grad_ref, 0, far_out.shape[0])


def last_pass_kernel(ex, base_ref, far_ref, early_ref, far_out, grad_ref, order_ref, mine_ref, send_ref, full_ref):
    late = far_out.shape[1]
    acc = far_ref[...] + inner_products((early_ref, far_out), grad_ref, far_out.shape[0], far_out.shape[0])
    far = slot_sources(lax.axis_index("ex"))[3]
    full_ref[...] = base_ref[...]
    for b in range(ex):
        hit = order_ref[b] == far
        at = b * (EARLY + late)
        full_ref[at : at + EARLY, :] = full_ref[at : at + EARLY, :] + jnp.where(hit, acc[:EARLY], 0.0)
        at = at + EARLY
        full_ref[at : at + late, :] = full_ref[at : at + late, :] + jnp.where(hit, acc[early_ref.shape[1] :], 0.0)
    half = mine_ref.shape[0]
    side = lax.axis_index("feat")
    mine_ref[...] = full_ref[pl.ds(pl.multiple_of(side * half, half), half), :]
    send_ref[...] = full_ref[pl.ds(pl.multiple_of((1 - side) * half, half), half), :]


def score_call(kernel, ex, arrays, order, out_shape, scratch=()):
    return pl.pallas_call(
        functools.partial(kernel, ex),
        out_shape=out_shape,
        in_specs=[VMEM] * len(arrays) + [SMEM],
        out_specs=jax.tree.map(lambda _: VMEM, out_shape),
        scratch_shapes=scratch,
        compiler_params=pltpu.CompilerParams(vmem_limit_bytes=40 << 20),
        cost_estimate=pl.CostEstimate(flops=1000, bytes_accessed=1000, transcendentals=0),
    )(*arrays, order)


def after(x, *others):
    return lax.optimization_barrier((x, *others))[0]


PAIRS = [(0, 1), (1, 0), (2, 3), (3, 2)]
MIDDLE = [(1, 2), (2, 1)]
OUTWARD = [(1, 0), (2, 3)]


def per_device_line(train_grads, queries, left_factor, right_factor, block_order):
    ex = lax.axis_size("ex")
    swap = [(0, 1), (1, 0)]
    count = queries.shape[1]
    n = train_grads.shape[0]
    late_raw = queries[0, EARLY:]
    late_other = lax.ppermute(late_raw, "feat", swap)
    raw = after(queries, late_raw)[0, :EARLY]
    terms = factor_terms(left_factor, after(right_factor, raw), train_grads.shape[1])
    raw_near = lax.ppermute(raw, "ex", PAIRS)
    raw_mid = lax.ppermute(raw, "ex", MIDDLE)
    grads = regroup(after(train_grads, *terms))
    raw_mid_out = lax.ppermute(after(raw_mid, grads), "ex", OUTWARD)
    raw_far_mid = lax.ppermute(after(raw_near, late_other), "ex", MIDDLE)

    late = condition(after(late_raw, raw_near, raw_mid, grads), late_other, *terms)
    mid = lax.ppermute(late, "ex", MIDDLE)
    near = lax.ppermute(late, "ex", PAIRS)
    early_0 = jnp.concatenate([raw, raw_near, raw_mid + raw_mid_out], axis=0)
    early_0_other = lax.ppermute(after(early_0, late, raw_far_mid), "feat", swap)
    raw_far_out = lax.ppermute(after(raw_far_mid, mid), "ex", OUTWARD)
    mid_out = lax.ppermute(mid, "ex", OUTWARD)
    far_mid = lax.ppermute(near, "ex", MIDDLE)
    early_1 = raw_far_mid + raw_far_out
    cond_0 = condition(after(early_0, near, mid), early_0_other, *terms)
    early_1_other = lax.ppermute(after(early_1, cond_0), "feat", swap)
    part = far_mid.shape[0] // 2
    far_out_0 = lax.ppermute(far_mid[:part], "ex", OUTWARD)
    far_out_1 = lax.ppermute(far_mid[part:], "ex", OUTWARD)
    cond_1 = condition(after(early_1, far_mid), early_1_other, *terms)

    base = score_call(
        first_pass_kernel, ex, (cond_0, late, near, mid + mid_out, far_mid, grads), block_order,
        jax.ShapeDtypeStruct((ex * count, n), F32),
    )
    far_0 = score_call(
        far_pass_kernel, ex, (cond_1, far_out_0, after(grads, base)), block_order,
        jax.ShapeDtypeStruct((cond_1.shape[1] + count - EARLY, n), F32),
    )
    half = jax.ShapeDtypeStruct((ex * count // 2, n), F32)
    mine, send = score_call(
        last_pass_kernel, ex, (base, far_0, cond_1, far_out_1, grads), block_order, (half, half),
        [pltpu.VMEM((ex * count, n), F32)],
    )
    scores = mine + lax.ppermute(send, "feat", swap)
    return scores.T[:, None, :]


def per_device_gather(train_grads, queries, left_factor, right_factor, block_order):
    row_count = train_grads.shape[0]
    part_rows = train_grads.shape[1]
    right_width = train_grads.shape[2]
    flat_grads = train_grads.reshape(row_count, part_rows * right_width)
    local_queries = queries[0]
    block_size = local_queries.shape[0]
    regrouped = lax.all_to_all(local_queries, "feat", split_axis=0, concat_axis=1, tiled=True)
    whole_mix = jnp.einsum(
        "ik,qkj->qij", left_factor, regrouped.astype(F32), precision=lax.Precision.HIGHEST
    )
    whole_cond = jnp.einsum(
        "qij,jl->qil", whole_mix, right_factor, precision=lax.Precision.HIGHEST
    ).astype(BF16)
    conditioned = lax.all_to_all(whole_cond, "feat", split_axis=1, concat_axis=0, tiled=True)
    conditioned = conditioned.reshape(block_size, part_rows * right_width)
    partials = lax.dot_general(
        flat_grads,
        lax.all_gather(conditioned, "ex", axis=0, tiled=True),
        (((1,), (1,)), ((), ())),
        preferred_element_type=F32,
    )
    block_count = lax.axis_size("ex")
    partials = jnp.take(partials.reshape(row_count, block_count, block_size), block_order, axis=1)
    partials = partials.reshape(row_count, block_count * block_size)
    owned_scores = lax.psum_scatter(partials, "feat", scatter_dimension=1, tiled=True)
    return owned_scores.reshape(row_count, 1, owned_scores.shape[1])


def solution(mesh):
    short_line = mesh.shape["ex"] == 4 and mesh.shape["feat"] == 2
    return jax.shard_map(
        per_device_line if short_line else per_device_gather,
        mesh=mesh,
        in_specs=(
            P(("grp", "ex"), "feat", None),
            P("pb", ("grp", "ex"), "feat", None),
            P("grp", None),
            P("grp", None),
            P("grp"),
        ),
        out_specs=P(("grp", "ex"), "pb", "feat"),
        check_vma=False,
    )
```

```python
import functools

import jax
import jax.numpy as jnp
from jax import lax
from jax.experimental import pallas as pl
from jax.experimental.pallas import tpu as pltpu
from jax.sharding import PartitionSpec as P

F32 = jnp.float32
BF16 = jnp.bfloat16
EARLY = 4
TILE = 16
EXAMPLES = 32
DEEP = 32
VMEM = pl.BlockSpec(memory_space=pltpu.VMEM)
SMEM = pl.BlockSpec(memory_space=pltpu.SMEM)


def parts_of(x, count):
    terms = []
    for _ in range(count):
        top = x.astype(BF16)
        terms.append(top)
        x = x - top.astype(F32)
    return terms


def factor_kernel(left_ref, right_ref, left_out, right_out):
    rows = left_out.shape[0] // 3
    side = lax.axis_index("feat")
    here = pl.ds(pl.multiple_of(side * rows, rows), rows)
    there = pl.ds(pl.multiple_of((1 - side) * rows, rows), rows)
    left = jnp.concatenate([left_ref[here, here], left_ref[here, there]], axis=1)
    left_out[...] = jnp.concatenate(parts_of(left, 3), axis=0)
    right_out[...] = jnp.concatenate(parts_of(right_ref[...], 2), axis=0)


def factor_terms(left, right, rows):
    wide, width = left.shape[1], right.shape[1]
    return pl.pallas_call(
        factor_kernel,
        out_shape=(
            jax.ShapeDtypeStruct((3 * rows, wide), BF16),
            jax.ShapeDtypeStruct((2 * width, width), BF16),
        ),
        in_specs=[VMEM] * 2,
        out_specs=(VMEM, VMEM),
        compiler_params=pltpu.CompilerParams(vmem_limit_bytes=16 << 20),
    )(left, right)


def condition_kernel(own_ref, far_ref, left_ref, right_ref, out_ref, wide_ref):
    count, rows, width = own_ref.shape
    left_terms = left_ref[...]
    right_0, right_1 = right_ref[:width], right_ref[width:]
    for q in range(count):
        query = jnp.concatenate([own_ref[q], far_ref[q]], axis=0)
        mixed = jnp.dot(left_terms, query, preferred_element_type=F32)
        mixed = mixed[:rows] + (mixed[rows : 2 * rows] + mixed[2 * rows :])
        mixed_0, mixed_1 = parts_of(mixed, 2)
        both = jnp.dot(jnp.concatenate([mixed_0, mixed_1], axis=0), right_0, preferred_element_type=F32)
        cross = jnp.dot(mixed_0, right_1, preferred_element_type=F32)
        wide_ref[:, q, :] = both[:rows] + (both[rows:] + cross)
    out_ref[...] = wide_ref[...].astype(BF16)


def condition(own, far, left_terms, right_terms):
    count, rows, width = own.shape
    return pl.pallas_call(
        condition_kernel,
        out_shape=jax.ShapeDtypeStruct((rows, count, width), BF16),
        in_specs=[VMEM] * 4,
        out_specs=VMEM,
        scratch_shapes=[pltpu.VMEM((rows, count, width), F32)],
        compiler_params=pltpu.CompilerParams(vmem_limit_bytes=24 << 20),
        cost_estimate=pl.CostEstimate(flops=count * 3_000_000 * 40, bytes_accessed=8 * count * rows * width, transcendentals=0),
    )(own, far, left_terms, right_terms)


def regroup_kernel(grads_ref, out_ref, held_ref, sems):
    examples, rows, width = held_ref.shape
    blocks = examples // EXAMPLES
    copies = []
    for b in range(blocks):
        part = pl.ds(b * EXAMPLES, EXAMPLES)
        copies.append(pltpu.make_async_copy(grads_ref.at[part], held_ref.at[part], sems.at[b]))
        copies[-1].start()
    i = lax.broadcasted_iota(jnp.int32, (TILE * TILE, TILE * TILE), 0)
    j = lax.broadcasted_iota(jnp.int32, (TILE * TILE, TILE * TILE), 1)
    swap = jnp.where((i // TILE == j % TILE) & (i % TILE == j // TILE), 1.0, 0.0).astype(BF16)
    for b in range(blocks):
        copies[b].wait()

        @pl.loop(b * EXAMPLES // TILE, (b + 1) * EXAMPLES // TILE)
        def _(step):
            n = pl.ds(pl.multiple_of(step * TILE, TILE), TILE)
            for r in range(0, rows, TILE):
                tile = held_ref[n, r : r + TILE, :].reshape(TILE * TILE, width)
                turned = jnp.dot(swap, tile, preferred_element_type=F32).astype(BF16)
                out_ref[r : r + TILE, n, :] = turned.reshape(TILE, TILE, width)


def regroup(grads):
    n, rows, width = grads.shape
    return pl.pallas_call(
        regroup_kernel,
        out_shape=jax.ShapeDtypeStruct((rows, n, width), BF16),
        in_specs=[pl.BlockSpec(memory_space=pltpu.HBM)],
        out_specs=VMEM,
        scratch_shapes=[pltpu.VMEM((n, rows, width), BF16), pltpu.SemaphoreType.DMA((n // EXAMPLES,))],
        compiler_params=pltpu.CompilerParams(vmem_limit_bytes=44 << 20),
        cost_estimate=pl.CostEstimate(flops=6_000_000_000, bytes_accessed=16_000_000, transcendentals=0),
    )(grads)


def inner_products(query_refs, grad_ref, first=0):
    total = sum(ref.shape[1] for ref in query_refs)

    def body(i, acc):
        at = [i * DEEP + j for j in range(DEEP)]
        queries = [jnp.concatenate([ref[r] for ref in query_refs], axis=0) for r in at]
        return acc + lax.dot_general(
            jnp.concatenate(queries, axis=1),
            jnp.concatenate([grad_ref[first + r] for r in at], axis=1),
            (((1,), (1,)), ((), ())),
            preferred_element_type=F32,
        )

    start = jnp.zeros((total, grad_ref.shape[1]), F32)
    return lax.fori_loop(0, query_refs[0].shape[0] // DEEP, body, start)


def first_pass_kernel(ex, early_0, early_1, own_ref, near, mid, far_in, grad_ref, order_ref, out_ref):
    late = own_ref.shape[1]
    acc = inner_products((early_0, early_1, own_ref, near, mid, far_in), grad_ref)
    me = lax.axis_index("ex")
    sources = slot_sources(me)
    early = [acc[EARLY * s : EARLY * (s + 1)] for s in range(ex)]
    base = EARLY * ex
    slots = [acc[base + late * s : base + late * (s + 1)] for s in range(4)]
    for b in range(ex):
        block = order_ref[b]
        low = jnp.zeros_like(early[0])
        high = jnp.zeros_like(slots[0])
        for s in range(ex):
            hit = sources[s] == block
            low = low + jnp.where(hit, early[s], 0.0)
            high = high + jnp.where(hit, slots[s], 0.0)
        at = b * (EARLY + late)
        out_ref[at : at + EARLY, :] = low
        out_ref[at + EARLY : at + EARLY + late, :] = high


def slot_sources(me):
    low_pair = me < 2
    near = jnp.where(low_pair, 1 - me, 5 - me)
    return [me, near, jnp.where(low_pair, 2, 1), jnp.where(low_pair, 3, 0)]


def far_pass_kernel(ex, far_out, grad_ref, order_ref, out_ref):
    out_ref[...] = inner_products((far_out,), grad_ref)


def last_pass_kernel(ex, base_ref, far_ref, far_out, grad_ref, order_ref, mine_ref, send_ref, full_ref):
    late = far_out.shape[1]
    acc = far_ref[...] + inner_products((far_out,), grad_ref, far_out.shape[0])
    far = slot_sources(lax.axis_index("ex"))[3]
    full_ref[...] = base_ref[...]
    for b in range(ex):
        at = b * (EARLY + late) + EARLY
        full_ref[at : at + late, :] = full_ref[at : at + late, :] + jnp.where(order_ref[b] == far, acc, 0.0)
    half = mine_ref.shape[0]
    side = lax.axis_index("feat")
    mine_ref[...] = full_ref[pl.ds(pl.multiple_of(side * half, half), half), :]
    send_ref[...] = full_ref[pl.ds(pl.multiple_of((1 - side) * half, half), half), :]


def score_call(kernel, ex, arrays, order, out_shape, scratch=()):
    return pl.pallas_call(
        functools.partial(kernel, ex),
        out_shape=out_shape,
        in_specs=[VMEM] * len(arrays) + [SMEM],
        out_specs=jax.tree.map(lambda _: VMEM, out_shape),
        scratch_shapes=scratch,
        compiler_params=pltpu.CompilerParams(vmem_limit_bytes=40 << 20),
        cost_estimate=pl.CostEstimate(flops=1000, bytes_accessed=1000, transcendentals=0),
    )(*arrays, order)


def after(x, *others):
    return lax.optimization_barrier((x, *others))[0]


PAIRS = [(0, 1), (1, 0), (2, 3), (3, 2)]
MIDDLE = [(1, 2), (2, 1)]
OUTWARD = [(1, 0), (2, 3)]


def per_device_line(train_grads, queries, left_factor, right_factor, block_order):
    ex = lax.axis_size("ex")
    swap = [(0, 1), (1, 0)]
    count = queries.shape[1]
    n = train_grads.shape[0]
    late_raw = queries[0, EARLY:]
    late_other = lax.ppermute(late_raw, "feat", swap)
    raw = after(queries, late_raw)[0, :EARLY]
    terms = factor_terms(left_factor, after(right_factor, raw), train_grads.shape[1])
    raw_near = lax.ppermute(raw, "ex", PAIRS)
    raw_mid = lax.ppermute(raw, "ex", MIDDLE)
    raw_mid_out = lax.ppermute(after(raw_mid, *terms), "ex", OUTWARD)
    early_0 = jnp.concatenate([raw, after(raw_near, raw_mid)], axis=0)
    raw_far_mid = lax.ppermute(after(raw_near, early_0), "ex", MIDDLE)

    late = condition(after(late_raw, raw_near, raw_mid), late_other, *terms)
    near = lax.ppermute(late, "ex", PAIRS)
    mid = lax.ppermute(late, "ex", MIDDLE)
    grads = regroup(after(train_grads, late))
    early_0_other = lax.ppermute(after(early_0, late), "feat", swap)
    raw_far_out = lax.ppermute(after(raw_far_mid, grads), "ex", OUTWARD)
    far_mid = lax.ppermute(after(near, grads), "ex", MIDDLE)
    mid_out = lax.ppermute(after(mid, near, grads), "ex", OUTWARD)
    cond_0 = condition(after(early_0, near, mid), early_0_other, *terms)
    early_1 = jnp.concatenate([raw_mid + raw_mid_out, after(raw_far_mid, near, mid) + raw_far_out], axis=0)
    early_1_other = lax.ppermute(after(early_1, cond_0), "feat", swap)
    part = far_mid.shape[0] // 2
    far_out_0 = lax.ppermute(far_mid[:part], "ex", OUTWARD)
    far_out_1 = lax.ppermute(far_mid[part:], "ex", OUTWARD)
    cond_1 = condition(after(early_1, far_mid), early_1_other, *terms)

    base = score_call(
        first_pass_kernel, ex, (cond_0, cond_1, late, near, mid + mid_out, far_mid, grads), block_order,
        jax.ShapeDtypeStruct((ex * count, n), F32),
    )
    far_0 = score_call(
        far_pass_kernel, ex, (far_out_0, after(grads, base)), block_order,
        jax.ShapeDtypeStruct((count - EARLY, n), F32),
    )
    half = jax.ShapeDtypeStruct((ex * count // 2, n), F32)
    mine, send = score_call(
        last_pass_kernel, ex, (base, far_0, far_out_1, grads), block_order, (half, half),
        [pltpu.VMEM((ex * count, n), F32)],
    )
    scores = mine + lax.ppermute(send, "feat", swap)
    return scores.T[:, None, :]


def per_device_gather(train_grads, queries, left_factor, right_factor, block_order):
    row_count = train_grads.shape[0]
    part_rows = train_grads.shape[1]
    right_width = train_grads.shape[2]
    flat_grads = train_grads.reshape(row_count, part_rows * right_width)
    local_queries = queries[0]
    block_size = local_queries.shape[0]
    regrouped = lax.all_to_all(local_queries, "feat", split_axis=0, concat_axis=1, tiled=True)
    whole_mix = jnp.einsum(
        "ik,qkj->qij", left_factor, regrouped.astype(F32), precision=lax.Precision.HIGHEST
    )
    whole_cond = jnp.einsum(
        "qij,jl->qil", whole_mix, right_factor, precision=lax.Precision.HIGHEST
    ).astype(BF16)
    conditioned = lax.all_to_all(whole_cond, "feat", split_axis=1, concat_axis=0, tiled=True)
    conditioned = conditioned.reshape(block_size, part_rows * right_width)
    partials = lax.dot_general(
        flat_grads,
        lax.all_gather(conditioned, "ex", axis=0, tiled=True),
        (((1,), (1,)), ((), ())),
        preferred_element_type=F32,
    )
    block_count = lax.axis_size("ex")
    partials = jnp.take(partials.reshape(row_count, block_count, block_size), block_order, axis=1)
    partials = partials.reshape(row_count, block_count * block_size)
    owned_scores = lax.psum_scatter(partials, "feat", scatter_dimension=1, tiled=True)
    return owned_scores.reshape(row_count, 1, owned_scores.shape[1])


def solution(mesh):
    short_line = mesh.shape["ex"] == 4 and mesh.shape["feat"] == 2
    return jax.shard_map(
        per_device_line if short_line else per_device_gather,
        mesh=mesh,
        in_specs=(
            P(("grp", "ex"), "feat", None),
            P("pb", ("grp", "ex"), "feat", None),
            P("grp", None),
            P("grp", None),
            P("grp"),
        ),
        out_specs=P(("grp", "ex"), "pb", "feat"),
        check_vma=False,
    )
```

```python
import functools

import jax
import jax.numpy as jnp
from jax import lax
from jax.experimental import pallas as pl
from jax.experimental.pallas import tpu as pltpu
from jax.sharding import PartitionSpec as P

F32 = jnp.float32
BF16 = jnp.bfloat16
EARLY = 4
TILE = 16
EXAMPLES = 32
DEEP = 32
VMEM = pl.BlockSpec(memory_space=pltpu.VMEM)
SMEM = pl.BlockSpec(memory_space=pltpu.SMEM)


def parts_of(x, count):
    terms = []
    for _ in range(count):
        top = x.astype(BF16)
        terms.append(top)
        x = x - top.astype(F32)
    return terms


def factor_kernel(left_ref, right_ref, left_out, right_out):
    rows = left_out.shape[0] // 3
    side = lax.axis_index("feat")
    here = pl.ds(pl.multiple_of(side * rows, rows), rows)
    there = pl.ds(pl.multiple_of((1 - side) * rows, rows), rows)
    left = jnp.concatenate([left_ref[here, here], left_ref[here, there]], axis=1)
    left_out[...] = jnp.concatenate(parts_of(left, 3), axis=0)
    right_out[...] = jnp.concatenate(parts_of(right_ref[...], 2), axis=0)


def factor_terms(left, right, rows):
    wide, width = left.shape[1], right.shape[1]
    return pl.pallas_call(
        factor_kernel,
        out_shape=(
            jax.ShapeDtypeStruct((3 * rows, wide), BF16),
            jax.ShapeDtypeStruct((2 * width, width), BF16),
        ),
        in_specs=[VMEM] * 2,
        out_specs=(VMEM, VMEM),
        compiler_params=pltpu.CompilerParams(vmem_limit_bytes=16 << 20),
    )(left, right)


def condition_kernel(own_ref, far_ref, left_ref, right_ref, out_ref, wide_ref):
    count, rows, width = own_ref.shape
    left_terms = left_ref[...]
    right_0, right_1 = right_ref[:width], right_ref[width:]
    for q in range(count):
        query = jnp.concatenate([own_ref[q], far_ref[q]], axis=0)
        mixed = jnp.dot(left_terms, query, preferred_element_type=F32)
        mixed = mixed[:rows] + (mixed[rows : 2 * rows] + mixed[2 * rows :])
        mixed_0, mixed_1 = parts_of(mixed, 2)
        both = jnp.dot(jnp.concatenate([mixed_0, mixed_1], axis=0), right_0, preferred_element_type=F32)
        cross = jnp.dot(mixed_0, right_1, preferred_element_type=F32)
        wide_ref[:, q, :] = both[:rows] + (both[rows:] + cross)
    out_ref[...] = wide_ref[...].astype(BF16)


def condition(own, far, left_terms, right_terms):
    count, rows, width = own.shape
    return pl.pallas_call(
        condition_kernel,
        out_shape=jax.ShapeDtypeStruct((rows, count, width), BF16),
        in_specs=[VMEM] * 4,
        out_specs=VMEM,
        scratch_shapes=[pltpu.VMEM((rows, count, width), F32)],
        compiler_params=pltpu.CompilerParams(vmem_limit_bytes=24 << 20),
        cost_estimate=pl.CostEstimate(flops=count * 3_000_000 * 40, bytes_accessed=8 * count * rows * width, transcendentals=0),
    )(own, far, left_terms, right_terms)


def regroup_kernel(grads_ref, out_ref, held_ref, sems):
    examples, rows, width = held_ref.shape
    blocks = examples // EXAMPLES
    copies = []
    for b in range(blocks):
        part = pl.ds(b * EXAMPLES, EXAMPLES)
        copies.append(pltpu.make_async_copy(grads_ref.at[part], held_ref.at[part], sems.at[b]))
        copies[-1].start()
    i = lax.broadcasted_iota(jnp.int32, (TILE * TILE, TILE * TILE), 0)
    j = lax.broadcasted_iota(jnp.int32, (TILE * TILE, TILE * TILE), 1)
    swap = jnp.where((i // TILE == j % TILE) & (i % TILE == j // TILE), 1.0, 0.0).astype(BF16)
    for b in range(blocks):
        copies[b].wait()

        @pl.loop(b * EXAMPLES // TILE, (b + 1) * EXAMPLES // TILE)
        def _(step):
            n = pl.ds(pl.multiple_of(step * TILE, TILE), TILE)
            for r in range(0, rows, TILE):
                tile = held_ref[n, r : r + TILE, :].reshape(TILE * TILE, width)
                turned = jnp.dot(swap, tile, preferred_element_type=F32).astype(BF16)
                out_ref[r : r + TILE, n, :] = turned.reshape(TILE, TILE, width)


def regroup(grads):
    n, rows, width = grads.shape
    return pl.pallas_call(
        regroup_kernel,
        out_shape=jax.ShapeDtypeStruct((rows, n, width), BF16),
        in_specs=[pl.BlockSpec(memory_space=pltpu.HBM)],
        out_specs=VMEM,
        scratch_shapes=[pltpu.VMEM((n, rows, width), BF16), pltpu.SemaphoreType.DMA((n // EXAMPLES,))],
        compiler_params=pltpu.CompilerParams(vmem_limit_bytes=44 << 20),
        cost_estimate=pl.CostEstimate(flops=6_000_000_000, bytes_accessed=16_000_000, transcendentals=0),
    )(grads)


def inner_products(query_refs, grad_ref, first=0, rows=None):
    total = sum(ref.shape[1] for ref in query_refs)
    rows = rows or grad_ref.shape[0]
    starts = [0 if ref.shape[0] == rows else first for ref in query_refs]

    def body(i, acc):
        at = [i * DEEP + j for j in range(DEEP)]
        queries = [
            jnp.concatenate([ref[start + r] for ref, start in zip(query_refs, starts)], axis=0) for r in at
        ]
        return acc + lax.dot_general(
            jnp.concatenate(queries, axis=1),
            jnp.concatenate([grad_ref[first + r] for r in at], axis=1),
            (((1,), (1,)), ((), ())),
            preferred_element_type=F32,
        )

    start = jnp.zeros((total, grad_ref.shape[1]), F32)
    return lax.fori_loop(0, rows // DEEP, body, start)


def first_pass_kernel(ex, early_ref, own_ref, near, mid, far_in, grad_ref, order_ref, out_ref):
    late = own_ref.shape[1]
    acc = inner_products((early_ref, own_ref, near, mid, far_in), grad_ref)
    sources = slot_sources(lax.axis_index("ex"))
    early = [acc[EARLY * s : EARLY * (s + 1)] for s in range(2)]
    base = early_ref.shape[1]
    slots = [acc[base + late * s : base + late * (s + 1)] for s in range(ex)]
    for b in range(ex):
        block = order_ref[b]
        low = jnp.zeros_like(early[0])
        for source, slot in zip(sources, early):
            low = low + jnp.where(source == block, slot, 0.0)
        high = jnp.zeros_like(slots[0])
        for source, slot in zip(sources, slots):
            high = high + jnp.where(source == block, slot, 0.0)
        at = b * (EARLY + late)
        out_ref[at : at + EARLY, :] = low
        out_ref[at + EARLY : at + EARLY + late, :] = high


def slot_sources(me):
    low_pair = me < 2
    near = jnp.where(low_pair, 1 - me, 5 - me)
    return [me, near, jnp.where(low_pair, 2, 1), jnp.where(low_pair, 3, 0)]


def far_pass_kernel(ex, early_ref, far_out, grad_ref, order_ref, out_ref):
    out_ref[...] = inner_products((early_ref, far_out), grad_ref, 0, far_out.shape[0])


def last_pass_kernel(ex, base_ref, far_ref, early_ref, far_out, grad_ref, order_ref, mine_ref, send_ref, full_ref):
    late = far_out.shape[1]
    acc = far_ref[...] + inner_products((early_ref, far_out), grad_ref, far_out.shape[0], far_out.shape[0])
    mid, far = slot_sources(lax.axis_index("ex"))[2:]
    full_ref[...] = base_ref[...]
    for b in range(ex):
        near_hit, hit = order_ref[b] == mid, order_ref[b] == far
        low = jnp.where(near_hit, acc[:EARLY], 0.0) + jnp.where(hit, acc[EARLY : 2 * EARLY], 0.0)
        at = b * (EARLY + late)
        full_ref[at : at + EARLY, :] = full_ref[at : at + EARLY, :] + low
        at = at + EARLY
        full_ref[at : at + late, :] = full_ref[at : at + late, :] + jnp.where(hit, acc[2 * EARLY :], 0.0)
    half = mine_ref.shape[0]
    side = lax.axis_index("feat")
    mine_ref[...] = full_ref[pl.ds(pl.multiple_of(side * half, half), half), :]
    send_ref[...] = full_ref[pl.ds(pl.multiple_of((1 - side) * half, half), half), :]


def score_call(kernel, ex, arrays, order, out_shape, scratch=()):
    return pl.pallas_call(
        functools.partial(kernel, ex),
        out_shape=out_shape,
        in_specs=[VMEM] * len(arrays) + [SMEM],
        out_specs=jax.tree.map(lambda _: VMEM, out_shape),
        scratch_shapes=scratch,
        compiler_params=pltpu.CompilerParams(vmem_limit_bytes=40 << 20),
        cost_estimate=pl.CostEstimate(flops=1000, bytes_accessed=1000, transcendentals=0),
    )(*arrays, order)


def after(x, *others):
    return lax.optimization_barrier((x, *others))[0]


PAIRS = [(0, 1), (1, 0), (2, 3), (3, 2)]
MIDDLE = [(1, 2), (2, 1)]
OUTWARD = [(1, 0), (2, 3)]


def per_device_line(train_grads, queries, left_factor, right_factor, block_order):
    ex = lax.axis_size("ex")
    swap = [(0, 1), (1, 0)]
    count = queries.shape[1]
    n = train_grads.shape[0]
    late_raw = queries[0, EARLY:]
    late_other = lax.ppermute(late_raw, "feat", swap)
    raw = after(queries, late_raw)[0, :EARLY]
    terms = factor_terms(left_factor, after(right_factor, raw), train_grads.shape[1])
    raw_near = lax.ppermute(raw, "ex", PAIRS)
    raw_mid = lax.ppermute(raw, "ex", MIDDLE)
    raw_mid_out = lax.ppermute(after(raw_mid, *terms), "ex", OUTWARD)
    early_0 = jnp.concatenate([raw, after(raw_near, raw_mid)], axis=0)
    raw_far_mid = lax.ppermute(after(raw_near, early_0, late_other), "ex", MIDDLE)

    late = condition(after(late_raw, raw_near, raw_mid), late_other, *terms)
    near = lax.ppermute(late, "ex", PAIRS)
    mid = lax.ppermute(late, "ex", MIDDLE)
    grads = regroup(after(train_grads, late, raw_mid_out))
    early_0_other = lax.ppermute(after(early_0, late, raw_far_mid, raw_mid_out), "feat", swap)
    raw_far_out = lax.ppermute(after(raw_far_mid, grads), "ex", OUTWARD)
    far_mid = lax.ppermute(after(near, grads), "ex", MIDDLE)
    mid_out = lax.ppermute(after(mid, near, grads), "ex", OUTWARD)
    cond_0 = condition(after(early_0, near, mid), early_0_other, *terms)
    early_1 = jnp.concatenate([raw_mid + raw_mid_out, after(raw_far_mid, near, mid) + raw_far_out], axis=0)
    early_1_other = lax.ppermute(after(early_1, cond_0), "feat", swap)
    part = far_mid.shape[0] // 2
    far_out_0 = lax.ppermute(far_mid[:part], "ex", OUTWARD)
    far_out_1 = lax.ppermute(far_mid[part:], "ex", OUTWARD)
    cond_1 = condition(after(early_1, far_mid), early_1_other, *terms)

    base = score_call(
        first_pass_kernel, ex, (cond_0, late, near, mid + mid_out, far_mid, grads), block_order,
        jax.ShapeDtypeStruct((ex * count, n), F32),
    )
    far_0 = score_call(
        far_pass_kernel, ex, (cond_1, far_out_0, after(grads, base)), block_order,
        jax.ShapeDtypeStruct((2 * EARLY + count - EARLY, n), F32),
    )
    half = jax.ShapeDtypeStruct((ex * count // 2, n), F32)
    mine, send = score_call(
        last_pass_kernel, ex, (base, far_0, cond_1, far_out_1, grads), block_order, (half, half),
        [pltpu.VMEM((ex * count, n), F32)],
    )
    scores = mine + lax.ppermute(send, "feat", swap)
    return scores.T[:, None, :]


def per_device_gather(train_grads, queries, left_factor, right_factor, block_order):
    row_count = train_grads.shape[0]
    part_rows = train_grads.shape[1]
    right_width = train_grads.shape[2]
    flat_grads = train_grads.reshape(row_count, part_rows * right_width)
    local_queries = queries[0]
    block_size = local_queries.shape[0]
    regrouped = lax.all_to_all(local_queries, "feat", split_axis=0, concat_axis=1, tiled=True)
    whole_mix = jnp.einsum(
        "ik,qkj->qij", left_factor, regrouped.astype(F32), precision=lax.Precision.HIGHEST
    )
    whole_cond = jnp.einsum(
        "qij,jl->qil", whole_mix, right_factor, precision=lax.Precision.HIGHEST
    ).astype(BF16)
    conditioned = lax.all_to_all(whole_cond, "feat", split_axis=1, concat_axis=0, tiled=True)
    conditioned = conditioned.reshape(block_size, part_rows * right_width)
    partials = lax.dot_general(
        flat_grads,
        lax.all_gather(conditioned, "ex", axis=0, tiled=True),
        (((1,), (1,)), ((), ())),
        preferred_element_type=F32,
    )
    block_count = lax.axis_size("ex")
    partials = jnp.take(partials.reshape(row_count, block_count, block_size), block_order, axis=1)
    partials = partials.reshape(row_count, block_count * block_size)
    owned_scores = lax.psum_scatter(partials, "feat", scatter_dimension=1, tiled=True)
    return owned_scores.reshape(row_count, 1, owned_scores.shape[1])


def solution(mesh):
    short_line = mesh.shape["ex"] == 4 and mesh.shape["feat"] == 2
    return jax.shard_map(
        per_device_line if short_line else per_device_gather,
        mesh=mesh,
        in_specs=(
            P(("grp", "ex"), "feat", None),
            P("pb", ("grp", "ex"), "feat", None),
            P("grp", None),
            P("grp", None),
            P("grp"),
        ),
        out_specs=P(("grp", "ex"), "pb", "feat"),
        check_vma=False,
    )
```

```python
import functools

import jax
import jax.numpy as jnp
from jax import lax
from jax.experimental import pallas as pl
from jax.experimental.pallas import tpu as pltpu
from jax.sharding import PartitionSpec as P

F32 = jnp.float32
BF16 = jnp.bfloat16
EARLY = 4
TILE = 16
EXAMPLES = 32
DEEP = 32
VMEM = pl.BlockSpec(memory_space=pltpu.VMEM)
SMEM = pl.BlockSpec(memory_space=pltpu.SMEM)


def parts_of(x, count):
    terms = []
    for _ in range(count):
        top = x.astype(BF16)
        terms.append(top)
        x = x - top.astype(F32)
    return terms


def factor_kernel(left_ref, right_ref, left_out, right_out):
    rows = left_out.shape[0] // 3
    side = lax.axis_index("feat")
    here = pl.ds(pl.multiple_of(side * rows, rows), rows)
    there = pl.ds(pl.multiple_of((1 - side) * rows, rows), rows)
    left = jnp.concatenate([left_ref[here, here], left_ref[here, there]], axis=1)
    left_out[...] = jnp.concatenate(parts_of(left, 3), axis=0)
    right_out[...] = jnp.concatenate(parts_of(right_ref[...], 2), axis=0)


def factor_terms(left, right, rows):
    wide, width = left.shape[1], right.shape[1]
    return pl.pallas_call(
        factor_kernel,
        out_shape=(
            jax.ShapeDtypeStruct((3 * rows, wide), BF16),
            jax.ShapeDtypeStruct((2 * width, width), BF16),
        ),
        in_specs=[VMEM] * 2,
        out_specs=(VMEM, VMEM),
        compiler_params=pltpu.CompilerParams(vmem_limit_bytes=16 << 20),
    )(left, right)


def condition_kernel(own_ref, far_ref, left_ref, right_ref, out_ref, wide_ref):
    count, rows, width = own_ref.shape
    left_terms = left_ref[...]
    right_0, right_1 = right_ref[:width], right_ref[width:]
    for q in range(count):
        query = jnp.concatenate([own_ref[q], far_ref[q]], axis=0)
        mixed = jnp.dot(left_terms, query, preferred_element_type=F32)
        mixed = mixed[:rows] + (mixed[rows : 2 * rows] + mixed[2 * rows :])
        mixed_0, mixed_1 = parts_of(mixed, 2)
        both = jnp.dot(jnp.concatenate([mixed_0, mixed_1], axis=0), right_0, preferred_element_type=F32)
        cross = jnp.dot(mixed_0, right_1, preferred_element_type=F32)
        wide_ref[:, q, :] = both[:rows] + (both[rows:] + cross)
    out_ref[...] = wide_ref[...].astype(BF16)


def condition(own, far, left_terms, right_terms):
    count, rows, width = own.shape
    return pl.pallas_call(
        condition_kernel,
        out_shape=jax.ShapeDtypeStruct((rows, count, width), BF16),
        in_specs=[VMEM] * 4,
        out_specs=VMEM,
        scratch_shapes=[pltpu.VMEM((rows, count, width), F32)],
        compiler_params=pltpu.CompilerParams(vmem_limit_bytes=24 << 20),
        cost_estimate=pl.CostEstimate(flops=count * 3_000_000 * 40, bytes_accessed=8 * count * rows * width, transcendentals=0),
    )(own, far, left_terms, right_terms)


def regroup_kernel(grads_ref, out_ref, held_ref, sems):
    examples, rows, width = held_ref.shape
    blocks = examples // EXAMPLES
    copies = []
    for b in range(blocks):
        part = pl.ds(b * EXAMPLES, EXAMPLES)
        copies.append(pltpu.make_async_copy(grads_ref.at[part], held_ref.at[part], sems.at[b]))
        copies[-1].start()
    i = lax.broadcasted_iota(jnp.int32, (TILE * TILE, TILE * TILE), 0)
    j = lax.broadcasted_iota(jnp.int32, (TILE * TILE, TILE * TILE), 1)
    swap = jnp.where((i // TILE == j % TILE) & (i % TILE == j // TILE), 1.0, 0.0).astype(BF16)
    for b in range(blocks):
        copies[b].wait()

        @pl.loop(b * EXAMPLES // TILE, (b + 1) * EXAMPLES // TILE)
        def _(step):
            n = pl.ds(pl.multiple_of(step * TILE, TILE), TILE)
            for r in range(0, rows, TILE):
                tile = held_ref[n, r : r + TILE, :].reshape(TILE * TILE, width)
                turned = jnp.dot(swap, tile, preferred_element_type=F32).astype(BF16)
                out_ref[r : r + TILE, n, :] = turned.reshape(TILE, TILE, width)


def regroup(grads):
    n, rows, width = grads.shape
    return pl.pallas_call(
        regroup_kernel,
        out_shape=jax.ShapeDtypeStruct((rows, n, width), BF16),
        in_specs=[pl.BlockSpec(memory_space=pltpu.HBM)],
        out_specs=VMEM,
        scratch_shapes=[pltpu.VMEM((n, rows, width), BF16), pltpu.SemaphoreType.DMA((n // EXAMPLES,))],
        compiler_params=pltpu.CompilerParams(vmem_limit_bytes=44 << 20),
        cost_estimate=pl.CostEstimate(flops=6_000_000_000, bytes_accessed=16_000_000, transcendentals=0),
    )(grads)


def inner_products(query_refs, grad_ref, first=0, rows=None):
    total = sum(ref.shape[1] for ref in query_refs)
    rows = rows or grad_ref.shape[0]
    starts = [0 if ref.shape[0] == rows else first for ref in query_refs]

    def body(i, acc):
        at = [i * DEEP + j for j in range(DEEP)]
        queries = [
            jnp.concatenate([ref[start + r] for ref, start in zip(query_refs, starts)], axis=0) for r in at
        ]
        return acc + lax.dot_general(
            jnp.concatenate(queries, axis=1),
            jnp.concatenate([grad_ref[first + r] for r in at], axis=1),
            (((1,), (1,)), ((), ())),
            preferred_element_type=F32,
        )

    start = jnp.zeros((total, grad_ref.shape[1]), F32)
    return lax.fori_loop(0, rows // DEEP, body, start)


def first_pass_kernel(ex, early_ref, own_ref, near, far_in, grad_ref, order_ref, out_ref):
    late = own_ref.shape[1]
    acc = inner_products((early_ref, own_ref, near, far_in), grad_ref)
    sources = slot_sources(lax.axis_index("ex"))
    early = [acc[EARLY * s : EARLY * (s + 1)] for s in range(2)]
    base = early_ref.shape[1]
    slots = [acc[base + late * s : base + late * (s + 1)] for s in range(3)]
    for b in range(ex):
        block = order_ref[b]
        low = jnp.zeros_like(early[0])
        for source, slot in zip(sources, early):
            low = low + jnp.where(source == block, slot, 0.0)
        high = jnp.zeros_like(slots[0])
        for source, slot in zip(sources[:2] + sources[3:], slots):
            high = high + jnp.where(source == block, slot, 0.0)
        at = b * (EARLY + late)
        out_ref[at : at + EARLY, :] = low
        out_ref[at + EARLY : at + EARLY + late, :] = high


def slot_sources(me):
    low_pair = me < 2
    near = jnp.where(low_pair, 1 - me, 5 - me)
    return [me, near, jnp.where(low_pair, 2, 1), jnp.where(low_pair, 3, 0)]


def far_pass_kernel(ex, early_ref, mid_ref, far_out, grad_ref, order_ref, out_ref):
    out_ref[...] = inner_products((early_ref, mid_ref, far_out), grad_ref, 0, far_out.shape[0])


def last_pass_kernel(
    ex, base_ref, far_ref, early_ref, mid_ref, far_out, grad_ref, order_ref, mine_ref, send_ref, full_ref
):
    late = far_out.shape[1]
    rows = far_out.shape[0]
    acc = far_ref[...] + inner_products((early_ref, mid_ref, far_out), grad_ref, rows, rows)
    mid, far = slot_sources(lax.axis_index("ex"))[2:]
    low_mid, low_far = acc[:EARLY], acc[EARLY : 2 * EARLY]
    high_mid, high_far = acc[2 * EARLY : 2 * EARLY + late], acc[2 * EARLY + late :]
    full_ref[...] = base_ref[...]
    for b in range(ex):
        mid_hit, far_hit = order_ref[b] == mid, order_ref[b] == far
        low = jnp.where(mid_hit, low_mid, 0.0) + jnp.where(far_hit, low_far, 0.0)
        high = jnp.where(mid_hit, high_mid, 0.0) + jnp.where(far_hit, high_far, 0.0)
        at = b * (EARLY + late)
        full_ref[at : at + EARLY, :] = full_ref[at : at + EARLY, :] + low
        at = at + EARLY
        full_ref[at : at + late, :] = full_ref[at : at + late, :] + high
    half = mine_ref.shape[0]
    side = lax.axis_index("feat")
    mine_ref[...] = full_ref[pl.ds(pl.multiple_of(side * half, half), half), :]
    send_ref[...] = full_ref[pl.ds(pl.multiple_of((1 - side) * half, half), half), :]


def score_call(kernel, ex, arrays, order, out_shape, scratch=()):
    return pl.pallas_call(
        functools.partial(kernel, ex),
        out_shape=out_shape,
        in_specs=[VMEM] * len(arrays) + [SMEM],
        out_specs=jax.tree.map(lambda _: VMEM, out_shape),
        scratch_shapes=scratch,
        compiler_params=pltpu.CompilerParams(vmem_limit_bytes=40 << 20),
        cost_estimate=pl.CostEstimate(flops=1000, bytes_accessed=1000, transcendentals=0),
    )(*arrays, order)


def after(x, *others):
    return lax.optimization_barrier((x, *others))[0]


PAIRS = [(0, 1), (1, 0), (2, 3), (3, 2)]
MIDDLE = [(1, 2), (2, 1)]
OUTWARD = [(1, 0), (2, 3)]


def per_device_line(train_grads, queries, left_factor, right_factor, block_order):
    ex = lax.axis_size("ex")
    swap = [(0, 1), (1, 0)]
    count = queries.shape[1]
    n = train_grads.shape[0]
    late_raw = queries[0, EARLY:]
    late_other = lax.ppermute(late_raw, "feat", swap)
    raw = after(queries, late_raw)[0, :EARLY]
    terms = factor_terms(left_factor, after(right_factor, raw), train_grads.shape[1])
    raw_near = lax.ppermute(raw, "ex", PAIRS)
    raw_mid = lax.ppermute(raw, "ex", MIDDLE)
    raw_mid_out = lax.ppermute(after(raw_mid, *terms), "ex", OUTWARD)
    early_0 = jnp.concatenate([raw, after(raw_near, raw_mid)], axis=0)
    raw_far_mid = lax.ppermute(after(raw_near, early_0, late_other), "ex", MIDDLE)

    late = condition(after(late_raw, raw_near, raw_mid), late_other, *terms)
    near = lax.ppermute(late, "ex", PAIRS)
    mid = lax.ppermute(late, "ex", MIDDLE)
    grads = regroup(after(train_grads, late, raw_mid_out))
    early_0_other = lax.ppermute(after(early_0, late, raw_far_mid, raw_mid_out), "feat", swap)
    raw_far_out = lax.ppermute(after(raw_far_mid, grads), "ex", OUTWARD)
    far_mid = lax.ppermute(after(near, grads), "ex", MIDDLE)
    mid_out = lax.ppermute(after(mid, near, grads), "ex", OUTWARD)
    cond_0 = condition(after(early_0, near, mid), early_0_other, *terms)
    early_1 = jnp.concatenate([raw_mid + raw_mid_out, after(raw_far_mid, near, mid) + raw_far_out], axis=0)
    early_1_other = lax.ppermute(after(early_1, cond_0), "feat", swap)
    part = far_mid.shape[0] // 2
    far_out_0 = lax.ppermute(far_mid[:part], "ex", OUTWARD)
    far_out_1 = lax.ppermute(far_mid[part:], "ex", OUTWARD)
    cond_1 = condition(after(early_1, far_mid), early_1_other, *terms)

    base = score_call(
        first_pass_kernel, ex, (cond_0, late, near, far_mid, grads), block_order,
        jax.ShapeDtypeStruct((ex * count, n), F32),
    )
    mid = mid + mid_out
    far_0 = score_call(
        far_pass_kernel, ex, (cond_1, mid, far_out_0, after(grads, base)), block_order,
        jax.ShapeDtypeStruct((2 * count, n), F32),
    )
    half = jax.ShapeDtypeStruct((ex * count // 2, n), F32)
    mine, send = score_call(
        last_pass_kernel, ex, (base, far_0, cond_1, mid, far_out_1, grads), block_order, (half, half),
        [pltpu.VMEM((ex * count, n), F32)],
    )
    scores = mine + lax.ppermute(send, "feat", swap)
    return scores.T[:, None, :]


def per_device_gather(train_grads, queries, left_factor, right_factor, block_order):
    row_count = train_grads.shape[0]
    part_rows = train_grads.shape[1]
    right_width = train_grads.shape[2]
    flat_grads = train_grads.reshape(row_count, part_rows * right_width)
    local_queries = queries[0]
    block_size = local_queries.shape[0]
    regrouped = lax.all_to_all(local_queries, "feat", split_axis=0, concat_axis=1, tiled=True)
    whole_mix = jnp.einsum(
        "ik,qkj->qij", left_factor, regrouped.astype(F32), precision=lax.Precision.HIGHEST
    )
    whole_cond = jnp.einsum(
        "qij,jl->qil", whole_mix, right_factor, precision=lax.Precision.HIGHEST
    ).astype(BF16)
    conditioned = lax.all_to_all(whole_cond, "feat", split_axis=1, concat_axis=0, tiled=True)
    conditioned = conditioned.reshape(block_size, part_rows * right_width)
    partials = lax.dot_general(
        flat_grads,
        lax.all_gather(conditioned, "ex", axis=0, tiled=True),
        (((1,), (1,)), ((), ())),
        preferred_element_type=F32,
    )
    block_count = lax.axis_size("ex")
    partials = jnp.take(partials.reshape(row_count, block_count, block_size), block_order, axis=1)
    partials = partials.reshape(row_count, block_count * block_size)
    owned_scores = lax.psum_scatter(partials, "feat", scatter_dimension=1, tiled=True)
    return owned_scores.reshape(row_count, 1, owned_scores.shape[1])


def solution(mesh):
    short_line = mesh.shape["ex"] == 4 and mesh.shape["feat"] == 2
    return jax.shard_map(
        per_device_line if short_line else per_device_gather,
        mesh=mesh,
        in_specs=(
            P(("grp", "ex"), "feat", None),
            P("pb", ("grp", "ex"), "feat", None),
            P("grp", None),
            P("grp", None),
            P("grp"),
        ),
        out_specs=P(("grp", "ex"), "pb", "feat"),
        check_vma=False,
    )
```

```python
import functools

import jax
import jax.numpy as jnp
from jax import lax
from jax.experimental import pallas as pl
from jax.experimental.pallas import tpu as pltpu
from jax.sharding import PartitionSpec as P

F32 = jnp.float32
BF16 = jnp.bfloat16
EARLY = 4
TILE = 16
EXAMPLES = 32
DEEP = 32
VMEM = pl.BlockSpec(memory_space=pltpu.VMEM)
SMEM = pl.BlockSpec(memory_space=pltpu.SMEM)


def parts_of(x, count):
    terms = []
    for _ in range(count):
        top = x.astype(BF16)
        terms.append(top)
        x = x - top.astype(F32)
    return terms


def factor_kernel(left_ref, right_ref, left_out, right_out):
    rows = left_out.shape[0] // 3
    side = lax.axis_index("feat")
    here = pl.ds(pl.multiple_of(side * rows, rows), rows)
    there = pl.ds(pl.multiple_of((1 - side) * rows, rows), rows)
    left = jnp.concatenate([left_ref[here, here], left_ref[here, there]], axis=1)
    left_out[...] = jnp.concatenate(parts_of(left, 3), axis=0)
    right_out[...] = jnp.concatenate(parts_of(right_ref[...], 2), axis=0)


def factor_terms(left, right, rows):
    wide, width = left.shape[1], right.shape[1]
    return pl.pallas_call(
        factor_kernel,
        out_shape=(
            jax.ShapeDtypeStruct((3 * rows, wide), BF16),
            jax.ShapeDtypeStruct((2 * width, width), BF16),
        ),
        in_specs=[VMEM] * 2,
        out_specs=(VMEM, VMEM),
        compiler_params=pltpu.CompilerParams(vmem_limit_bytes=16 << 20),
    )(left, right)


def condition_kernel(own_ref, far_ref, left_ref, right_ref, out_ref, wide_ref):
    count, rows, width = own_ref.shape
    left_terms = left_ref[...]
    right_0, right_1 = right_ref[:width], right_ref[width:]
    for q in range(count):
        query = jnp.concatenate([own_ref[q], far_ref[q]], axis=0)
        mixed = jnp.dot(left_terms, query, preferred_element_type=F32)
        mixed = mixed[:rows] + (mixed[rows : 2 * rows] + mixed[2 * rows :])
        mixed_0, mixed_1 = parts_of(mixed, 2)
        both = jnp.dot(jnp.concatenate([mixed_0, mixed_1], axis=0), right_0, preferred_element_type=F32)
        cross = jnp.dot(mixed_0, right_1, preferred_element_type=F32)
        wide_ref[:, q, :] = both[:rows] + (both[rows:] + cross)
    out_ref[...] = wide_ref[...].astype(BF16)


def condition(own, far, left_terms, right_terms):
    count, rows, width = own.shape
    return pl.pallas_call(
        condition_kernel,
        out_shape=jax.ShapeDtypeStruct((rows, count, width), BF16),
        in_specs=[VMEM] * 4,
        out_specs=VMEM,
        scratch_shapes=[pltpu.VMEM((rows, count, width), F32)],
        compiler_params=pltpu.CompilerParams(vmem_limit_bytes=24 << 20),
        cost_estimate=pl.CostEstimate(flops=count * 3_000_000 * 40, bytes_accessed=8 * count * rows * width, transcendentals=0),
    )(own, far, left_terms, right_terms)


def split_kernel(queries_ref, early_ref, late_ref, sems):
    early = pltpu.make_async_copy(queries_ref.at[0, pl.ds(0, EARLY)], early_ref, sems.at[0])
    late = pltpu.make_async_copy(queries_ref.at[0, pl.ds(EARLY, late_ref.shape[0])], late_ref, sems.at[1])
    early.start()
    late.start()
    early.wait()
    late.wait()


def split(queries):
    _, count, rows, width = queries.shape
    return pl.pallas_call(
        split_kernel,
        out_shape=(
            jax.ShapeDtypeStruct((EARLY, rows, width), BF16),
            jax.ShapeDtypeStruct((count - EARLY, rows, width), BF16),
        ),
        in_specs=[pl.BlockSpec(memory_space=pltpu.HBM)],
        out_specs=(VMEM, VMEM),
        scratch_shapes=[pltpu.SemaphoreType.DMA((2,))],
        compiler_params=pltpu.CompilerParams(vmem_limit_bytes=62_300_000),
    )(queries)


def regroup_kernel(grads_ref, out_ref, held_ref, sems):
    examples, rows, width = held_ref.shape
    blocks = examples // EXAMPLES
    copies = []
    for b in range(blocks):
        part = pl.ds(b * EXAMPLES, EXAMPLES)
        copies.append(pltpu.make_async_copy(grads_ref.at[part], held_ref.at[part], sems.at[b]))
        copies[-1].start()
    i = lax.broadcasted_iota(jnp.int32, (TILE * TILE, TILE * TILE), 0)
    j = lax.broadcasted_iota(jnp.int32, (TILE * TILE, TILE * TILE), 1)
    swap = jnp.where((i // TILE == j % TILE) & (i % TILE == j // TILE), 1.0, 0.0).astype(BF16)
    for b in range(blocks):
        copies[b].wait()

        @pl.loop(b * EXAMPLES // TILE, (b + 1) * EXAMPLES // TILE)
        def _(step):
            n = pl.ds(pl.multiple_of(step * TILE, TILE), TILE)
            for r in range(0, rows, TILE):
                tile = held_ref[n, r : r + TILE, :].reshape(TILE * TILE, width)
                turned = jnp.dot(swap, tile, preferred_element_type=F32).astype(BF16)
                out_ref[r : r + TILE, n, :] = turned.reshape(TILE, TILE, width)


def regroup(grads):
    n, rows, width = grads.shape
    return pl.pallas_call(
        regroup_kernel,
        out_shape=jax.ShapeDtypeStruct((rows, n, width), BF16),
        in_specs=[pl.BlockSpec(memory_space=pltpu.HBM)],
        out_specs=VMEM,
        scratch_shapes=[pltpu.VMEM((n, rows, width), BF16), pltpu.SemaphoreType.DMA((n // EXAMPLES,))],
        compiler_params=pltpu.CompilerParams(vmem_limit_bytes=44 << 20),
        cost_estimate=pl.CostEstimate(flops=6_000_000_000, bytes_accessed=16_000_000, transcendentals=0),
    )(grads)


def inner_products(query_refs, grad_ref, first=0, rows=None):
    total = sum(ref.shape[1] for ref in query_refs)
    rows = rows or grad_ref.shape[0]
    starts = [0 if ref.shape[0] == rows else first for ref in query_refs]

    def body(i, acc):
        at = [i * DEEP + j for j in range(DEEP)]
        queries = [
            jnp.concatenate([ref[start + r] for ref, start in zip(query_refs, starts)], axis=0) for r in at
        ]
        return acc + lax.dot_general(
            jnp.concatenate(queries, axis=1),
            jnp.concatenate([grad_ref[first + r] for r in at], axis=1),
            (((1,), (1,)), ((), ())),
            preferred_element_type=F32,
        )

    start = jnp.zeros((total, grad_ref.shape[1]), F32)
    return lax.fori_loop(0, rows // DEEP, body, start)


def first_pass_kernel(ex, early_ref, own_ref, near, far_in, grad_ref, order_ref, out_ref):
    late = own_ref.shape[1]
    acc = inner_products((early_ref, own_ref, near, far_in), grad_ref)
    sources = slot_sources(lax.axis_index("ex"))
    early = [acc[EARLY * s : EARLY * (s + 1)] for s in range(2)]
    base = early_ref.shape[1]
    slots = [acc[base + late * s : base + late * (s + 1)] for s in range(3)]
    for b in range(ex):
        block = order_ref[b]
        low = jnp.zeros_like(early[0])
        for source, slot in zip(sources, early):
            low = low + jnp.where(source == block, slot, 0.0)
        high = jnp.zeros_like(slots[0])
        for source, slot in zip(sources[:2] + sources[3:], slots):
            high = high + jnp.where(source == block, slot, 0.0)
        at = b * (EARLY + late)
        out_ref[at : at + EARLY, :] = low
        out_ref[at + EARLY : at + EARLY + late, :] = high


def slot_sources(me):
    low_pair = me < 2
    near = jnp.where(low_pair, 1 - me, 5 - me)
    return [me, near, jnp.where(low_pair, 2, 1), jnp.where(low_pair, 3, 0)]


def far_pass_kernel(ex, early_ref, mid_ref, far_out, grad_ref, order_ref, out_ref):
    out_ref[...] = inner_products((early_ref, mid_ref, far_out), grad_ref, 0, far_out.shape[0])


def last_pass_kernel(
    ex, base_ref, far_ref, early_ref, mid_ref, far_out, grad_ref, order_ref, mine_ref, send_ref, full_ref
):
    late = far_out.shape[1]
    rows = far_out.shape[0]
    acc = far_ref[...] + inner_products((early_ref, mid_ref, far_out), grad_ref, rows, rows)
    mid, far = slot_sources(lax.axis_index("ex"))[2:]
    low_mid, low_far = acc[:EARLY], acc[EARLY : 2 * EARLY]
    high_mid, high_far = acc[2 * EARLY : 2 * EARLY + late], acc[2 * EARLY + late :]
    full_ref[...] = base_ref[...]
    for b in range(ex):
        mid_hit, far_hit = order_ref[b] == mid, order_ref[b] == far
        low = jnp.where(mid_hit, low_mid, 0.0) + jnp.where(far_hit, low_far, 0.0)
        high = jnp.where(mid_hit, high_mid, 0.0) + jnp.where(far_hit, high_far, 0.0)
        at = b * (EARLY + late)
        full_ref[at : at + EARLY, :] = full_ref[at : at + EARLY, :] + low
        at = at + EARLY
        full_ref[at : at + late, :] = full_ref[at : at + late, :] + high
    half = mine_ref.shape[0]
    side = lax.axis_index("feat")
    mine_ref[...] = full_ref[pl.ds(pl.multiple_of(side * half, half), half), :]
    send_ref[...] = full_ref[pl.ds(pl.multiple_of((1 - side) * half, half), half), :]


def score_call(kernel, ex, arrays, order, out_shape, scratch=()):
    return pl.pallas_call(
        functools.partial(kernel, ex),
        out_shape=out_shape,
        in_specs=[VMEM] * len(arrays) + [SMEM],
        out_specs=jax.tree.map(lambda _: VMEM, out_shape),
        scratch_shapes=scratch,
        compiler_params=pltpu.CompilerParams(vmem_limit_bytes=40 << 20),
        cost_estimate=pl.CostEstimate(flops=1000, bytes_accessed=1000, transcendentals=0),
    )(*arrays, order)


def after(x, *others):
    return lax.optimization_barrier((x, *others))[0]


PAIRS = [(0, 1), (1, 0), (2, 3), (3, 2)]
MIDDLE = [(1, 2), (2, 1)]
OUTWARD = [(1, 0), (2, 3)]


def per_device_line(train_grads, queries, left_factor, right_factor, block_order):
    ex = lax.axis_size("ex")
    swap = [(0, 1), (1, 0)]
    count = queries.shape[1]
    n = train_grads.shape[0]
    raw, late_raw = split(queries)
    late_other = lax.ppermute(late_raw, "feat", swap)
    terms = factor_terms(left_factor, after(right_factor, raw), train_grads.shape[1])
    raw_near = lax.ppermute(raw, "ex", PAIRS)
    raw_mid = lax.ppermute(raw, "ex", MIDDLE)
    raw_mid_out = lax.ppermute(after(raw_mid, *terms), "ex", OUTWARD)
    early_0 = jnp.concatenate([raw, after(raw_near, raw_mid)], axis=0)
    raw_far_mid = lax.ppermute(after(raw_near, early_0, late_other), "ex", MIDDLE)

    late = condition(after(late_raw, raw_near, raw_mid), late_other, *terms)
    near = lax.ppermute(late, "ex", PAIRS)
    mid = lax.ppermute(late, "ex", MIDDLE)
    grads = regroup(after(train_grads, late, raw_mid_out))
    early_0_other = lax.ppermute(after(early_0, late, raw_far_mid, raw_mid_out), "feat", swap)
    raw_far_out = lax.ppermute(after(raw_far_mid, grads), "ex", OUTWARD)
    far_mid = lax.ppermute(after(near, grads), "ex", MIDDLE)
    mid_out = lax.ppermute(after(mid, near, grads), "ex", OUTWARD)
    cond_0 = condition(after(early_0, near, mid), early_0_other, *terms)
    early_1 = jnp.concatenate([raw_mid + raw_mid_out, after(raw_far_mid, near, mid) + raw_far_out], axis=0)
    early_1_other = lax.ppermute(after(early_1, cond_0), "feat", swap)
    part = far_mid.shape[0] // 2
    far_out_0 = lax.ppermute(far_mid[:part], "ex", OUTWARD)
    far_out_1 = lax.ppermute(far_mid[part:], "ex", OUTWARD)
    cond_1 = condition(after(early_1, far_mid), early_1_other, *terms)

    base = score_call(
        first_pass_kernel, ex, (cond_0, late, near, far_mid, grads), block_order,
        jax.ShapeDtypeStruct((ex * count, n), F32),
    )
    mid = mid + mid_out
    far_0 = score_call(
        far_pass_kernel, ex, (cond_1, mid, far_out_0, after(grads, base)), block_order,
        jax.ShapeDtypeStruct((2 * count, n), F32),
    )
    half = jax.ShapeDtypeStruct((ex * count // 2, n), F32)
    mine, send = score_call(
        last_pass_kernel, ex, (base, far_0, cond_1, mid, far_out_1, grads), block_order, (half, half),
        [pltpu.VMEM((ex * count, n), F32)],
    )
    scores = mine + lax.ppermute(send, "feat", swap)
    return scores.T[:, None, :]


def per_device_gather(train_grads, queries, left_factor, right_factor, block_order):
    row_count = train_grads.shape[0]
    part_rows = train_grads.shape[1]
    right_width = train_grads.shape[2]
    flat_grads = train_grads.reshape(row_count, part_rows * right_width)
    local_queries = queries[0]
    block_size = local_queries.shape[0]
    regrouped = lax.all_to_all(local_queries, "feat", split_axis=0, concat_axis=1, tiled=True)
    whole_mix = jnp.einsum(
        "ik,qkj->qij", left_factor, regrouped.astype(F32), precision=lax.Precision.HIGHEST
    )
    whole_cond = jnp.einsum(
        "qij,jl->qil", whole_mix, right_factor, precision=lax.Precision.HIGHEST
    ).astype(BF16)
    conditioned = lax.all_to_all(whole_cond, "feat", split_axis=1, concat_axis=0, tiled=True)
    conditioned = conditioned.reshape(block_size, part_rows * right_width)
    partials = lax.dot_general(
        flat_grads,
        lax.all_gather(conditioned, "ex", axis=0, tiled=True),
        (((1,), (1,)), ((), ())),
        preferred_element_type=F32,
    )
    block_count = lax.axis_size("ex")
    partials = jnp.take(partials.reshape(row_count, block_count, block_size), block_order, axis=1)
    partials = partials.reshape(row_count, block_count * block_size)
    owned_scores = lax.psum_scatter(partials, "feat", scatter_dimension=1, tiled=True)
    return owned_scores.reshape(row_count, 1, owned_scores.shape[1])


def solution(mesh):
    short_line = mesh.shape["ex"] == 4 and mesh.shape["feat"] == 2
    return jax.shard_map(
        per_device_line if short_line else per_device_gather,
        mesh=mesh,
        in_specs=(
            P(("grp", "ex"), "feat", None),
            P("pb", ("grp", "ex"), "feat", None),
            P("grp", None),
            P("grp", None),
            P("grp"),
        ),
        out_specs=P(("grp", "ex"), "pb", "feat"),
        check_vma=False,
    )
```

```python
import functools

import jax
import jax.numpy as jnp
from jax import lax
from jax.experimental import pallas as pl
from jax.experimental.pallas import tpu as pltpu
from jax.sharding import PartitionSpec as P

F32 = jnp.float32
BF16 = jnp.bfloat16
EARLY = 4
TILE = 16
EXAMPLES = 32
DEEP = 32
VMEM = pl.BlockSpec(memory_space=pltpu.VMEM)
SMEM = pl.BlockSpec(memory_space=pltpu.SMEM)


def parts_of(x, count):
    terms = []
    for _ in range(count):
        top = x.astype(BF16)
        terms.append(top)
        x = x - top.astype(F32)
    return terms


def factor_kernel(left_ref, right_ref, left_out, right_out):
    rows = left_out.shape[0] // 3
    side = lax.axis_index("feat")
    here = pl.ds(pl.multiple_of(side * rows, rows), rows)
    there = pl.ds(pl.multiple_of((1 - side) * rows, rows), rows)
    left = jnp.concatenate([left_ref[here, here], left_ref[here, there]], axis=1)
    left_out[...] = jnp.concatenate(parts_of(left, 3), axis=0)
    right_out[...] = jnp.concatenate(parts_of(right_ref[...], 2), axis=0)


def factor_terms(left, right, rows):
    wide, width = left.shape[1], right.shape[1]
    return pl.pallas_call(
        factor_kernel,
        out_shape=(
            jax.ShapeDtypeStruct((3 * rows, wide), BF16),
            jax.ShapeDtypeStruct((2 * width, width), BF16),
        ),
        in_specs=[VMEM] * 2,
        out_specs=(VMEM, VMEM),
        compiler_params=pltpu.CompilerParams(vmem_limit_bytes=16 << 20),
    )(left, right)


def condition_kernel(own_ref, far_ref, left_ref, right_ref, out_ref, wide_ref):
    count, rows, width = own_ref.shape
    left_terms = left_ref[...]
    right_0, right_1 = right_ref[:width], right_ref[width:]
    for q in range(count):
        query = jnp.concatenate([own_ref[q], far_ref[q]], axis=0)
        mixed = jnp.dot(left_terms, query, preferred_element_type=F32)
        mixed = mixed[:rows] + (mixed[rows : 2 * rows] + mixed[2 * rows :])
        mixed_0, mixed_1 = parts_of(mixed, 2)
        both = jnp.dot(jnp.concatenate([mixed_0, mixed_1], axis=0), right_0, preferred_element_type=F32)
        cross = jnp.dot(mixed_0, right_1, preferred_element_type=F32)
        wide_ref[:, q, :] = both[:rows] + (both[rows:] + cross)
    out_ref[...] = wide_ref[...].astype(BF16)


def condition(own, far, left_terms, right_terms):
    count, rows, width = own.shape
    return pl.pallas_call(
        condition_kernel,
        out_shape=jax.ShapeDtypeStruct((rows, count, width), BF16),
        in_specs=[VMEM] * 4,
        out_specs=VMEM,
        scratch_shapes=[pltpu.VMEM((rows, count, width), F32)],
        compiler_params=pltpu.CompilerParams(vmem_limit_bytes=24 << 20),
        cost_estimate=pl.CostEstimate(flops=count * 3_000_000 * 40, bytes_accessed=8 * count * rows * width, transcendentals=0),
    )(own, far, left_terms, right_terms)


def regroup_kernel(grads_ref, out_ref, held_ref, sems):
    examples, rows, width = held_ref.shape
    blocks = examples // EXAMPLES
    copies = []
    for b in range(blocks):
        part = pl.ds(b * EXAMPLES, EXAMPLES)
        copies.append(pltpu.make_async_copy(grads_ref.at[part], held_ref.at[part], sems.at[b]))
        copies[-1].start()
    i = lax.broadcasted_iota(jnp.int32, (TILE * TILE, TILE * TILE), 0)
    j = lax.broadcasted_iota(jnp.int32, (TILE * TILE, TILE * TILE), 1)
    swap = jnp.where((i // TILE == j % TILE) & (i % TILE == j // TILE), 1.0, 0.0).astype(BF16)
    for b in range(blocks):
        copies[b].wait()

        @pl.loop(b * EXAMPLES // TILE, (b + 1) * EXAMPLES // TILE)
        def _(step):
            n = pl.ds(pl.multiple_of(step * TILE, TILE), TILE)
            for r in range(0, rows, TILE):
                tile = held_ref[n, r : r + TILE, :].reshape(TILE * TILE, width)
                turned = jnp.dot(swap, tile, preferred_element_type=F32).astype(BF16)
                out_ref[r : r + TILE, n, :] = turned.reshape(TILE, TILE, width)


def regroup(grads):
    n, rows, width = grads.shape
    return pl.pallas_call(
        regroup_kernel,
        out_shape=jax.ShapeDtypeStruct((rows, n, width), BF16),
        in_specs=[pl.BlockSpec(memory_space=pltpu.HBM)],
        out_specs=VMEM,
        scratch_shapes=[pltpu.VMEM((n, rows, width), BF16), pltpu.SemaphoreType.DMA((n // EXAMPLES,))],
        compiler_params=pltpu.CompilerParams(vmem_limit_bytes=44 << 20),
        cost_estimate=pl.CostEstimate(flops=6_000_000_000, bytes_accessed=16_000_000, transcendentals=0),
    )(grads)


def inner_products(query_refs, grad_ref, first=0, rows=None):
    total = sum(ref.shape[1] for ref in query_refs)
    rows = rows or grad_ref.shape[0]
    starts = [0 if ref.shape[0] == rows else first for ref in query_refs]

    def body(i, acc):
        at = [i * DEEP + j for j in range(DEEP)]
        queries = [
            jnp.concatenate([ref[start + r] for ref, start in zip(query_refs, starts)], axis=0) for r in at
        ]
        return acc + lax.dot_general(
            jnp.concatenate(queries, axis=1),
            jnp.concatenate([grad_ref[first + r] for r in at], axis=1),
            (((1,), (1,)), ((), ())),
            preferred_element_type=F32,
        )

    start = jnp.zeros((total, grad_ref.shape[1]), F32)
    return lax.fori_loop(0, rows // DEEP, body, start)


def first_pass_kernel(ex, early_ref, own_ref, near, far_in, grad_ref, order_ref, out_ref):
    late = own_ref.shape[1]
    acc = inner_products((early_ref, own_ref, near, far_in), grad_ref)
    sources = slot_sources(lax.axis_index("ex"))
    early = [acc[EARLY * s : EARLY * (s + 1)] for s in range(2)]
    base = early_ref.shape[1]
    slots = [acc[base + late * s : base + late * (s + 1)] for s in range(3)]
    for b in range(ex):
        block = order_ref[b]
        low = jnp.zeros_like(early[0])
        for source, slot in zip(sources, early):
            low = low + jnp.where(source == block, slot, 0.0)
        high = jnp.zeros_like(slots[0])
        for source, slot in zip(sources[:2] + sources[3:], slots):
            high = high + jnp.where(source == block, slot, 0.0)
        at = b * (EARLY + late)
        out_ref[at : at + EARLY, :] = low
        out_ref[at + EARLY : at + EARLY + late, :] = high


def slot_sources(me):
    low_pair = me < 2
    near = jnp.where(low_pair, 1 - me, 5 - me)
    return [me, near, jnp.where(low_pair, 2, 1), jnp.where(low_pair, 3, 0)]


def far_pass_kernel(ex, early_ref, mid_ref, far_out, grad_ref, order_ref, out_ref):
    out_ref[...] = inner_products((early_ref, mid_ref, far_out), grad_ref, 0, far_out.shape[0])


def last_pass_kernel(
    ex, base_ref, far_ref, early_ref, mid_ref, far_out, grad_ref, order_ref, mine_ref, send_ref, full_ref
):
    late = far_out.shape[1]
    rows = far_out.shape[0]
    acc = far_ref[...] + inner_products((early_ref, mid_ref, far_out), grad_ref, rows, rows)
    mid, far = slot_sources(lax.axis_index("ex"))[2:]
    low_mid, low_far = acc[:EARLY], acc[EARLY : 2 * EARLY]
    high_mid, high_far = acc[2 * EARLY : 2 * EARLY + late], acc[2 * EARLY + late :]
    full_ref[...] = base_ref[...]
    for b in range(ex):
        mid_hit, far_hit = order_ref[b] == mid, order_ref[b] == far
        low = jnp.where(mid_hit, low_mid, 0.0) + jnp.where(far_hit, low_far, 0.0)
        high = jnp.where(mid_hit, high_mid, 0.0) + jnp.where(far_hit, high_far, 0.0)
        at = b * (EARLY + late)
        full_ref[at : at + EARLY, :] = full_ref[at : at + EARLY, :] + low
        at = at + EARLY
        full_ref[at : at + late, :] = full_ref[at : at + late, :] + high
    half = mine_ref.shape[0]
    side = lax.axis_index("feat")
    mine_ref[...] = full_ref[pl.ds(pl.multiple_of(side * half, half), half), :]
    send_ref[...] = full_ref[pl.ds(pl.multiple_of((1 - side) * half, half), half), :]


def score_call(kernel, ex, arrays, order, out_shape, scratch=()):
    return pl.pallas_call(
        functools.partial(kernel, ex),
        out_shape=out_shape,
        in_specs=[VMEM] * len(arrays) + [SMEM],
        out_specs=jax.tree.map(lambda _: VMEM, out_shape),
        scratch_shapes=scratch,
        compiler_params=pltpu.CompilerParams(vmem_limit_bytes=40 << 20),
        cost_estimate=pl.CostEstimate(flops=1000, bytes_accessed=1000, transcendentals=0),
    )(*arrays, order)


def after(x, *others):
    return lax.optimization_barrier((x, *others))[0]


PAIRS = [(0, 1), (1, 0), (2, 3), (3, 2)]
MIDDLE = [(1, 2), (2, 1)]
OUTWARD = [(1, 0), (2, 3)]


def per_device_line(train_grads, queries, left_factor, right_factor, block_order):
    ex = lax.axis_size("ex")
    swap = [(0, 1), (1, 0)]
    count = queries.shape[1]
    n = train_grads.shape[0]
    late_raw = queries[0, EARLY:]
    late_other = lax.ppermute(late_raw, "feat", swap)
    raw = after(queries, late_raw)[0, :EARLY]
    terms = factor_terms(left_factor, after(right_factor, raw), train_grads.shape[1])
    raw_near = lax.ppermute(raw, "ex", PAIRS)
    raw_mid = lax.ppermute(raw, "ex", MIDDLE)
    raw_mid_out = lax.ppermute(after(raw_mid, *terms), "ex", OUTWARD)
    early_0 = jnp.concatenate([raw, raw_near], axis=0)
    raw_far_mid = lax.ppermute(after(raw_near, early_0, late_other), "ex", MIDDLE)

    late = condition(after(late_raw, raw_near, raw_mid, early_0), late_other, *terms)
    near = lax.ppermute(late, "ex", PAIRS)
    mid = lax.ppermute(late, "ex", MIDDLE)
    grads = regroup(after(train_grads, late, raw_mid_out))
    early_0_other = lax.ppermute(after(early_0, late, raw_far_mid, raw_mid_out), "feat", swap)
    raw_far_out = lax.ppermute(after(raw_far_mid, grads), "ex", OUTWARD)
    far_mid = lax.ppermute(after(near, grads), "ex", MIDDLE)
    mid_out = lax.ppermute(after(mid, near, grads), "ex", OUTWARD)
    cond_0 = condition(after(early_0, near, mid), early_0_other, *terms)
    early_1 = jnp.concatenate([raw_mid + raw_mid_out, after(raw_far_mid, near, mid) + raw_far_out], axis=0)
    early_1_other = lax.ppermute(after(early_1, cond_0), "feat", swap)
    part = far_mid.shape[0] // 2
    far_out_0 = lax.ppermute(far_mid[:part], "ex", OUTWARD)
    far_out_1 = lax.ppermute(far_mid[part:], "ex", OUTWARD)
    cond_1 = condition(after(early_1, far_mid), early_1_other, *terms)

    base = score_call(
        first_pass_kernel, ex, (cond_0, late, near, far_mid, grads), block_order,
        jax.ShapeDtypeStruct((ex * count, n), F32),
    )
    mid = mid + mid_out
    far_0 = score_call(
        far_pass_kernel, ex, (cond_1, mid, far_out_0, after(grads, base)), block_order,
        jax.ShapeDtypeStruct((2 * count, n), F32),
    )
    half = jax.ShapeDtypeStruct((ex * count // 2, n), F32)
    mine, send = score_call(
        last_pass_kernel, ex, (base, far_0, cond_1, mid, far_out_1, grads), block_order, (half, half),
        [pltpu.VMEM((ex * count, n), F32)],
    )
    scores = mine + lax.ppermute(send, "feat", swap)
    return scores.T[:, None, :]


def per_device_gather(train_grads, queries, left_factor, right_factor, block_order):
    row_count = train_grads.shape[0]
    part_rows = train_grads.shape[1]
    right_width = train_grads.shape[2]
    flat_grads = train_grads.reshape(row_count, part_rows * right_width)
    local_queries = queries[0]
    block_size = local_queries.shape[0]
    regrouped = lax.all_to_all(local_queries, "feat", split_axis=0, concat_axis=1, tiled=True)
    whole_mix = jnp.einsum(
        "ik,qkj->qij", left_factor, regrouped.astype(F32), precision=lax.Precision.HIGHEST
    )
    whole_cond = jnp.einsum(
        "qij,jl->qil", whole_mix, right_factor, precision=lax.Precision.HIGHEST
    ).astype(BF16)
    conditioned = lax.all_to_all(whole_cond, "feat", split_axis=1, concat_axis=0, tiled=True)
    conditioned = conditioned.reshape(block_size, part_rows * right_width)
    partials = lax.dot_general(
        flat_grads,
        lax.all_gather(conditioned, "ex", axis=0, tiled=True),
        (((1,), (1,)), ((), ())),
        preferred_element_type=F32,
    )
    block_count = lax.axis_size("ex")
    partials = jnp.take(partials.reshape(row_count, block_count, block_size), block_order, axis=1)
    partials = partials.reshape(row_count, block_count * block_size)
    owned_scores = lax.psum_scatter(partials, "feat", scatter_dimension=1, tiled=True)
    return owned_scores.reshape(row_count, 1, owned_scores.shape[1])


def solution(mesh):
    short_line = mesh.shape["ex"] == 4 and mesh.shape["feat"] == 2
    return jax.shard_map(
        per_device_line if short_line else per_device_gather,
        mesh=mesh,
        in_specs=(
            P(("grp", "ex"), "feat", None),
            P("pb", ("grp", "ex"), "feat", None),
            P("grp", None),
            P("grp", None),
            P("grp"),
        ),
        out_specs=P(("grp", "ex"), "pb", "feat"),
        check_vma=False,
    )
```

```python
import functools

import jax
import jax.numpy as jnp
from jax import lax
from jax.experimental import pallas as pl
from jax.experimental.pallas import tpu as pltpu
from jax.sharding import PartitionSpec as P

F32 = jnp.float32
BF16 = jnp.bfloat16
EARLY = 4
TILE = 16
EXAMPLES = 32
DEEP = 32
VMEM = pl.BlockSpec(memory_space=pltpu.VMEM)
SMEM = pl.BlockSpec(memory_space=pltpu.SMEM)


def parts_of(x, count):
    terms = []
    for _ in range(count):
        top = x.astype(BF16)
        terms.append(top)
        x = x - top.astype(F32)
    return terms


def factor_kernel(left_ref, right_ref, left_out, right_out):
    rows = left_out.shape[0] // 3
    side = lax.axis_index("feat")
    here = pl.ds(pl.multiple_of(side * rows, rows), rows)
    there = pl.ds(pl.multiple_of((1 - side) * rows, rows), rows)
    left = jnp.concatenate([left_ref[here, here], left_ref[here, there]], axis=1)
    left_out[...] = jnp.concatenate(parts_of(left, 3), axis=0)
    right_out[...] = jnp.concatenate(parts_of(right_ref[...], 2), axis=0)


def factor_terms(left, right, rows):
    wide, width = left.shape[1], right.shape[1]
    return pl.pallas_call(
        factor_kernel,
        out_shape=(
            jax.ShapeDtypeStruct((3 * rows, wide), BF16),
            jax.ShapeDtypeStruct((2 * width, width), BF16),
        ),
        in_specs=[VMEM] * 2,
        out_specs=(VMEM, VMEM),
        compiler_params=pltpu.CompilerParams(vmem_limit_bytes=16 << 20),
    )(left, right)


def condition_kernel(own_ref, far_ref, left_ref, right_ref, out_ref, wide_ref):
    count, rows, width = own_ref.shape
    left_terms = left_ref[...]
    right_0, right_1 = right_ref[:width], right_ref[width:]
    for q in range(count):
        query = jnp.concatenate([own_ref[q], far_ref[q]], axis=0)
        mixed = jnp.dot(left_terms, query, preferred_element_type=F32)
        mixed = mixed[:rows] + (mixed[rows : 2 * rows] + mixed[2 * rows :])
        mixed_0, mixed_1 = parts_of(mixed, 2)
        both = jnp.dot(jnp.concatenate([mixed_0, mixed_1], axis=0), right_0, preferred_element_type=F32)
        cross = jnp.dot(mixed_0, right_1, preferred_element_type=F32)
        wide_ref[:, q, :] = both[:rows] + (both[rows:] + cross)
    out_ref[...] = wide_ref[...].astype(BF16)


def condition(own, far, left_terms, right_terms):
    count, rows, width = own.shape
    return pl.pallas_call(
        condition_kernel,
        out_shape=jax.ShapeDtypeStruct((rows, count, width), BF16),
        in_specs=[VMEM] * 4,
        out_specs=VMEM,
        scratch_shapes=[pltpu.VMEM((rows, count, width), F32)],
        compiler_params=pltpu.CompilerParams(vmem_limit_bytes=24 << 20),
        cost_estimate=pl.CostEstimate(flops=count * 3_000_000 * 40, bytes_accessed=8 * count * rows * width, transcendentals=0),
    )(own, far, left_terms, right_terms)


def regroup_kernel(grads_ref, out_ref, held_ref, sems):
    examples, rows, width = held_ref.shape
    blocks = examples // EXAMPLES
    copies = []
    for b in range(blocks):
        part = pl.ds(b * EXAMPLES, EXAMPLES)
        copies.append(pltpu.make_async_copy(grads_ref.at[part], held_ref.at[part], sems.at[b]))
        copies[-1].start()
    i = lax.broadcasted_iota(jnp.int32, (TILE * TILE, TILE * TILE), 0)
    j = lax.broadcasted_iota(jnp.int32, (TILE * TILE, TILE * TILE), 1)
    swap = jnp.where((i // TILE == j % TILE) & (i % TILE == j // TILE), 1.0, 0.0).astype(BF16)
    for b in range(blocks):
        copies[b].wait()

        @pl.loop(b * EXAMPLES // TILE, (b + 1) * EXAMPLES // TILE)
        def _(step):
            n = pl.ds(pl.multiple_of(step * TILE, TILE), TILE)
            for r in range(0, rows, TILE):
                tile = held_ref[n, r : r + TILE, :].reshape(TILE * TILE, width)
                turned = jnp.dot(swap, tile, preferred_element_type=F32).astype(BF16)
                out_ref[r : r + TILE, n, :] = turned.reshape(TILE, TILE, width)


def regroup(grads):
    n, rows, width = grads.shape
    return pl.pallas_call(
        regroup_kernel,
        out_shape=jax.ShapeDtypeStruct((rows, n, width), BF16),
        in_specs=[pl.BlockSpec(memory_space=pltpu.HBM)],
        out_specs=VMEM,
        scratch_shapes=[pltpu.VMEM((n, rows, width), BF16), pltpu.SemaphoreType.DMA((n // EXAMPLES,))],
        compiler_params=pltpu.CompilerParams(vmem_limit_bytes=44 << 20),
        cost_estimate=pl.CostEstimate(flops=6_000_000_000, bytes_accessed=16_000_000, transcendentals=0),
    )(grads)


def inner_products(query_refs, grad_ref, first=0, rows=None):
    total = sum(ref.shape[1] for ref in query_refs)
    rows = rows or grad_ref.shape[0]
    starts = [0 if ref.shape[0] == rows else first for ref in query_refs]

    def body(i, acc):
        at = [i * DEEP + j for j in range(DEEP)]
        queries = [
            jnp.concatenate([ref[start + r] for ref, start in zip(query_refs, starts)], axis=0) for r in at
        ]
        return acc + lax.dot_general(
            jnp.concatenate(queries, axis=1),
            jnp.concatenate([grad_ref[first + r] for r in at], axis=1),
            (((1,), (1,)), ((), ())),
            preferred_element_type=F32,
        )

    start = jnp.zeros((total, grad_ref.shape[1]), F32)
    return lax.fori_loop(0, rows // DEEP, body, start)


def first_pass_kernel(ex, early_ref, own_ref, near, far_in, grad_ref, order_ref, out_ref):
    late = own_ref.shape[1]
    acc = inner_products((early_ref, own_ref, near, far_in), grad_ref)
    sources = slot_sources(lax.axis_index("ex"))
    early = [acc[EARLY * s : EARLY * (s + 1)] for s in range(2)]
    base = early_ref.shape[1]
    slots = [acc[base + late * s : base + late * (s + 1)] for s in range(3)]
    for b in range(ex):
        block = order_ref[b]
        low = jnp.zeros_like(early[0])
        for source, slot in zip(sources, early):
            low = low + jnp.where(source == block, slot, 0.0)
        high = jnp.zeros_like(slots[0])
        for source, slot in zip(sources[:2] + sources[3:], slots):
            high = high + jnp.where(source == block, slot, 0.0)
        at = b * (EARLY + late)
        out_ref[at : at + EARLY, :] = low
        out_ref[at + EARLY : at + EARLY + late, :] = high


def slot_sources(me):
    low_pair = me < 2
    near = jnp.where(low_pair, 1 - me, 5 - me)
    return [me, near, jnp.where(low_pair, 2, 1), jnp.where(low_pair, 3, 0)]


def far_pass_kernel(ex, early_ref, mid_ref, far_out, grad_ref, order_ref, out_ref):
    out_ref[...] = inner_products((early_ref, mid_ref, far_out), grad_ref, 0, far_out.shape[0])


def last_pass_kernel(
    ex, base_ref, far_ref, early_ref, mid_ref, far_out, grad_ref, order_ref, mine_ref, send_ref, full_ref
):
    late = far_out.shape[1]
    rows = far_out.shape[0]
    acc = far_ref[...] + inner_products((early_ref, mid_ref, far_out), grad_ref, rows, rows)
    mid, far = slot_sources(lax.axis_index("ex"))[2:]
    low_mid, low_far = acc[:EARLY], acc[EARLY : 2 * EARLY]
    high_mid, high_far = acc[2 * EARLY : 2 * EARLY + late], acc[2 * EARLY + late :]
    full_ref[...] = base_ref[...]
    for b in range(ex):
        mid_hit, far_hit = order_ref[b] == mid, order_ref[b] == far
        low = jnp.where(mid_hit, low_mid, 0.0) + jnp.where(far_hit, low_far, 0.0)
        high = jnp.where(mid_hit, high_mid, 0.0) + jnp.where(far_hit, high_far, 0.0)
        at = b * (EARLY + late)
        full_ref[at : at + EARLY, :] = full_ref[at : at + EARLY, :] + low
        at = at + EARLY
        full_ref[at : at + late, :] = full_ref[at : at + late, :] + high
    half = mine_ref.shape[0]
    side = lax.axis_index("feat")
    mine_ref[...] = full_ref[pl.ds(pl.multiple_of(side * half, half), half), :]
    send_ref[...] = full_ref[pl.ds(pl.multiple_of((1 - side) * half, half), half), :]


def score_call(kernel, ex, arrays, order, out_shape, scratch=()):
    return pl.pallas_call(
        functools.partial(kernel, ex),
        out_shape=out_shape,
        in_specs=[VMEM] * len(arrays) + [SMEM],
        out_specs=jax.tree.map(lambda _: VMEM, out_shape),
        scratch_shapes=scratch,
        compiler_params=pltpu.CompilerParams(vmem_limit_bytes=40 << 20),
        cost_estimate=pl.CostEstimate(flops=1000, bytes_accessed=1000, transcendentals=0),
    )(*arrays, order)


def after(x, *others):
    return lax.optimization_barrier((x, *others))[0]


PAIRS = [(0, 1), (1, 0), (2, 3), (3, 2)]
MIDDLE = [(1, 2), (2, 1)]
OUTWARD = [(1, 0), (2, 3)]


def per_device_line(train_grads, queries, left_factor, right_factor, block_order):
    ex = lax.axis_size("ex")
    swap = [(0, 1), (1, 0)]
    count = queries.shape[1]
    n = train_grads.shape[0]
    late_raw = queries[0, EARLY:]
    late_other = lax.ppermute(late_raw, "feat", swap)
    raw = after(queries, late_raw)[0, :EARLY]
    terms = factor_terms(left_factor, after(right_factor, raw), train_grads.shape[1])
    raw_near = lax.ppermute(raw, "ex", PAIRS)
    raw_mid = lax.ppermute(raw, "ex", MIDDLE)
    raw_mid_out = lax.ppermute(after(raw_mid, *terms), "ex", OUTWARD)
    early_0 = jnp.concatenate([raw, raw_near], axis=0)
    raw_far_mid = lax.ppermute(after(raw_near, early_0, late_other), "ex", MIDDLE)

    late = condition(after(late_raw, raw_near, raw_mid, early_0), late_other, *terms)
    near = lax.ppermute(late, "ex", PAIRS)
    mid = lax.ppermute(late, "ex", MIDDLE)
    grads = regroup(after(train_grads, late, raw_mid_out, raw_far_mid))
    early_0_other = lax.ppermute(after(early_0, late, raw_mid_out), "feat", swap)
    raw_far_out = lax.ppermute(after(raw_far_mid, grads), "ex", OUTWARD)
    far_mid = lax.ppermute(after(near, grads), "ex", MIDDLE)
    mid_out = lax.ppermute(after(mid, near, grads), "ex", OUTWARD)
    cond_0 = condition(after(early_0, near, mid), early_0_other, *terms)
    early_1 = jnp.concatenate([raw_mid + raw_mid_out, after(raw_far_mid, near, mid) + raw_far_out], axis=0)
    early_1_other = lax.ppermute(after(early_1, cond_0), "feat", swap)
    part = far_mid.shape[0] // 2
    far_out_0 = lax.ppermute(far_mid[:part], "ex", OUTWARD)
    far_out_1 = lax.ppermute(far_mid[part:], "ex", OUTWARD)
    cond_1 = condition(after(early_1, far_mid, mid_out), early_1_other, *terms)

    base = score_call(
        first_pass_kernel, ex, (cond_0, late, near, far_mid, grads), block_order,
        jax.ShapeDtypeStruct((ex * count, n), F32),
    )
    mid = mid + mid_out
    far_0 = score_call(
        far_pass_kernel, ex, (cond_1, mid, far_out_0, after(grads, base)), block_order,
        jax.ShapeDtypeStruct((2 * count, n), F32),
    )
    half = jax.ShapeDtypeStruct((ex * count // 2, n), F32)
    mine, send = score_call(
        last_pass_kernel, ex, (base, far_0, cond_1, mid, far_out_1, grads), block_order, (half, half),
        [pltpu.VMEM((ex * count, n), F32)],
    )
    scores = mine + lax.ppermute(send, "feat", swap)
    return scores.T[:, None, :]


def per_device_gather(train_grads, queries, left_factor, right_factor, block_order):
    row_count = train_grads.shape[0]
    part_rows = train_grads.shape[1]
    right_width = train_grads.shape[2]
    flat_grads = train_grads.reshape(row_count, part_rows * right_width)
    local_queries = queries[0]
    block_size = local_queries.shape[0]
    regrouped = lax.all_to_all(local_queries, "feat", split_axis=0, concat_axis=1, tiled=True)
    whole_mix = jnp.einsum(
        "ik,qkj->qij", left_factor, regrouped.astype(F32), precision=lax.Precision.HIGHEST
    )
    whole_cond = jnp.einsum(
        "qij,jl->qil", whole_mix, right_factor, precision=lax.Precision.HIGHEST
    ).astype(BF16)
    conditioned = lax.all_to_all(whole_cond, "feat", split_axis=1, concat_axis=0, tiled=True)
    conditioned = conditioned.reshape(block_size, part_rows * right_width)
    partials = lax.dot_general(
        flat_grads,
        lax.all_gather(conditioned, "ex", axis=0, tiled=True),
        (((1,), (1,)), ((), ())),
        preferred_element_type=F32,
    )
    block_count = lax.axis_size("ex")
    partials = jnp.take(partials.reshape(row_count, block_count, block_size), block_order, axis=1)
    partials = partials.reshape(row_count, block_count * block_size)
    owned_scores = lax.psum_scatter(partials, "feat", scatter_dimension=1, tiled=True)
    return owned_scores.reshape(row_count, 1, owned_scores.shape[1])


def solution(mesh):
    short_line = mesh.shape["ex"] == 4 and mesh.shape["feat"] == 2
    return jax.shard_map(
        per_device_line if short_line else per_device_gather,
        mesh=mesh,
        in_specs=(
            P(("grp", "ex"), "feat", None),
            P("pb", ("grp", "ex"), "feat", None),
            P("grp", None),
            P("grp", None),
            P("grp"),
        ),
        out_specs=P(("grp", "ex"), "pb", "feat"),
        check_vma=False,
    )
```

```python
import functools

import jax
import jax.numpy as jnp
from jax import lax
from jax.experimental import pallas as pl
from jax.experimental.pallas import tpu as pltpu
from jax.sharding import PartitionSpec as P

F32 = jnp.float32
BF16 = jnp.bfloat16
EARLY = 4
TILE = 16
EXAMPLES = 32
DEEP = 32
VMEM = pl.BlockSpec(memory_space=pltpu.VMEM)
SMEM = pl.BlockSpec(memory_space=pltpu.SMEM)


def parts_of(x, count):
    terms = []
    for _ in range(count):
        top = x.astype(BF16)
        terms.append(top)
        x = x - top.astype(F32)
    return terms


def factor_kernel(left_ref, right_ref, left_out, right_out):
    rows = left_out.shape[0] // 3
    side = lax.axis_index("feat")
    here = pl.ds(pl.multiple_of(side * rows, rows), rows)
    there = pl.ds(pl.multiple_of((1 - side) * rows, rows), rows)
    left = jnp.concatenate([left_ref[here, here], left_ref[here, there]], axis=1)
    left_out[...] = jnp.concatenate(parts_of(left, 3), axis=0)
    right_out[...] = jnp.concatenate(parts_of(right_ref[...], 2), axis=0)


def factor_terms(left, right, rows):
    wide, width = left.shape[1], right.shape[1]
    return pl.pallas_call(
        factor_kernel,
        out_shape=(
            jax.ShapeDtypeStruct((3 * rows, wide), BF16),
            jax.ShapeDtypeStruct((2 * width, width), BF16),
        ),
        in_specs=[VMEM] * 2,
        out_specs=(VMEM, VMEM),
        compiler_params=pltpu.CompilerParams(vmem_limit_bytes=16 << 20),
    )(left, right)


def condition_kernel(own_ref, far_ref, left_ref, right_ref, out_ref, wide_ref):
    count, rows, width = own_ref.shape
    left_terms = left_ref[...]
    right_0, right_1 = right_ref[:width], right_ref[width:]
    for q in range(count):
        query = jnp.concatenate([own_ref[q], far_ref[q]], axis=0)
        mixed = jnp.dot(left_terms, query, preferred_element_type=F32)
        mixed = mixed[:rows] + (mixed[rows : 2 * rows] + mixed[2 * rows :])
        mixed_0, mixed_1 = parts_of(mixed, 2)
        both = jnp.dot(jnp.concatenate([mixed_0, mixed_1], axis=0), right_0, preferred_element_type=F32)
        cross = jnp.dot(mixed_0, right_1, preferred_element_type=F32)
        wide_ref[:, q, :] = both[:rows] + (both[rows:] + cross)
    out_ref[...] = wide_ref[...].astype(BF16)


def condition(own, far, left_terms, right_terms):
    count, rows, width = own.shape
    return pl.pallas_call(
        condition_kernel,
        out_shape=jax.ShapeDtypeStruct((rows, count, width), BF16),
        in_specs=[VMEM] * 4,
        out_specs=VMEM,
        scratch_shapes=[pltpu.VMEM((rows, count, width), F32)],
        compiler_params=pltpu.CompilerParams(vmem_limit_bytes=24 << 20),
        cost_estimate=pl.CostEstimate(flops=count * 3_000_000 * 40, bytes_accessed=8 * count * rows * width, transcendentals=0),
    )(own, far, left_terms, right_terms)


def regroup_kernel(grads_ref, out_ref, held_ref, sems):
    examples, rows, width = held_ref.shape
    blocks = examples // EXAMPLES
    copies = []
    for b in range(blocks):
        part = pl.ds(b * EXAMPLES, EXAMPLES)
        copies.append(pltpu.make_async_copy(grads_ref.at[part], held_ref.at[part], sems.at[b]))
        copies[-1].start()
    i = lax.broadcasted_iota(jnp.int32, (TILE * TILE, TILE * TILE), 0)
    j = lax.broadcasted_iota(jnp.int32, (TILE * TILE, TILE * TILE), 1)
    swap = jnp.where((i // TILE == j % TILE) & (i % TILE == j // TILE), 1.0, 0.0).astype(BF16)
    for b in range(blocks):
        copies[b].wait()

        @pl.loop(b * EXAMPLES // TILE, (b + 1) * EXAMPLES // TILE)
        def _(step):
            n = pl.ds(pl.multiple_of(step * TILE, TILE), TILE)
            for r in range(0, rows, TILE):
                tile = held_ref[n, r : r + TILE, :].reshape(TILE * TILE, width)
                turned = jnp.dot(swap, tile, preferred_element_type=F32).astype(BF16)
                out_ref[r : r + TILE, n, :] = turned.reshape(TILE, TILE, width)


def regroup(grads):
    n, rows, width = grads.shape
    return pl.pallas_call(
        regroup_kernel,
        out_shape=jax.ShapeDtypeStruct((rows, n, width), BF16),
        in_specs=[pl.BlockSpec(memory_space=pltpu.HBM)],
        out_specs=VMEM,
        scratch_shapes=[pltpu.VMEM((n, rows, width), BF16), pltpu.SemaphoreType.DMA((n // EXAMPLES,))],
        compiler_params=pltpu.CompilerParams(vmem_limit_bytes=44 << 20),
        cost_estimate=pl.CostEstimate(flops=6_000_000_000, bytes_accessed=16_000_000, transcendentals=0),
    )(grads)


def inner_products(query_refs, grad_ref, first=0, rows=None):
    total = sum(ref.shape[1] for ref in query_refs)
    rows = rows or grad_ref.shape[0]
    starts = [0 if ref.shape[0] == rows else first for ref in query_refs]

    def body(i, acc):
        at = [i * DEEP + j for j in range(DEEP)]
        queries = [
            jnp.concatenate([ref[start + r] for ref, start in zip(query_refs, starts)], axis=0) for r in at
        ]
        return acc + lax.dot_general(
            jnp.concatenate(queries, axis=1),
            jnp.concatenate([grad_ref[first + r] for r in at], axis=1),
            (((1,), (1,)), ((), ())),
            preferred_element_type=F32,
        )

    start = jnp.zeros((total, grad_ref.shape[1]), F32)
    return lax.fori_loop(0, rows // DEEP, body, start)


def first_pass_kernel(ex, early_ref, own_ref, near, far_in, grad_ref, order_ref, out_ref):
    late = own_ref.shape[1]
    acc = inner_products((early_ref, own_ref, near, far_in), grad_ref)
    sources = slot_sources(lax.axis_index("ex"))
    early = [acc[EARLY * s : EARLY * (s + 1)] for s in range(2)]
    base = early_ref.shape[1]
    slots = [acc[base + late * s : base + late * (s + 1)] for s in range(3)]
    for b in range(ex):
        block = order_ref[b]
        low = jnp.zeros_like(early[0])
        for source, slot in zip(sources, early):
            low = low + jnp.where(source == block, slot, 0.0)
        high = jnp.zeros_like(slots[0])
        for source, slot in zip(sources[:2] + sources[3:], slots):
            high = high + jnp.where(source == block, slot, 0.0)
        at = b * (EARLY + late)
        out_ref[at : at + EARLY, :] = low
        out_ref[at + EARLY : at + EARLY + late, :] = high


def slot_sources(me):
    low_pair = me < 2
    near = jnp.where(low_pair, 1 - me, 5 - me)
    return [me, near, jnp.where(low_pair, 2, 1), jnp.where(low_pair, 3, 0)]


def far_pass_kernel(first, ex, early_ref, mid_ref, far_out, grad_ref, order_ref, out_ref):
    out_ref[...] = inner_products((early_ref, mid_ref, far_out), grad_ref, first, far_out.shape[0])


def last_pass_kernel(
    ex, base_ref, far_0, far_1, early_ref, mid_ref, far_out, grad_ref, order_ref, mine_ref, send_ref, full_ref
):
    late = far_out.shape[1]
    rows = far_out.shape[0]
    first = grad_ref.shape[0] - rows
    acc = far_0[...] + far_1[...] + inner_products((early_ref, mid_ref, far_out), grad_ref, first, rows)
    mid, far = slot_sources(lax.axis_index("ex"))[2:]
    low_mid, low_far = acc[:EARLY], acc[EARLY : 2 * EARLY]
    high_mid, high_far = acc[2 * EARLY : 2 * EARLY + late], acc[2 * EARLY + late :]
    full_ref[...] = base_ref[...]
    for b in range(ex):
        mid_hit, far_hit = order_ref[b] == mid, order_ref[b] == far
        low = jnp.where(mid_hit, low_mid, 0.0) + jnp.where(far_hit, low_far, 0.0)
        high = jnp.where(mid_hit, high_mid, 0.0) + jnp.where(far_hit, high_far, 0.0)
        at = b * (EARLY + late)
        full_ref[at : at + EARLY, :] = full_ref[at : at + EARLY, :] + low
        at = at + EARLY
        full_ref[at : at + late, :] = full_ref[at : at + late, :] + high
    half = mine_ref.shape[0]
    side = lax.axis_index("feat")
    mine_ref[...] = full_ref[pl.ds(pl.multiple_of(side * half, half), half), :]
    send_ref[...] = full_ref[pl.ds(pl.multiple_of((1 - side) * half, half), half), :]


def score_call(kernel, ex, arrays, order, out_shape, scratch=()):
    return pl.pallas_call(
        functools.partial(kernel, ex),
        out_shape=out_shape,
        in_specs=[VMEM] * len(arrays) + [SMEM],
        out_specs=jax.tree.map(lambda _: VMEM, out_shape),
        scratch_shapes=scratch,
        compiler_params=pltpu.CompilerParams(vmem_limit_bytes=40 << 20),
        cost_estimate=pl.CostEstimate(flops=1000, bytes_accessed=1000, transcendentals=0),
    )(*arrays, order)


def after(x, *others):
    return lax.optimization_barrier((x, *others))[0]


PAIRS = [(0, 1), (1, 0), (2, 3), (3, 2)]
MIDDLE = [(1, 2), (2, 1)]
OUTWARD = [(1, 0), (2, 3)]


def per_device_line(train_grads, queries, left_factor, right_factor, block_order):
    ex = lax.axis_size("ex")
    swap = [(0, 1), (1, 0)]
    count = queries.shape[1]
    n = train_grads.shape[0]
    late_raw = queries[0, EARLY:]
    late_other = lax.ppermute(late_raw, "feat", swap)
    raw = after(queries, late_raw)[0, :EARLY]
    terms = factor_terms(left_factor, after(right_factor, raw), train_grads.shape[1])
    raw_near = lax.ppermute(raw, "ex", PAIRS)
    raw_mid = lax.ppermute(raw, "ex", MIDDLE)
    raw_mid_out = lax.ppermute(after(raw_mid, *terms), "ex", OUTWARD)
    early_0 = jnp.concatenate([raw, raw_near], axis=0)
    raw_far_mid = lax.ppermute(after(raw_near, early_0, late_other), "ex", MIDDLE)

    late = condition(after(late_raw, raw_near, raw_mid, early_0), late_other, *terms)
    near = lax.ppermute(late, "ex", PAIRS)
    mid = lax.ppermute(late, "ex", MIDDLE)
    grads = regroup(after(train_grads, late, raw_mid_out, raw_far_mid))
    early_0_other = lax.ppermute(after(early_0, late, raw_mid_out), "feat", swap)
    raw_far_out = lax.ppermute(after(raw_far_mid, grads), "ex", OUTWARD)
    far_mid = lax.ppermute(after(near, grads), "ex", MIDDLE)
    mid_out = lax.ppermute(after(mid, near, grads), "ex", OUTWARD)
    cond_0 = condition(after(early_0, near, mid), early_0_other, *terms)
    early_1 = jnp.concatenate([raw_mid + raw_mid_out, after(raw_far_mid, near, mid) + raw_far_out], axis=0)
    early_1_other = lax.ppermute(after(early_1, cond_0), "feat", swap)
    rows = far_mid.shape[0]
    cuts = [0, rows // 2, 3 * rows // 4, rows]
    far_out = [lax.ppermute(far_mid[a:b], "ex", OUTWARD) for a, b in zip(cuts, cuts[1:])]
    cond_1 = condition(after(early_1, far_mid, mid_out), early_1_other, *terms)

    base = score_call(
        first_pass_kernel, ex, (cond_0, late, near, far_mid, grads), block_order,
        jax.ShapeDtypeStruct((ex * count, n), F32),
    )
    mid = mid + mid_out
    far_sums, earlier = [], base
    for first, arrived in zip(cuts, far_out[:-1]):
        earlier = score_call(
            functools.partial(far_pass_kernel, first), ex, (cond_1, mid, arrived, after(grads, earlier)), block_order,
            jax.ShapeDtypeStruct((2 * count, n), F32),
        )
        far_sums.append(earlier)
    half = jax.ShapeDtypeStruct((ex * count // 2, n), F32)
    mine, send = score_call(
        last_pass_kernel, ex, (base, *far_sums, cond_1, mid, far_out[-1], grads), block_order, (half, half),
        [pltpu.VMEM((ex * count, n), F32)],
    )
    scores = mine + lax.ppermute(send, "feat", swap)
    return scores.T[:, None, :]


def per_device_gather(train_grads, queries, left_factor, right_factor, block_order):
    row_count = train_grads.shape[0]
    part_rows = train_grads.shape[1]
    right_width = train_grads.shape[2]
    flat_grads = train_grads.reshape(row_count, part_rows * right_width)
    local_queries = queries[0]
    block_size = local_queries.shape[0]
    regrouped = lax.all_to_all(local_queries, "feat", split_axis=0, concat_axis=1, tiled=True)
    whole_mix = jnp.einsum(
        "ik,qkj->qij", left_factor, regrouped.astype(F32), precision=lax.Precision.HIGHEST
    )
    whole_cond = jnp.einsum(
        "qij,jl->qil", whole_mix, right_factor, precision=lax.Precision.HIGHEST
    ).astype(BF16)
    conditioned = lax.all_to_all(whole_cond, "feat", split_axis=1, concat_axis=0, tiled=True)
    conditioned = conditioned.reshape(block_size, part_rows * right_width)
    partials = lax.dot_general(
        flat_grads,
        lax.all_gather(conditioned, "ex", axis=0, tiled=True),
        (((1,), (1,)), ((), ())),
        preferred_element_type=F32,
    )
    block_count = lax.axis_size("ex")
    partials = jnp.take(partials.reshape(row_count, block_count, block_size), block_order, axis=1)
    partials = partials.reshape(row_count, block_count * block_size)
    owned_scores = lax.psum_scatter(partials, "feat", scatter_dimension=1, tiled=True)
    return owned_scores.reshape(row_count, 1, owned_scores.shape[1])


def solution(mesh):
    short_line = mesh.shape["ex"] == 4 and mesh.shape["feat"] == 2
    return jax.shard_map(
        per_device_line if short_line else per_device_gather,
        mesh=mesh,
        in_specs=(
            P(("grp", "ex"), "feat", None),
            P("pb", ("grp", "ex"), "feat", None),
            P("grp", None),
            P("grp", None),
            P("grp"),
        ),
        out_specs=P(("grp", "ex"), "pb", "feat"),
        check_vma=False,
    )
```

```python
import functools

import jax
import jax.numpy as jnp
from jax import lax
from jax.experimental import pallas as pl
from jax.experimental.pallas import tpu as pltpu
from jax.sharding import PartitionSpec as P

F32 = jnp.float32
BF16 = jnp.bfloat16
EARLY = 4
TILE = 16
EXAMPLES = 32
DEEP = 32
VMEM = pl.BlockSpec(memory_space=pltpu.VMEM)
SMEM = pl.BlockSpec(memory_space=pltpu.SMEM)


def parts_of(x, count):
    terms = []
    for _ in range(count):
        top = x.astype(BF16)
        terms.append(top)
        x = x - top.astype(F32)
    return terms


def factor_kernel(left_ref, right_ref, left_out, right_out):
    rows = left_out.shape[0] // 3
    side = lax.axis_index("feat")
    here = pl.ds(pl.multiple_of(side * rows, rows), rows)
    there = pl.ds(pl.multiple_of((1 - side) * rows, rows), rows)
    left = jnp.concatenate([left_ref[here, here], left_ref[here, there]], axis=1)
    left_out[...] = jnp.concatenate(parts_of(left, 3), axis=0)
    right_out[...] = jnp.concatenate(parts_of(right_ref[...], 2), axis=0)


def factor_terms(left, right, rows):
    wide, width = left.shape[1], right.shape[1]
    return pl.pallas_call(
        factor_kernel,
        out_shape=(
            jax.ShapeDtypeStruct((3 * rows, wide), BF16),
            jax.ShapeDtypeStruct((2 * width, width), BF16),
        ),
        in_specs=[VMEM] * 2,
        out_specs=(VMEM, VMEM),
        compiler_params=pltpu.CompilerParams(vmem_limit_bytes=16 << 20),
    )(left, right)


def condition_kernel(own_ref, far_ref, left_ref, right_ref, out_ref, wide_ref):
    count, rows, width = own_ref.shape
    left_terms = left_ref[...]
    right_0, right_1 = right_ref[:width], right_ref[width:]
    for q in range(count):
        query = jnp.concatenate([own_ref[q], far_ref[q]], axis=0)
        mixed = jnp.dot(left_terms, query, preferred_element_type=F32)
        mixed = mixed[:rows] + (mixed[rows : 2 * rows] + mixed[2 * rows :])
        mixed_0, mixed_1 = parts_of(mixed, 2)
        both = jnp.dot(jnp.concatenate([mixed_0, mixed_1], axis=0), right_0, preferred_element_type=F32)
        cross = jnp.dot(mixed_0, right_1, preferred_element_type=F32)
        wide_ref[:, q, :] = both[:rows] + (both[rows:] + cross)
    out_ref[...] = wide_ref[...].astype(BF16)


def condition(own, far, left_terms, right_terms):
    count, rows, width = own.shape
    return pl.pallas_call(
        condition_kernel,
        out_shape=jax.ShapeDtypeStruct((rows, count, width), BF16),
        in_specs=[VMEM] * 4,
        out_specs=VMEM,
        scratch_shapes=[pltpu.VMEM((rows, count, width), F32)],
        compiler_params=pltpu.CompilerParams(vmem_limit_bytes=24 << 20),
        cost_estimate=pl.CostEstimate(flops=count * 3_000_000 * 40, bytes_accessed=8 * count * rows * width, transcendentals=0),
    )(own, far, left_terms, right_terms)


def regroup_kernel(grads_ref, out_ref, held_ref, sems):
    examples, rows, width = held_ref.shape
    blocks = examples // EXAMPLES
    copies = []
    for b in range(blocks):
        part = pl.ds(b * EXAMPLES, EXAMPLES)
        copies.append(pltpu.make_async_copy(grads_ref.at[part], held_ref.at[part], sems.at[b]))
        copies[-1].start()
    i = lax.broadcasted_iota(jnp.int32, (TILE * TILE, TILE * TILE), 0)
    j = lax.broadcasted_iota(jnp.int32, (TILE * TILE, TILE * TILE), 1)
    swap = jnp.where((i // TILE == j % TILE) & (i % TILE == j // TILE), 1.0, 0.0).astype(BF16)
    for b in range(blocks):
        copies[b].wait()

        @pl.loop(b * EXAMPLES // TILE, (b + 1) * EXAMPLES // TILE)
        def _(step):
            n = pl.ds(pl.multiple_of(step * TILE, TILE), TILE)
            for r in range(0, rows, TILE):
                tile = held_ref[n, r : r + TILE, :].reshape(TILE * TILE, width)
                turned = jnp.dot(swap, tile, preferred_element_type=F32).astype(BF16)
                out_ref[r : r + TILE, n, :] = turned.reshape(TILE, TILE, width)


def regroup(grads):
    n, rows, width = grads.shape
    return pl.pallas_call(
        regroup_kernel,
        out_shape=jax.ShapeDtypeStruct((rows, n, width), BF16),
        in_specs=[pl.BlockSpec(memory_space=pltpu.HBM)],
        out_specs=VMEM,
        scratch_shapes=[pltpu.VMEM((n, rows, width), BF16), pltpu.SemaphoreType.DMA((n // EXAMPLES,))],
        compiler_params=pltpu.CompilerParams(vmem_limit_bytes=44 << 20),
        cost_estimate=pl.CostEstimate(flops=6_000_000_000, bytes_accessed=16_000_000, transcendentals=0),
    )(grads)


def inner_products(query_refs, grad_ref, first=0, rows=None):
    total = sum(ref.shape[1] for ref in query_refs)
    rows = rows or grad_ref.shape[0]
    starts = [0 if ref.shape[0] == rows else first for ref in query_refs]

    def body(i, acc):
        at = [i * DEEP + j for j in range(DEEP)]
        queries = [
            jnp.concatenate([ref[start + r] for ref, start in zip(query_refs, starts)], axis=0) for r in at
        ]
        return acc + lax.dot_general(
            jnp.concatenate(queries, axis=1),
            jnp.concatenate([grad_ref[first + r] for r in at], axis=1),
            (((1,), (1,)), ((), ())),
            preferred_element_type=F32,
        )

    start = jnp.zeros((total, grad_ref.shape[1]), F32)
    return lax.fori_loop(0, rows // DEEP, body, start)


def first_pass_kernel(ex, early_ref, own_ref, near, grad_ref, order_ref, out_ref):
    late = own_ref.shape[1]
    acc = inner_products((early_ref, own_ref, near), grad_ref)
    sources = slot_sources(lax.axis_index("ex"))
    early = [acc[EARLY * s : EARLY * (s + 1)] for s in range(2)]
    base = early_ref.shape[1]
    slots = [acc[base + late * s : base + late * (s + 1)] for s in range(2)]
    for b in range(ex):
        block = order_ref[b]
        low = jnp.zeros_like(early[0])
        for source, slot in zip(sources, early):
            low = low + jnp.where(source == block, slot, 0.0)
        high = jnp.zeros_like(slots[0])
        for source, slot in zip(sources, slots):
            high = high + jnp.where(source == block, slot, 0.0)
        at = b * (EARLY + late)
        out_ref[at : at + EARLY, :] = low
        out_ref[at + EARLY : at + EARLY + late, :] = high


def slot_sources(me):
    low_pair = me < 2
    near = jnp.where(low_pair, 1 - me, 5 - me)
    return [me, near, jnp.where(low_pair, 2, 1), jnp.where(low_pair, 3, 0)]


def far_pass_kernel(first, ex, early_ref, mid_ref, far_in, far_out, grad_ref, order_ref, out_ref, far_ref):
    far_ref[...] = far_in[...] + far_out[...]
    out_ref[...] = inner_products((early_ref, mid_ref, far_ref), grad_ref, first, far_out.shape[0])


def last_pass_kernel(
    ex, base_ref, far_0, far_1, early_ref, mid_ref, far_in, far_out, grad_ref, order_ref,
    mine_ref, send_ref, full_ref, far_ref,
):
    late = far_out.shape[1]
    rows = far_out.shape[0]
    first = grad_ref.shape[0] - rows
    far_ref[...] = far_in[...] + far_out[...]
    acc = far_0[...] + far_1[...] + inner_products((early_ref, mid_ref, far_ref), grad_ref, first, rows)
    mid, far = slot_sources(lax.axis_index("ex"))[2:]
    low_mid, low_far = acc[:EARLY], acc[EARLY : 2 * EARLY]
    high_mid, high_far = acc[2 * EARLY : 2 * EARLY + late], acc[2 * EARLY + late :]
    full_ref[...] = base_ref[...]
    for b in range(ex):
        mid_hit, far_hit = order_ref[b] == mid, order_ref[b] == far
        low = jnp.where(mid_hit, low_mid, 0.0) + jnp.where(far_hit, low_far, 0.0)
        high = jnp.where(mid_hit, high_mid, 0.0) + jnp.where(far_hit, high_far, 0.0)
        at = b * (EARLY + late)
        full_ref[at : at + EARLY, :] = full_ref[at : at + EARLY, :] + low
        at = at + EARLY
        full_ref[at : at + late, :] = full_ref[at : at + late, :] + high
    half = mine_ref.shape[0]
    side = lax.axis_index("feat")
    mine_ref[...] = full_ref[pl.ds(pl.multiple_of(side * half, half), half), :]
    send_ref[...] = full_ref[pl.ds(pl.multiple_of((1 - side) * half, half), half), :]


def score_call(kernel, ex, arrays, order, out_shape, scratch=()):
    return pl.pallas_call(
        functools.partial(kernel, ex),
        out_shape=out_shape,
        in_specs=[VMEM] * len(arrays) + [SMEM],
        out_specs=jax.tree.map(lambda _: VMEM, out_shape),
        scratch_shapes=scratch,
        compiler_params=pltpu.CompilerParams(vmem_limit_bytes=40 << 20),
        cost_estimate=pl.CostEstimate(flops=1000, bytes_accessed=1000, transcendentals=0),
    )(*arrays, order)


def after(x, *others):
    return lax.optimization_barrier((x, *others))[0]


PAIRS = [(0, 1), (1, 0), (2, 3), (3, 2)]
MIDDLE = [(1, 2), (2, 1)]
OUTWARD = [(1, 0), (2, 3)]


def per_device_line(train_grads, queries, left_factor, right_factor, block_order):
    ex = lax.axis_size("ex")
    swap = [(0, 1), (1, 0)]
    count = queries.shape[1]
    n = train_grads.shape[0]
    late_raw = queries[0, EARLY:]
    late_other = lax.ppermute(late_raw, "feat", swap)
    raw = after(queries, late_raw)[0, :EARLY]
    terms = factor_terms(left_factor, after(right_factor, raw), train_grads.shape[1])
    raw_near = lax.ppermute(raw, "ex", PAIRS)
    raw_mid = lax.ppermute(raw, "ex", MIDDLE)
    raw_mid_out = lax.ppermute(after(raw_mid, *terms), "ex", OUTWARD)
    early_0 = jnp.concatenate([raw, raw_near], axis=0)
    raw_far_mid = lax.ppermute(after(raw_near, early_0, late_other), "ex", MIDDLE)

    late = condition(after(late_raw, raw_near, raw_mid, early_0), late_other, *terms)
    near = lax.ppermute(late, "ex", PAIRS)
    mid = lax.ppermute(late, "ex", MIDDLE)
    grads = regroup(after(train_grads, late, raw_mid_out, raw_far_mid))
    early_0_other = lax.ppermute(after(early_0, late, raw_mid_out), "feat", swap)
    raw_far_out = lax.ppermute(after(raw_far_mid, grads), "ex", OUTWARD)
    far_mid = lax.ppermute(after(near, grads), "ex", MIDDLE)
    mid_out = lax.ppermute(after(mid, near, grads), "ex", OUTWARD)
    cond_0 = condition(after(early_0, near, mid), early_0_other, *terms)
    early_1 = jnp.concatenate([raw_mid + raw_mid_out, after(raw_far_mid, near, mid) + raw_far_out], axis=0)
    early_1_other = lax.ppermute(after(early_1, cond_0), "feat", swap)
    base = score_call(
        first_pass_kernel, ex, (cond_0, late, near, grads), block_order,
        jax.ShapeDtypeStruct((ex * count, n), F32),
    )
    rows = far_mid.shape[0]
    cuts = [0, rows // 2, 3 * rows // 4, rows]
    far_in = [after(far_mid, base)[a:b] for a, b in zip(cuts, cuts[1:])]
    far_out = [lax.ppermute(x, "ex", OUTWARD) for x in far_in]
    cond_1 = condition(after(early_1, far_mid, mid_out), early_1_other, *terms)

    mid = mid + mid_out
    far_sums, earlier = [], base
    for first, held, arrived in zip(cuts, far_in[:-1], far_out[:-1]):
        earlier = score_call(
            functools.partial(far_pass_kernel, first), ex, (cond_1, mid, held, arrived, after(grads, earlier)),
            block_order, jax.ShapeDtypeStruct((2 * count, n), F32), [pltpu.VMEM(arrived.shape, BF16)],
        )
        far_sums.append(earlier)
    half = jax.ShapeDtypeStruct((ex * count // 2, n), F32)
    mine, send = score_call(
        last_pass_kernel, ex, (base, *far_sums, cond_1, mid, far_in[-1], far_out[-1], grads), block_order,
        (half, half), [pltpu.VMEM((ex * count, n), F32), pltpu.VMEM(far_out[-1].shape, BF16)],
    )
    scores = mine + lax.ppermute(send, "feat", swap)
    return scores.T[:, None, :]


def per_device_gather(train_grads, queries, left_factor, right_factor, block_order):
    row_count = train_grads.shape[0]
    part_rows = train_grads.shape[1]
    right_width = train_grads.shape[2]
    flat_grads = train_grads.reshape(row_count, part_rows * right_width)
    local_queries = queries[0]
    block_size = local_queries.shape[0]
    regrouped = lax.all_to_all(local_queries, "feat", split_axis=0, concat_axis=1, tiled=True)
    whole_mix = jnp.einsum(
        "ik,qkj->qij", left_factor, regrouped.astype(F32), precision=lax.Precision.HIGHEST
    )
    whole_cond = jnp.einsum(
        "qij,jl->qil", whole_mix, right_factor, precision=lax.Precision.HIGHEST
    ).astype(BF16)
    conditioned = lax.all_to_all(whole_cond, "feat", split_axis=1, concat_axis=0, tiled=True)
    conditioned = conditioned.reshape(block_size, part_rows * right_width)
    partials = lax.dot_general(
        flat_grads,
        lax.all_gather(conditioned, "ex", axis=0, tiled=True),
        (((1,), (1,)), ((), ())),
        preferred_element_type=F32,
    )
    block_count = lax.axis_size("ex")
    partials = jnp.take(partials.reshape(row_count, block_count, block_size), block_order, axis=1)
    partials = partials.reshape(row_count, block_count * block_size)
    owned_scores = lax.psum_scatter(partials, "feat", scatter_dimension=1, tiled=True)
    return owned_scores.reshape(row_count, 1, owned_scores.shape[1])


def solution(mesh):
    short_line = mesh.shape["ex"] == 4 and mesh.shape["feat"] == 2
    return jax.shard_map(
        per_device_line if short_line else per_device_gather,
        mesh=mesh,
        in_specs=(
            P(("grp", "ex"), "feat", None),
            P("pb", ("grp", "ex"), "feat", None),
            P("grp", None),
            P("grp", None),
            P("grp"),
        ),
        out_specs=P(("grp", "ex"), "pb", "feat"),
        check_vma=False,
    )
```

```python
import functools

import jax
import jax.numpy as jnp
from jax import lax
from jax.experimental import pallas as pl
from jax.experimental.pallas import tpu as pltpu
from jax.sharding import PartitionSpec as P

F32 = jnp.float32
BF16 = jnp.bfloat16
EARLY = 4
TILE = 16
EXAMPLES = 32
DEEP = 32
VMEM = pl.BlockSpec(memory_space=pltpu.VMEM)
SMEM = pl.BlockSpec(memory_space=pltpu.SMEM)


def parts_of(x, count):
    terms = []
    for _ in range(count):
        top = x.astype(BF16)
        terms.append(top)
        x = x - top.astype(F32)
    return terms


def factor_kernel(left_ref, right_ref, left_out, right_out):
    rows = left_out.shape[0] // 3
    side = lax.axis_index("feat")
    here = pl.ds(pl.multiple_of(side * rows, rows), rows)
    there = pl.ds(pl.multiple_of((1 - side) * rows, rows), rows)
    left = jnp.concatenate([left_ref[here, here], left_ref[here, there]], axis=1)
    left_out[...] = jnp.concatenate(parts_of(left, 3), axis=0)
    right_out[...] = jnp.concatenate(parts_of(right_ref[...], 2), axis=0)


def factor_terms(left, right, rows):
    wide, width = left.shape[1], right.shape[1]
    return pl.pallas_call(
        factor_kernel,
        out_shape=(
            jax.ShapeDtypeStruct((3 * rows, wide), BF16),
            jax.ShapeDtypeStruct((2 * width, width), BF16),
        ),
        in_specs=[VMEM] * 2,
        out_specs=(VMEM, VMEM),
        compiler_params=pltpu.CompilerParams(vmem_limit_bytes=16 << 20),
    )(left, right)


def condition_kernel(own_ref, far_ref, left_ref, right_ref, out_ref, wide_ref):
    count, rows, width = own_ref.shape
    left_terms = left_ref[...]
    right_0, right_1 = right_ref[:width], right_ref[width:]
    for q in range(count):
        query = jnp.concatenate([own_ref[q], far_ref[q]], axis=0)
        mixed = jnp.dot(left_terms, query, preferred_element_type=F32)
        mixed = mixed[:rows] + (mixed[rows : 2 * rows] + mixed[2 * rows :])
        mixed_0, mixed_1 = parts_of(mixed, 2)
        both = jnp.dot(jnp.concatenate([mixed_0, mixed_1], axis=0), right_0, preferred_element_type=F32)
        cross = jnp.dot(mixed_0, right_1, preferred_element_type=F32)
        wide_ref[:, q, :] = both[:rows] + (both[rows:] + cross)
    out_ref[...] = wide_ref[...].astype(BF16)


def condition(own, far, left_terms, right_terms):
    count, rows, width = own.shape
    return pl.pallas_call(
        condition_kernel,
        out_shape=jax.ShapeDtypeStruct((rows, count, width), BF16),
        in_specs=[VMEM] * 4,
        out_specs=VMEM,
        scratch_shapes=[pltpu.VMEM((rows, count, width), F32)],
        compiler_params=pltpu.CompilerParams(vmem_limit_bytes=24 << 20),
        cost_estimate=pl.CostEstimate(flops=count * 3_000_000 * 40, bytes_accessed=8 * count * rows * width, transcendentals=0),
    )(own, far, left_terms, right_terms)


def regroup_kernel(grads_ref, out_ref, held_ref, sems):
    examples, rows, width = held_ref.shape
    blocks = examples // EXAMPLES
    copies = []
    for b in range(blocks):
        part = pl.ds(b * EXAMPLES, EXAMPLES)
        copies.append(pltpu.make_async_copy(grads_ref.at[part], held_ref.at[part], sems.at[b]))
        copies[-1].start()
    i = lax.broadcasted_iota(jnp.int32, (TILE * TILE, TILE * TILE), 0)
    j = lax.broadcasted_iota(jnp.int32, (TILE * TILE, TILE * TILE), 1)
    swap = jnp.where((i // TILE == j % TILE) & (i % TILE == j // TILE), 1.0, 0.0).astype(BF16)
    for b in range(blocks):
        copies[b].wait()

        @pl.loop(b * EXAMPLES // TILE, (b + 1) * EXAMPLES // TILE)
        def _(step):
            n = pl.ds(pl.multiple_of(step * TILE, TILE), TILE)
            for r in range(0, rows, TILE):
                tile = held_ref[n, r : r + TILE, :].reshape(TILE * TILE, width)
                turned = jnp.dot(swap, tile, preferred_element_type=F32).astype(BF16)
                out_ref[r : r + TILE, n, :] = turned.reshape(TILE, TILE, width)


def regroup(grads):
    n, rows, width = grads.shape
    return pl.pallas_call(
        regroup_kernel,
        out_shape=jax.ShapeDtypeStruct((rows, n, width), BF16),
        in_specs=[pl.BlockSpec(memory_space=pltpu.HBM)],
        out_specs=VMEM,
        scratch_shapes=[pltpu.VMEM((n, rows, width), BF16), pltpu.SemaphoreType.DMA((n // EXAMPLES,))],
        compiler_params=pltpu.CompilerParams(vmem_limit_bytes=44 << 20),
        cost_estimate=pl.CostEstimate(flops=6_000_000_000, bytes_accessed=16_000_000, transcendentals=0),
    )(grads)


def inner_products(query_refs, grad_ref, first=0, rows=None):
    total = sum(ref.shape[1] for ref in query_refs)
    rows = rows or grad_ref.shape[0]
    starts = [0 if ref.shape[0] == rows else first for ref in query_refs]

    def body(i, acc):
        at = [i * DEEP + j for j in range(DEEP)]
        queries = [
            jnp.concatenate([ref[start + r] for ref, start in zip(query_refs, starts)], axis=0) for r in at
        ]
        return acc + lax.dot_general(
            jnp.concatenate(queries, axis=1),
            jnp.concatenate([grad_ref[first + r] for r in at], axis=1),
            (((1,), (1,)), ((), ())),
            preferred_element_type=F32,
        )

    start = jnp.zeros((total, grad_ref.shape[1]), F32)
    return lax.fori_loop(0, rows // DEEP, body, start)


def first_pass_kernel(ex, early_ref, own_ref, near, grad_ref, order_ref, out_ref):
    late = own_ref.shape[1]
    acc = inner_products((early_ref, own_ref, near), grad_ref)
    sources = slot_sources(lax.axis_index("ex"))
    early = [acc[EARLY * s : EARLY * (s + 1)] for s in range(2)]
    base = early_ref.shape[1]
    slots = [acc[base + late * s : base + late * (s + 1)] for s in range(2)]
    for b in range(ex):
        block = order_ref[b]
        low = jnp.zeros_like(early[0])
        for source, slot in zip(sources, early):
            low = low + jnp.where(source == block, slot, 0.0)
        high = jnp.zeros_like(slots[0])
        for source, slot in zip(sources, slots):
            high = high + jnp.where(source == block, slot, 0.0)
        at = b * (EARLY + late)
        out_ref[at : at + EARLY, :] = low
        out_ref[at + EARLY : at + EARLY + late, :] = high


def slot_sources(me):
    low_pair = me < 2
    near = jnp.where(low_pair, 1 - me, 5 - me)
    return [me, near, jnp.where(low_pair, 2, 1), jnp.where(low_pair, 3, 0)]


def middle_pass_kernel(ex, base_ref, early_ref, mid_ref, grad_ref, order_ref, out_ref):
    late = mid_ref.shape[1]
    acc = inner_products((early_ref, mid_ref), grad_ref)
    mid, far = slot_sources(lax.axis_index("ex"))[2:]
    out_ref[...] = base_ref[...]
    for b in range(ex):
        mid_hit, far_hit = order_ref[b] == mid, order_ref[b] == far
        low = jnp.where(mid_hit, acc[:EARLY], 0.0) + jnp.where(far_hit, acc[EARLY : 2 * EARLY], 0.0)
        at = b * (EARLY + late)
        out_ref[at : at + EARLY, :] = out_ref[at : at + EARLY, :] + low
        at = at + EARLY
        out_ref[at : at + late, :] = out_ref[at : at + late, :] + jnp.where(mid_hit, acc[2 * EARLY :], 0.0)


def far_pass_kernel(first, ex, far_in, far_out, grad_ref, order_ref, out_ref, far_ref):
    far_ref[...] = far_in[...] + far_out[...]
    out_ref[...] = inner_products((far_ref,), grad_ref, first, far_out.shape[0])


def last_pass_kernel(
    ex, base_ref, far_0, far_1, far_in, far_out, grad_ref, order_ref, mine_ref, send_ref, full_ref, far_ref
):
    rows, late, _ = far_out.shape
    far_ref[...] = far_in[...] + far_out[...]
    acc = far_0[...] + far_1[...] + inner_products((far_ref,), grad_ref, grad_ref.shape[0] - rows, rows)
    far = slot_sources(lax.axis_index("ex"))[3]
    full_ref[...] = base_ref[...]
    for b in range(ex):
        at = b * (EARLY + late) + EARLY
        full_ref[at : at + late, :] = full_ref[at : at + late, :] + jnp.where(order_ref[b] == far, acc, 0.0)
    half = mine_ref.shape[0]
    side = lax.axis_index("feat")
    mine_ref[...] = full_ref[pl.ds(pl.multiple_of(side * half, half), half), :]
    send_ref[...] = full_ref[pl.ds(pl.multiple_of((1 - side) * half, half), half), :]


def score_call(kernel, ex, arrays, order, out_shape, scratch=()):
    return pl.pallas_call(
        functools.partial(kernel, ex),
        out_shape=out_shape,
        in_specs=[VMEM] * len(arrays) + [SMEM],
        out_specs=jax.tree.map(lambda _: VMEM, out_shape),
        scratch_shapes=scratch,
        compiler_params=pltpu.CompilerParams(vmem_limit_bytes=40 << 20),
        cost_estimate=pl.CostEstimate(flops=1000, bytes_accessed=1000, transcendentals=0),
    )(*arrays, order)


def after(x, *others):
    return lax.optimization_barrier((x, *others))[0]


PAIRS = [(0, 1), (1, 0), (2, 3), (3, 2)]
MIDDLE = [(1, 2), (2, 1)]
OUTWARD = [(1, 0), (2, 3)]


def per_device_line(train_grads, queries, left_factor, right_factor, block_order):
    ex = lax.axis_size("ex")
    swap = [(0, 1), (1, 0)]
    count = queries.shape[1]
    n = train_grads.shape[0]
    late_raw = queries[0, EARLY:]
    late_other = lax.ppermute(late_raw, "feat", swap)
    raw = after(queries, late_raw)[0, :EARLY]
    terms = factor_terms(left_factor, after(right_factor, raw), train_grads.shape[1])
    raw_near = lax.ppermute(raw, "ex", PAIRS)
    raw_mid = lax.ppermute(raw, "ex", MIDDLE)
    raw_mid_out = lax.ppermute(after(raw_mid, *terms), "ex", OUTWARD)
    early_0 = jnp.concatenate([raw, raw_near], axis=0)
    raw_far_mid = lax.ppermute(after(raw_near, early_0, late_other), "ex", MIDDLE)

    late = condition(after(late_raw, raw_near, raw_mid, early_0), late_other, *terms)
    near = lax.ppermute(late, "ex", PAIRS)
    mid = lax.ppermute(late, "ex", MIDDLE)
    grads = regroup(after(train_grads, late, raw_mid_out, raw_far_mid))
    early_0_other = lax.ppermute(after(early_0, late, raw_mid_out), "feat", swap)
    raw_far_out = lax.ppermute(after(raw_far_mid, grads), "ex", OUTWARD)
    far_mid = lax.ppermute(after(near, grads), "ex", MIDDLE)
    mid_out = lax.ppermute(after(mid, near, grads), "ex", OUTWARD)
    cond_0 = condition(after(early_0, near, mid), early_0_other, *terms)
    early_1 = jnp.concatenate([raw_mid + raw_mid_out, after(raw_far_mid, near, mid) + raw_far_out], axis=0)
    early_1_other = lax.ppermute(after(early_1, cond_0), "feat", swap)
    base = score_call(
        first_pass_kernel, ex, (cond_0, late, near, grads), block_order,
        jax.ShapeDtypeStruct((ex * count, n), F32),
    )
    rows = far_mid.shape[0]
    cuts = [0, rows // 2, 3 * rows // 4, rows]
    far_in = [after(far_mid, base)[a:b] for a, b in zip(cuts, cuts[1:])]
    far_out = [lax.ppermute(x, "ex", OUTWARD) for x in far_in]
    cond_1 = condition(after(early_1, far_mid, mid_out), early_1_other, *terms)

    mid = mid + mid_out
    base = score_call(
        middle_pass_kernel, ex, (base, cond_1, mid, grads), block_order,
        jax.ShapeDtypeStruct((ex * count, n), F32),
    )
    far_sums, earlier = [], base
    for first, held, arrived in zip(cuts, far_in[:-1], far_out[:-1]):
        earlier = score_call(
            functools.partial(far_pass_kernel, first), ex, (held, arrived, after(grads, earlier)),
            block_order, jax.ShapeDtypeStruct((count - EARLY, n), F32), [pltpu.VMEM(arrived.shape, BF16)],
        )
        far_sums.append(earlier)
    half = jax.ShapeDtypeStruct((ex * count // 2, n), F32)
    mine, send = score_call(
        last_pass_kernel, ex, (base, *far_sums, far_in[-1], far_out[-1], grads), block_order,
        (half, half), [pltpu.VMEM((ex * count, n), F32), pltpu.VMEM(far_out[-1].shape, BF16)],
    )
    scores = mine + lax.ppermute(send, "feat", swap)
    return scores.T[:, None, :]


def per_device_gather(train_grads, queries, left_factor, right_factor, block_order):
    row_count = train_grads.shape[0]
    part_rows = train_grads.shape[1]
    right_width = train_grads.shape[2]
    flat_grads = train_grads.reshape(row_count, part_rows * right_width)
    local_queries = queries[0]
    block_size = local_queries.shape[0]
    regrouped = lax.all_to_all(local_queries, "feat", split_axis=0, concat_axis=1, tiled=True)
    whole_mix = jnp.einsum(
        "ik,qkj->qij", left_factor, regrouped.astype(F32), precision=lax.Precision.HIGHEST
    )
    whole_cond = jnp.einsum(
        "qij,jl->qil", whole_mix, right_factor, precision=lax.Precision.HIGHEST
    ).astype(BF16)
    conditioned = lax.all_to_all(whole_cond, "feat", split_axis=1, concat_axis=0, tiled=True)
    conditioned = conditioned.reshape(block_size, part_rows * right_width)
    partials = lax.dot_general(
        flat_grads,
        lax.all_gather(conditioned, "ex", axis=0, tiled=True),
        (((1,), (1,)), ((), ())),
        preferred_element_type=F32,
    )
    block_count = lax.axis_size("ex")
    partials = jnp.take(partials.reshape(row_count, block_count, block_size), block_order, axis=1)
    partials = partials.reshape(row_count, block_count * block_size)
    owned_scores = lax.psum_scatter(partials, "feat", scatter_dimension=1, tiled=True)
    return owned_scores.reshape(row_count, 1, owned_scores.shape[1])


def solution(mesh):
    short_line = mesh.shape["ex"] == 4 and mesh.shape["feat"] == 2
    return jax.shard_map(
        per_device_line if short_line else per_device_gather,
        mesh=mesh,
        in_specs=(
            P(("grp", "ex"), "feat", None),
            P("pb", ("grp", "ex"), "feat", None),
            P("grp", None),
            P("grp", None),
            P("grp"),
        ),
        out_specs=P(("grp", "ex"), "pb", "feat"),
        check_vma=False,
    )
```

```python
import functools

import jax
import jax.numpy as jnp
from jax import lax
from jax.experimental import pallas as pl
from jax.experimental.pallas import tpu as pltpu
from jax.sharding import PartitionSpec as P

F32 = jnp.float32
BF16 = jnp.bfloat16
EARLY = 4
TILE = 16
EXAMPLES = 16
DEEP = 32
VMEM = pl.BlockSpec(memory_space=pltpu.VMEM)
SMEM = pl.BlockSpec(memory_space=pltpu.SMEM)


def parts_of(x, count):
    terms = []
    for _ in range(count):
        top = x.astype(BF16)
        terms.append(top)
        x = x - top.astype(F32)
    return terms


def factor_kernel(left_ref, right_ref, left_out, right_out):
    rows = left_out.shape[0] // 3
    side = lax.axis_index("feat")
    here = pl.ds(pl.multiple_of(side * rows, rows), rows)
    there = pl.ds(pl.multiple_of((1 - side) * rows, rows), rows)
    left = jnp.concatenate([left_ref[here, here], left_ref[here, there]], axis=1)
    left_out[...] = jnp.concatenate(parts_of(left, 3), axis=0)
    right_out[...] = jnp.concatenate(parts_of(right_ref[...], 2), axis=0)


def factor_terms(left, right, rows):
    wide, width = left.shape[1], right.shape[1]
    return pl.pallas_call(
        factor_kernel,
        out_shape=(
            jax.ShapeDtypeStruct((3 * rows, wide), BF16),
            jax.ShapeDtypeStruct((2 * width, width), BF16),
        ),
        in_specs=[VMEM] * 2,
        out_specs=(VMEM, VMEM),
        compiler_params=pltpu.CompilerParams(vmem_limit_bytes=16 << 20),
    )(left, right)


def condition_kernel(own_ref, far_ref, left_ref, right_ref, out_ref, wide_ref):
    count, rows, width = own_ref.shape
    left_terms = left_ref[...]
    right_0, right_1 = right_ref[:width], right_ref[width:]
    for q in range(count):
        query = jnp.concatenate([own_ref[q], far_ref[q]], axis=0)
        mixed = jnp.dot(left_terms, query, preferred_element_type=F32)
        mixed = mixed[:rows] + (mixed[rows : 2 * rows] + mixed[2 * rows :])
        mixed_0, mixed_1 = parts_of(mixed, 2)
        both = jnp.dot(jnp.concatenate([mixed_0, mixed_1], axis=0), right_0, preferred_element_type=F32)
        cross = jnp.dot(mixed_0, right_1, preferred_element_type=F32)
        wide_ref[:, q, :] = both[:rows] + (both[rows:] + cross)
    out_ref[...] = wide_ref[...].astype(BF16)


def condition(own, far, left_terms, right_terms):
    count, rows, width = own.shape
    return pl.pallas_call(
        condition_kernel,
        out_shape=jax.ShapeDtypeStruct((rows, count, width), BF16),
        in_specs=[VMEM] * 4,
        out_specs=VMEM,
        scratch_shapes=[pltpu.VMEM((rows, count, width), F32)],
        compiler_params=pltpu.CompilerParams(vmem_limit_bytes=24 << 20),
        cost_estimate=pl.CostEstimate(flops=count * 3_000_000 * 40, bytes_accessed=8 * count * rows * width, transcendentals=0),
    )(own, far, left_terms, right_terms)


def regroup_kernel(grads_ref, out_ref, held_ref, sems):
    examples, rows, width = held_ref.shape
    blocks = examples // EXAMPLES
    copies = []
    for b in range(blocks):
        part = pl.ds(b * EXAMPLES, EXAMPLES)
        copies.append(pltpu.make_async_copy(grads_ref.at[part], held_ref.at[part], sems.at[b]))
        copies[-1].start()
    i = lax.broadcasted_iota(jnp.int32, (TILE * TILE, TILE * TILE), 0)
    j = lax.broadcasted_iota(jnp.int32, (TILE * TILE, TILE * TILE), 1)
    swap = jnp.where((i // TILE == j % TILE) & (i % TILE == j // TILE), 1.0, 0.0).astype(BF16)
    for b in range(blocks):
        copies[b].wait()

        @pl.loop(b * EXAMPLES // TILE, (b + 1) * EXAMPLES // TILE)
        def _(step):
            n = pl.ds(pl.multiple_of(step * TILE, TILE), TILE)
            for r in range(0, rows, TILE):
                tile = held_ref[n, r : r + TILE, :].reshape(TILE * TILE, width)
                turned = jnp.dot(swap, tile, preferred_element_type=F32).astype(BF16)
                out_ref[r : r + TILE, n, :] = turned.reshape(TILE, TILE, width)


def regroup(grads):
    n, rows, width = grads.shape
    return pl.pallas_call(
        regroup_kernel,
        out_shape=jax.ShapeDtypeStruct((rows, n, width), BF16),
        in_specs=[pl.BlockSpec(memory_space=pltpu.HBM)],
        out_specs=VMEM,
        scratch_shapes=[pltpu.VMEM((n, rows, width), BF16), pltpu.SemaphoreType.DMA((n // EXAMPLES,))],
        compiler_params=pltpu.CompilerParams(vmem_limit_bytes=44 << 20),
        cost_estimate=pl.CostEstimate(flops=6_000_000_000, bytes_accessed=16_000_000, transcendentals=0),
    )(grads)


def inner_products(query_refs, grad_ref, first=0, rows=None):
    total = sum(ref.shape[1] for ref in query_refs)
    rows = rows or grad_ref.shape[0]
    starts = [0 if ref.shape[0] == rows else first for ref in query_refs]

    def body(i, acc):
        at = [i * DEEP + j for j in range(DEEP)]
        queries = [
            jnp.concatenate([ref[start + r] for ref, start in zip(query_refs, starts)], axis=0) for r in at
        ]
        return acc + lax.dot_general(
            jnp.concatenate(queries, axis=1),
            jnp.concatenate([grad_ref[first + r] for r in at], axis=1),
            (((1,), (1,)), ((), ())),
            preferred_element_type=F32,
        )

    start = jnp.zeros((total, grad_ref.shape[1]), F32)
    return lax.fori_loop(0, rows // DEEP, body, start)


def first_pass_kernel(ex, early_ref, own_ref, near, grad_ref, order_ref, out_ref):
    late = own_ref.shape[1]
    acc = inner_products((early_ref, own_ref, near), grad_ref)
    sources = slot_sources(lax.axis_index("ex"))
    early = [acc[EARLY * s : EARLY * (s + 1)] for s in range(2)]
    base = early_ref.shape[1]
    slots = [acc[base + late * s : base + late * (s + 1)] for s in range(2)]
    for b in range(ex):
        block = order_ref[b]
        low = jnp.zeros_like(early[0])
        for source, slot in zip(sources, early):
            low = low + jnp.where(source == block, slot, 0.0)
        high = jnp.zeros_like(slots[0])
        for source, slot in zip(sources, slots):
            high = high + jnp.where(source == block, slot, 0.0)
        at = b * (EARLY + late)
        out_ref[at : at + EARLY, :] = low
        out_ref[at + EARLY : at + EARLY + late, :] = high


def slot_sources(me):
    low_pair = me < 2
    near = jnp.where(low_pair, 1 - me, 5 - me)
    return [me, near, jnp.where(low_pair, 2, 1), jnp.where(low_pair, 3, 0)]


def middle_pass_kernel(ex, base_ref, early_ref, mid_ref, grad_ref, order_ref, out_ref):
    late = mid_ref.shape[1]
    acc = inner_products((early_ref, mid_ref), grad_ref)
    mid, far = slot_sources(lax.axis_index("ex"))[2:]
    out_ref[...] = base_ref[...]
    for b in range(ex):
        mid_hit, far_hit = order_ref[b] == mid, order_ref[b] == far
        low = jnp.where(mid_hit, acc[:EARLY], 0.0) + jnp.where(far_hit, acc[EARLY : 2 * EARLY], 0.0)
        at = b * (EARLY + late)
        out_ref[at : at + EARLY, :] = out_ref[at : at + EARLY, :] + low
        at = at + EARLY
        out_ref[at : at + late, :] = out_ref[at : at + late, :] + jnp.where(mid_hit, acc[2 * EARLY :], 0.0)


def far_pass_kernel(first, ex, far_in, far_out, grad_ref, order_ref, out_ref, far_ref):
    far_ref[...] = far_in[...] + far_out[...]
    out_ref[...] = inner_products((far_ref,), grad_ref, first, far_out.shape[0])


def last_pass_kernel(
    ex, base_ref, far_0, far_1, far_in, far_out, grad_ref, order_ref, mine_ref, send_ref, full_ref, far_ref
):
    rows, late, _ = far_out.shape
    far_ref[...] = far_in[...] + far_out[...]
    acc = far_0[...] + far_1[...] + inner_products((far_ref,), grad_ref, grad_ref.shape[0] - rows, rows)
    far = slot_sources(lax.axis_index("ex"))[3]
    full_ref[...] = base_ref[...]
    for b in range(ex):
        at = b * (EARLY + late) + EARLY
        full_ref[at : at + late, :] = full_ref[at : at + late, :] + jnp.where(order_ref[b] == far, acc, 0.0)
    half = mine_ref.shape[0]
    side = lax.axis_index("feat")
    mine_ref[...] = full_ref[pl.ds(pl.multiple_of(side * half, half), half), :]
    send_ref[...] = full_ref[pl.ds(pl.multiple_of((1 - side) * half, half), half), :]


def score_call(kernel, ex, arrays, order, out_shape, scratch=()):
    return pl.pallas_call(
        functools.partial(kernel, ex),
        out_shape=out_shape,
        in_specs=[VMEM] * len(arrays) + [SMEM],
        out_specs=jax.tree.map(lambda _: VMEM, out_shape),
        scratch_shapes=scratch,
        compiler_params=pltpu.CompilerParams(vmem_limit_bytes=40 << 20),
        cost_estimate=pl.CostEstimate(flops=1000, bytes_accessed=1000, transcendentals=0),
    )(*arrays, order)


def after(x, *others):
    return lax.optimization_barrier((x, *others))[0]


PAIRS = [(0, 1), (1, 0), (2, 3), (3, 2)]
MIDDLE = [(1, 2), (2, 1)]
OUTWARD = [(1, 0), (2, 3)]


def per_device_line(train_grads, queries, left_factor, right_factor, block_order):
    ex = lax.axis_size("ex")
    swap = [(0, 1), (1, 0)]
    count = queries.shape[1]
    n = train_grads.shape[0]
    late_raw = queries[0, EARLY:]
    late_other = lax.ppermute(late_raw, "feat", swap)
    raw = after(queries, late_raw)[0, :EARLY]
    terms = factor_terms(left_factor, after(right_factor, raw), train_grads.shape[1])
    raw_near = lax.ppermute(raw, "ex", PAIRS)
    raw_mid = lax.ppermute(raw, "ex", MIDDLE)
    raw_mid_out = lax.ppermute(after(raw_mid, *terms), "ex", OUTWARD)
    early_0 = jnp.concatenate([raw, raw_near], axis=0)
    raw_far_mid = lax.ppermute(after(raw_near, early_0, late_other), "ex", MIDDLE)

    late = condition(after(late_raw, raw_near, raw_mid, early_0), late_other, *terms)
    near = lax.ppermute(late, "ex", PAIRS)
    mid = lax.ppermute(late, "ex", MIDDLE)
    grads = regroup(after(train_grads, late, raw_mid_out, raw_far_mid))
    early_0_other = lax.ppermute(after(early_0, late, raw_mid_out), "feat", swap)
    raw_far_out = lax.ppermute(after(raw_far_mid, grads), "ex", OUTWARD)
    far_mid = lax.ppermute(after(near, grads), "ex", MIDDLE)
    mid_out = lax.ppermute(after(mid, near, grads), "ex", OUTWARD)
    cond_0 = condition(after(early_0, near, mid), early_0_other, *terms)
    early_1 = jnp.concatenate([raw_mid + raw_mid_out, after(raw_far_mid, near, mid) + raw_far_out], axis=0)
    early_1_other = lax.ppermute(after(early_1, cond_0), "feat", swap)
    base = score_call(
        first_pass_kernel, ex, (cond_0, late, near, grads), block_order,
        jax.ShapeDtypeStruct((ex * count, n), F32),
    )
    rows = far_mid.shape[0]
    cuts = [0, rows // 2, 3 * rows // 4, rows]
    far_in = [after(far_mid, base)[a:b] for a, b in zip(cuts, cuts[1:])]
    far_out = [lax.ppermute(x, "ex", OUTWARD) for x in far_in]
    cond_1 = condition(after(early_1, far_mid, mid_out), early_1_other, *terms)

    mid = mid + mid_out
    base = score_call(
        middle_pass_kernel, ex, (base, cond_1, mid, grads), block_order,
        jax.ShapeDtypeStruct((ex * count, n), F32),
    )
    far_sums, earlier = [], base
    for first, held, arrived in zip(cuts, far_in[:-1], far_out[:-1]):
        earlier = score_call(
            functools.partial(far_pass_kernel, first), ex, (held, arrived, after(grads, earlier)),
            block_order, jax.ShapeDtypeStruct((count - EARLY, n), F32), [pltpu.VMEM(arrived.shape, BF16)],
        )
        far_sums.append(earlier)
    half = jax.ShapeDtypeStruct((ex * count // 2, n), F32)
    mine, send = score_call(
        last_pass_kernel, ex, (base, *far_sums, far_in[-1], far_out[-1], grads), block_order,
        (half, half), [pltpu.VMEM((ex * count, n), F32), pltpu.VMEM(far_out[-1].shape, BF16)],
    )
    scores = mine + lax.ppermute(send, "feat", swap)
    return scores.T[:, None, :]


def per_device_gather(train_grads, queries, left_factor, right_factor, block_order):
    row_count = train_grads.shape[0]
    part_rows = train_grads.shape[1]
    right_width = train_grads.shape[2]
    flat_grads = train_grads.reshape(row_count, part_rows * right_width)
    local_queries = queries[0]
    block_size = local_queries.shape[0]
    regrouped = lax.all_to_all(local_queries, "feat", split_axis=0, concat_axis=1, tiled=True)
    whole_mix = jnp.einsum(
        "ik,qkj->qij", left_factor, regrouped.astype(F32), precision=lax.Precision.HIGHEST
    )
    whole_cond = jnp.einsum(
        "qij,jl->qil", whole_mix, right_factor, precision=lax.Precision.HIGHEST
    ).astype(BF16)
    conditioned = lax.all_to_all(whole_cond, "feat", split_axis=1, concat_axis=0, tiled=True)
    conditioned = conditioned.reshape(block_size, part_rows * right_width)
    partials = lax.dot_general(
        flat_grads,
        lax.all_gather(conditioned, "ex", axis=0, tiled=True),
        (((1,), (1,)), ((), ())),
        preferred_element_type=F32,
    )
    block_count = lax.axis_size("ex")
    partials = jnp.take(partials.reshape(row_count, block_count, block_size), block_order, axis=1)
    partials = partials.reshape(row_count, block_count * block_size)
    owned_scores = lax.psum_scatter(partials, "feat", scatter_dimension=1, tiled=True)
    return owned_scores.reshape(row_count, 1, owned_scores.shape[1])


def solution(mesh):
    short_line = mesh.shape["ex"] == 4 and mesh.shape["feat"] == 2
    return jax.shard_map(
        per_device_line if short_line else per_device_gather,
        mesh=mesh,
        in_specs=(
            P(("grp", "ex"), "feat", None),
            P("pb", ("grp", "ex"), "feat", None),
            P("grp", None),
            P("grp", None),
            P("grp"),
        ),
        out_specs=P(("grp", "ex"), "pb", "feat"),
        check_vma=False,
    )
```
